32 devices in a mesh: rep: 4 (over x, core), shard: 8 (over z, y).
Axes of the slice: x: 2, y: 2, z: 4, core: 2. Of those that a mesh axis runs over, the one named last changes fastest.
Arguments:
- tokens: bfloat16 [32768, 1024], P(('rep', 'shard')), may hold values from -6 to 6
- w_query: bfloat16 [1024, 1024], P('shard'), may hold values from -0.1875 to 0.1875
- w_key: bfloat16 [1024, 1024], P('shard'), may hold values from -0.1875 to 0.1875
- w_value: bfloat16 [1024, 1024], P('shard'), may hold values from -0.1875 to 0.1875
- b_query: bfloat16 [1024], P('shard'), may hold values from -3 to 3
- b_value: bfloat16 [1024], P('shard'), may hold values from -3 to 3
- w_out: bfloat16 [1024, 1024], P('shard'), may hold values from -3 to 3
- b_out: bfloat16 [1024], P('shard'), may hold values from -3 to 3
- gain_one: bfloat16 [1024], P('shard'), may hold values from 0.5 to 1.5
- shift_one: bfloat16 [1024], P('shard'), may hold values from -3 to 3
- w_inner: bfloat16 [1024, 4096], P('shard'), may hold values from -0.1875 to 0.1875
- b_inner: bfloat16 [4096], P('shard'), may hold values from -3 to 3
- w_outer: bfloat16 [4096, 1024], P('shard'), may hold values from -0.09375 to 0.09375
- b_outer: bfloat16 [1024], P('shard'), may hold values from -3 to 3
- gain_two: bfloat16 [1024], P('shard'), may hold values from 0.5 to 1.5
- shift_two: bfloat16 [1024], P('shard'), may hold values from -3 to 3
- cotangent: bfloat16 [32768, 1024], P(('rep', 'shard')), may hold values from -6 to 6
Outputs:
- output: bfloat16 [32768, 1024], P(('rep', 'shard'))
- d_tokens: bfloat16 [32768, 1024], P(('rep', 'shard'))
- grad_w_query: float32 [1024, 1024], P('shard')
- grad_w_key: float32 [1024, 1024], P('shard')
- grad_w_value: float32 [1024, 1024], P('shard')
- grad_b_query: float32 [1024], P('shard')
- grad_b_value: float32 [1024], P('shard')
- grad_w_out: float32 [1024, 1024], P('shard')
- grad_b_out: float32 [1024], P('shard')
- grad_gain_one: float32 [1024], P('shard')
- grad_shift_one: float32 [1024], P('shard')
- grad_w_inner: float32 [1024, 4096], P('shard')
- grad_b_inner: float32 [4096], P('shard')
- grad_w_outer: float32 [4096, 1024], P('shard')
- grad_b_outer: float32 [1024], P('shard')
- grad_gain_two: float32 [1024], P('shard')
- grad_shift_two: float32 [1024], P('shard')
The draws below stay inside these ranges and needn't reach their ends.
All inputs are finite; a program needn't handle non-finite values.
Results may differ from the reference program's by a relative error of at most 0.017.
Values may be sent and summed in bfloat16 or wider, within the bound.
No kernel may reach another device: no remote copies, remote signals or barrier semaphores. Data moves between devices by JAX's collectives and lax.ppermute only.
A program may use at most 192 MiB of HBM per device.

```python
import math
import jax
import jax.numpy as jnp
from jax import lax

D = 1024
H = 16
DH = 64
FF = 4096
SEQ = 512
TOKENS = 32768


def steps_of(stream_key, extent, shards, least, largest):
    def one(dim, shards_of):
        steps = jax.random.uniform(jax.random.fold_in(jax.random.fold_in(stream_key, 6), dim), (shards_of,), jnp.float32, least / len(shards), largest / len(shards))
        return jnp.repeat(jnp.exp(steps), extent[dim] // shards_of).reshape((-1,) + (1,) * (len(extent) - dim - 1))

    factor_of = one(*shards[0])
    for cut in shards[1:]:
        factor_of = factor_of * one(*cut)
    return factor_of


def noise(key, dims, width, reach, shards=(), kind=jnp.bfloat16):
    array = jax.random.normal(key, dims, jnp.float32) * width
    if len(shards) > 0:
        array = steps_of(key, dims, shards, -0.22, 0.18) * array
    return jnp.clip(array, min=-reach, max=reach).astype(kind)


def setup_inputs(seed: int = 0) -> dict:
    streams_of = jax.random.split(jax.random.key(seed), 18)
    return {
        "tokens": noise(streams_of[0], (TOKENS, D), 1.0, 6.0, ((0, 32),)),
        "w_query": noise(streams_of[1], (D, D), D ** -0.5, 0.1875, ((0, 8),)),
        "w_key": noise(streams_of[2], (D, D), D ** -0.5, 0.1875, ((0, 8),)),
        "w_value": noise(streams_of[3], (D, D), D ** -0.5, 0.1875, ((0, 8),)),
        "b_query": noise(streams_of[4], (D,), 0.5, 3.0, ((0, 8),)),
        "b_value": noise(streams_of[5], (D,), 0.5, 3.0, ((0, 8),)),
        "w_out": noise(streams_of[6], (D, D), (2 * D // SEQ) ** -0.5, 3.0, ((0, 8),)),
        "b_out": noise(streams_of[7], (D,), 0.5, 3.0, ((0, 8),)),
        "gain_one": jnp.clip(1.0 + 0.1 * jax.random.normal(streams_of[8], (D,), jnp.float32), 0.5, 1.5).astype(jnp.bfloat16),
        "shift_one": noise(streams_of[9], (D,), 0.5, 3.0, ((0, 8),)),
        "w_inner": noise(streams_of[10], (D, FF), D ** -0.5, 0.1875, ((0, 8),)),
        "b_inner": noise(streams_of[11], (FF,), 0.5, 3.0, ((0, 8),)),
        "w_outer": noise(streams_of[12], (FF, D), FF ** -0.5, 0.09375, ((0, 8),)),
        "b_outer": noise(streams_of[13], (D,), 0.5, 3.0, ((0, 8),)),
        "gain_two": jnp.clip(1.0 + 0.1 * jax.random.normal(streams_of[14], (D,), jnp.float32), 0.5, 1.5).astype(jnp.bfloat16),
        "shift_two": noise(streams_of[15], (D,), 0.5, 3.0, ((0, 8),)),
        "cotangent": noise(streams_of[16], (TOKENS, D), 1.0, 6.0, ((0, 32),)),
    }


@jax.custom_vjp
def low(v):
    return lax.optimization_barrier(v.astype(jnp.bfloat16)).astype(jnp.float32)

@jax.custom_vjp
def low_back(v):
    return v

def low_keep(v):
    return (low(v), None)

def low_pass(kept, grad):
    return (grad,)

def back_keep(v):
    return (v, None)

def back_low(kept, grad):
    return (low(grad),)
low.defvjp(low_keep, low_pass)
low_back.defvjp(back_keep, back_low)

def product(left, right):
    return jnp.dot(left, right, precision=lax.Precision.HIGHEST, preferred_element_type=jnp.float32)

def layer_norm(values, gain, shift):
    centre = values - lax.optimization_barrier(jnp.mean(values, axis=-1, keepdims=True))
    spread = lax.optimization_barrier(jnp.mean(centre * centre, axis=-1, keepdims=True))
    return centre * lax.rsqrt(spread + 1e-12) * gain + shift

def attend_sequence(block):
    query, key, value = block
    scores = jnp.einsum('qhd,khd->hqk', query, key, precision=lax.Precision.HIGHEST) * 0.125
    scores = low_back(scores)
    top = lax.optimization_barrier(jnp.max(scores, axis=-1, keepdims=True))
    expo = jnp.exp(scores - top)
    probs = low(expo / lax.optimization_barrier(jnp.sum(expo, axis=-1, keepdims=True)))
    return jnp.einsum('hqk,khd->qhd', probs, value, precision=lax.Precision.HIGHEST)

def forward(tokens, w_query, w_key, w_value, b_query, b_value, w_out, b_out, gain_one, shift_one, w_inner, b_inner, w_outer, b_outer, gain_two, shift_two):
    count = tokens.shape[0]
    layout = (count // SEQ, SEQ, H, DH)
    query = low(low_back(product(tokens, w_query) + b_query))
    key = low(low_back(product(tokens, w_key)))
    value = low(low_back(product(tokens, w_value) + b_value))
    attended = lax.map(jax.checkpoint(attend_sequence), (query.reshape(layout), key.reshape(layout), value.reshape(layout)))
    attended = low(low_back(attended.reshape(count, D)))
    branch = low_back(product(attended, w_out) + b_out)
    first = layer_norm(tokens + branch, gain_one, shift_one)
    pre = low_back(product(low(first), w_inner) + b_inner)
    active = low(jax.nn.gelu(pre, approximate=False))
    second = first + low_back(product(active, w_outer) + b_outer)
    return layer_norm(second, gain_two, shift_two)

def reference(tokens, w_query, w_key, w_value, b_query, b_value, w_out, b_out, gain_one, shift_one, w_inner, b_inner, w_outer, b_outer, gain_two, shift_two, cotangent):
    params = tuple((p.astype(jnp.float32) for p in (w_query, w_key, w_value, b_query, b_value, w_out, b_out, gain_one, shift_one, w_inner, b_inner, w_outer, b_outer, gain_two, shift_two)))
    sequences = TOKENS // SEQ
    group = math.gcd(sequences, max(1, 4096 // SEQ))
    inputs = tokens.astype(jnp.float32).reshape(sequences // group, group * SEQ, D)
    cotans = cotangent.astype(jnp.float32).reshape(sequences // group, group * SEQ, D)

    def step(totals, item):
        piece, cotan = item
        result, pull = jax.vjp(forward, piece, *params)
        grads = pull(cotan)
        totals = tuple((a + b for a, b in zip(totals, grads[1:])))
        return (totals, (result.astype(jnp.bfloat16), grads[0].astype(jnp.bfloat16)))
    zeros = tuple((jnp.zeros(p.shape, jnp.float32) for p in params))
    sums, (results, d_inputs) = lax.scan(step, zeros, (inputs, cotans))
    return (results.reshape(TOKENS, D), d_inputs.reshape(TOKENS, D), sums[0], sums[1], sums[2], sums[3], sums[4], sums[5], sums[6], sums[7], sums[8], sums[9], sums[10], sums[11], sums[12], sums[13], sums[14])
```

```python
import functools

import jax
import jax.numpy as jnp
from jax import lax
from jax.experimental import pallas as pl
from jax.experimental.pallas import tpu as pltpu
from jax.sharding import PartitionSpec as P

D = 1024
H = 16
DH = 64
SEQ = 512
LANES = 128
PAIRS = D // LANES
AXES = ("rep", "shard")
RING_MOST = 16
LOW = jnp.bfloat16
FULL = jnp.float32


def project(left, right):
    return jnp.dot(left, right, preferred_element_type=FULL)


def gram(left, right):
    return lax.dot_general(left, right, (((0,), (0,)), ((), ())), preferred_element_type=FULL)


def against(left, right):
    return lax.dot_general(left, right, (((1,), (1,)), ((), ())), preferred_element_type=FULL)


def column_sum(values):
    return jnp.sum(values.astype(FULL), axis=0)


def normal(values):
    centre = values - jnp.mean(values, axis=-1, keepdims=True)
    spread = jnp.mean(centre * centre, axis=-1, keepdims=True)
    inverse = lax.rsqrt(spread + 1e-12)
    return centre * inverse, inverse


def normal_back(scaled, unit, inverse):
    mean = jnp.mean(scaled, axis=-1, keepdims=True)
    along = jnp.mean(scaled * unit, axis=-1, keepdims=True)
    return (scaled - mean - unit * along) * inverse


def head_mask(head):
    lane = lax.broadcasted_iota(jnp.int32, (SEQ, LANES), 1)
    return (lane // DH) == head


def attend_kernel(query_ref, key_ref, value_ref, out_ref, lse_ref):
    query = query_ref[...] * LOW(0.125)
    key = key_ref[...]
    value_t = value_ref[...].T
    parts = []
    for head in range(LANES // DH):
        own = jnp.where(head_mask(head), query, jnp.zeros_like(query))
        scores = against(key, own)
        top = jnp.max(scores, axis=0, keepdims=True)
        expo = jnp.exp(scores - top)
        total = jnp.sum(expo, axis=0, keepdims=True)
        mixed = project(value_t[head * DH : (head + 1) * DH], expo.astype(LOW))
        parts.append(mixed * (1.0 / total))
        lse_ref[0, head : head + 1, :] = top + jnp.log(total)
    out_ref[...] = jnp.concatenate(parts, axis=0).T.astype(LOW)


def attend_back_kernel(query_ref, key_ref, value_ref, d_ref, lse_ref, out_ref):
    pair = pl.program_id(1)
    query = query_ref[...] * LOW(0.125)
    key = key_ref[...]
    value = value_ref[...]
    d_out = d_ref[...]
    key_t = key.T
    d_key = None
    d_value = None
    d_query = []
    for head in range(LANES // DH):
        mask = head_mask(head)
        own = jnp.where(mask, query, jnp.zeros_like(query))
        d_own = jnp.where(mask, d_out, jnp.zeros_like(d_out))
        probs = jnp.exp(against(key, own) - lse_ref[0, head : head + 1, :])
        d_probs = against(value, d_own)
        inner = jnp.sum(probs * d_probs, axis=0, keepdims=True)
        d_scores = (probs * (d_probs - inner)).astype(LOW)
        part_value = project(probs.astype(LOW), d_own)
        part_key = project(d_scores, own)
        d_value = part_value if d_value is None else d_value + part_value
        d_key = part_key if d_key is None else d_key + part_key
        d_query.append(project(key_t[head * DH : (head + 1) * DH], d_scores))
    d_query = jnp.concatenate(d_query, axis=0).T * 0.125
    for place, grad in enumerate((d_query, d_key, d_value)):
        start = pl.multiple_of(place * D + pair * LANES, LANES)
        out_ref[:, pl.ds(start, LANES)] = grad.astype(LOW)


def column_block(place):
    return pl.BlockSpec((SEQ, LANES), lambda seq, pair: (seq, place * PAIRS + pair))


LSE_BLOCK = pl.BlockSpec((1, LANES // DH, SEQ), lambda seq, pair: (seq * PAIRS + pair, 0, 0))


def attend(qkv):
    count = qkv.shape[0]
    seqs = count // SEQ
    return pl.pallas_call(
        attend_kernel,
        grid=(seqs, PAIRS),
        in_specs=[column_block(0), column_block(1), column_block(2)],
        out_specs=[column_block(0), LSE_BLOCK],
        out_shape=[
            jax.ShapeDtypeStruct((count, D), LOW),
            jax.ShapeDtypeStruct((seqs * PAIRS, LANES // DH, SEQ), FULL),
        ],
        compiler_params=pltpu.CompilerParams(vmem_limit_bytes=32 * 2**20),
        name="attend",
    )(qkv, qkv, qkv)


def attend_back(qkv, d_attended, lse):
    count = qkv.shape[0]
    return pl.pallas_call(
        attend_back_kernel,
        grid=(count // SEQ, PAIRS),
        in_specs=[column_block(0), column_block(1), column_block(2), column_block(0), LSE_BLOCK],
        out_specs=pl.BlockSpec((SEQ, 3 * D), lambda seq, pair: (seq, 0)),
        out_shape=jax.ShapeDtypeStruct((count, 3 * D), LOW),
        compiler_params=pltpu.CompilerParams(vmem_limit_bytes=40 * 2**20),
        name="attend_back",
    )(qkv, qkv, qkv, d_attended, lse)


def assemble_kernel(count, size, place_ref, *refs):
    chunks, out_ref, sems = refs[:count], refs[count], refs[count + 1]
    copies = []
    for i in range(count):
        rows = chunks[i].shape[0]
        start = pl.multiple_of(place_ref[i], size)
        copies.append(pltpu.make_async_copy(chunks[i], out_ref.at[pl.ds(start, rows)], sems.at[i]))
    for copy in copies:
        copy.start()
    for copy in copies:
        copy.wait()


def assemble(chunks, places, rows):
    count = len(chunks)
    size = min(chunk.shape[0] for chunk in chunks)
    return pl.pallas_call(
        functools.partial(assemble_kernel, count, size),
        in_specs=[pl.BlockSpec(memory_space=pltpu.SMEM)] + [pl.BlockSpec(memory_space=pl.ANY)] * count,
        out_specs=pl.BlockSpec(memory_space=pl.ANY),
        out_shape=jax.ShapeDtypeStruct((rows,) + chunks[0].shape[1:], chunks[0].dtype),
        scratch_shapes=[pltpu.SemaphoreType.DMA((count,))],
        name="assemble",
    )(jnp.stack(places).astype(jnp.int32), *chunks)


class Links:
    def __init__(self, mesh):
        self.reps, self.size = mesh.shape["rep"], mesh.shape["shard"]
        size = self.size
        self.direct = size > RING_MOST or size % 2 == 1
        self.order = list(range(0, size, 2)) + list(range(size - 1, 0, -2))
        self.far = size // 2
        self.near = size - 1 - self.far
        rep = lax.axis_index("rep")
        shard = lax.axis_index("shard")
        self.core = rep % 2
        self.sign = 1 - 2 * self.core
        self.place = jnp.where(shard % 2 == 0, shard // 2, size - 1 - shard // 2)

    def owner(self, step):
        place = (self.place + self.sign * step + 2 * self.size) % self.size
        return jnp.where(place < self.size // 2, 2 * place, 2 * (self.size - place) - 1)

    def hop(self, values, sign):
        pairs = []
        for rep in range(self.reps):
            turn = sign if rep % 2 == 0 else -sign
            for i, shard in enumerate(self.order):
                target = self.order[(i + turn) % self.size]
                pairs.append((rep * self.size + shard, rep * self.size + target))
        return lax.ppermute(values, AXES, pairs)

    def swap(self, values, bit):
        pairs = []
        for rep in range(self.reps):
            for shard in range(self.size):
                pairs.append((rep * self.size + shard, (rep ^ bit) * self.size + shard))
        return lax.ppermute(values, AXES, pairs)

    def round_ring(self, values):
        found = []
        for sign, hops in ((1, self.far), (-1, self.near)):
            moving = values
            for step in range(1, hops + 1):
                moving = self.hop(moving, sign)
                found.append((moving, -sign * step))
        return found

    def gather_small(self, values):
        if self.direct:
            return lax.all_gather(values, "shard", axis=0, tiled=True)
        rows = values.shape[0]
        found = [(values, 0)] + self.round_ring(values)
        chunks = [chunk for chunk, _ in found]
        places = [self.owner(step) * rows for _, step in found]
        return assemble(chunks, places, self.size * rows)

    def gather(self, values):
        if self.direct:
            return lax.all_gather(values, "shard", axis=0, tiled=True)
        rows = values.shape[0]
        half = rows // 2
        mine = lax.dynamic_slice_in_dim(values, self.core * half, half, axis=0)
        chunks = [values]
        places = [self.owner(0) * rows]
        for chunk, step in self.round_ring(mine):
            chunks += [chunk, self.swap(chunk, 1)]
            places.append(self.owner(step) * rows + self.core * half)
            places.append(self.owner(-step) * rows + (1 - self.core) * half)
        return assemble(chunks, places, self.size * rows)

    def reduce(self, values):
        width = values.shape[1]
        rows = values.shape[0] // self.size
        if self.direct:
            own = lax.psum_scatter(values, "shard", scatter_dimension=0, tiled=True)
            return lax.psum(own, "rep").astype(FULL)
        half = rows // 2
        split = values.reshape(self.size, 2, half, width)
        other = lax.dynamic_index_in_dim(split, 1 - self.core, axis=1, keepdims=False)
        other = self.swap(other, 1)

        def piece(step):
            owner = self.owner(step)
            own = lax.dynamic_slice(split, (owner, self.core, 0, 0), (1, 1, half, width))
            pair = lax.dynamic_slice(other, (owner, 0, 0), (1, half, width))
            return own[0, 0].astype(FULL) + pair[0].astype(FULL)

        total = piece(0)
        for sign, hops in ((1, self.far), (-1, self.near)):
            moving = piece(sign * hops).astype(LOW)
            for step in range(hops - 1, -1, -1):
                moving = self.hop(moving, sign)
                if step > 0:
                    moving = (moving.astype(FULL) + piece(sign * step)).astype(LOW)
            total = total + moving.astype(FULL)
        total = total.astype(LOW)
        total = (total.astype(FULL) + self.swap(total, 2).astype(FULL)).astype(LOW)
        pair = self.swap(total, 1)
        low = jnp.where(self.core == 0, total, pair)
        high = jnp.where(self.core == 0, pair, total)
        return jnp.concatenate([low, high], axis=0).astype(FULL)


def shards(
    mesh,
    tokens,
    w_query,
    w_key,
    w_value,
    b_query,
    b_value,
    w_out,
    b_out,
    gain_one,
    shift_one,
    w_inner,
    b_inner,
    w_outer,
    b_outer,
    gain_two,
    shift_two,
    cotangent,
):
    links = Links(mesh)
    size = links.size
    width = D // size
    hidden = b_inner.shape[0]

    vectors = (b_query, b_value, b_out, gain_one, shift_one, b_outer, gain_two, shift_two)
    packed = jnp.concatenate(vectors + (b_inner,))
    used = packed.shape[0]
    room = -(-used // (32 * LANES)) * 32 * LANES
    packed = jnp.pad(packed, (0, room - used)).reshape(room // LANES, LANES)

    whole_qkv = links.gather(jnp.concatenate([w_query, w_key, w_value], axis=1))
    whole_small = links.gather_small(packed).reshape(size, room).astype(FULL)
    whole_out = links.gather(w_out)
    whole_inner = links.gather(w_inner)
    whole_outer = links.gather(w_outer)
    (bias_query, bias_value, bias_out, gain_first, shift_first, bias_outer, gain_second, shift_second) = (
        whole_small[:, i * width : (i + 1) * width].reshape(D) for i in range(len(vectors))
    )
    bias_inner = whole_small[:, used - hidden : used].reshape(size * hidden)

    bias_qkv = jnp.concatenate([bias_query, jnp.zeros((D,), FULL), bias_value])
    qkv = (project(tokens, whole_qkv) + bias_qkv).astype(LOW)
    attended, lse = attend(qkv)
    branch = project(attended, whole_out) + bias_out
    unit_one, inverse_one = normal(tokens.astype(FULL) + branch)
    first = unit_one * gain_first + shift_first
    first_low = first.astype(LOW)
    pre = project(first_low, whole_inner) + bias_inner
    below = 0.5 * (1.0 + lax.erf(pre * (0.5**0.5)))
    active = (pre * below).astype(LOW)
    slope = (below + pre * jnp.exp(-0.5 * pre * pre) * 0.3989422804014327).astype(LOW)
    second = first + project(active, whole_outer) + bias_outer
    unit_two, inverse_two = normal(second)
    output = (unit_two * gain_second + shift_second).astype(LOW)

    cot = cotangent.astype(FULL)
    grad_gain_two = jnp.sum(cot * unit_two, axis=0)
    grad_shift_two = jnp.sum(cot, axis=0)
    d_second = normal_back(cot * gain_second, unit_two, inverse_two)
    d_mid = d_second.astype(LOW)
    own_outer = links.reduce(gram(active, d_mid).astype(LOW))
    grad_b_outer = column_sum(d_mid)
    d_pre = (against(d_mid, whole_outer) * slope.astype(FULL)).astype(LOW)
    own_inner = links.reduce(gram(first_low, d_pre).astype(LOW))
    grad_b_inner = column_sum(d_pre)
    d_first = d_second + against(d_pre, whole_inner)
    grad_gain_one = jnp.sum(d_first * unit_one, axis=0)
    grad_shift_one = jnp.sum(d_first, axis=0)
    d_inner = normal_back(d_first * gain_first, unit_one, inverse_one)
    d_branch = d_inner.astype(LOW)
    own_out = links.reduce(gram(attended, d_branch).astype(LOW))
    grad_b_out = column_sum(d_branch)
    d_attended = against(d_branch, whole_out).astype(LOW)
    d_qkv = attend_back(qkv, d_attended, lse)
    own_qkv = links.reduce(gram(tokens, d_qkv).astype(LOW))
    grad_b_qkv = column_sum(d_qkv)
    d_tokens = (d_inner + against(d_qkv, whole_qkv)).astype(LOW)

    grads = (
        grad_b_qkv[:D],
        grad_b_qkv[2 * D :],
        grad_b_out,
        grad_gain_one,
        grad_shift_one,
        grad_b_outer,
        grad_gain_two,
        grad_shift_two,
    )
    small = jnp.concatenate(
        [grad.reshape(size, width) for grad in grads] + [grad_b_inner.reshape(size, hidden)], axis=1
    )
    small = jnp.pad(small, ((0, 0), (0, room - used))).astype(LOW)
    own_small = links.reduce(small.reshape(size * (room // LANES), LANES)).reshape(room)
    (
        own_bias_query,
        own_bias_value,
        own_bias_out,
        own_gain_one,
        own_shift_one,
        own_bias_outer,
        own_gain_two,
        own_shift_two,
    ) = (own_small[i * width : (i + 1) * width] for i in range(len(vectors)))
    own_bias_inner = own_small[used - hidden : used]
    return (
        output,
        d_tokens,
        own_qkv[:, :D],
        own_qkv[:, D : 2 * D],
        own_qkv[:, 2 * D :],
        own_bias_query,
        own_bias_value,
        own_out,
        own_bias_out,
        own_gain_one,
        own_shift_one,
        own_inner,
        own_bias_inner,
        own_outer,
        own_bias_outer,
        own_gain_two,
        own_shift_two,
    )


def solution(mesh):
    rows = P(("rep", "shard"), None)
    matrix = P("shard", None)
    vector = P("shard")
    return jax.shard_map(
        functools.partial(shards, mesh),
        mesh=mesh,
        in_specs=(
            rows,
            matrix,
            matrix,
            matrix,
            vector,
            vector,
            matrix,
            vector,
            vector,
            vector,
            matrix,
            vector,
            matrix,
            vector,
            vector,
            vector,
            rows,
        ),
        out_specs=(
            rows,
            rows,
            matrix,
            matrix,
            matrix,
            vector,
            vector,
            matrix,
            vector,
            vector,
            vector,
            matrix,
            vector,
            matrix,
            vector,
            vector,
            vector,
        ),
        check_vma=False,
    )
```

```python
import functools

import jax
import jax.numpy as jnp
from jax import lax
from jax.experimental import pallas as pl
from jax.experimental.pallas import tpu as pltpu
from jax.sharding import PartitionSpec as P

D = 1024
H = 16
DH = 64
SEQ = 512
LANES = 128
GROUPS = 2
PAIRS = D // LANES // GROUPS
WIDE = D // GROUPS
AXES = ("rep", "shard")
RING_MOST = 16
LOW = jnp.bfloat16
FULL = jnp.float32


def project(left, right):
    return jnp.dot(left, right, preferred_element_type=FULL)


def gram(left, right):
    return lax.dot_general(left, right, (((0,), (0,)), ((), ())), preferred_element_type=FULL)


def against(left, right):
    return lax.dot_general(left, right, (((1,), (1,)), ((), ())), preferred_element_type=FULL)


def column_sum(values):
    return jnp.sum(values.astype(FULL), axis=0)


def normal(values):
    centre = values - jnp.mean(values, axis=-1, keepdims=True)
    spread = jnp.mean(centre * centre, axis=-1, keepdims=True)
    inverse = lax.rsqrt(spread + 1e-12)
    return centre * inverse, inverse


def normal_back(scaled, unit, inverse):
    mean = jnp.mean(scaled, axis=-1, keepdims=True)
    along = jnp.mean(scaled * unit, axis=-1, keepdims=True)
    return (scaled - mean - unit * along) * inverse


def head_mask(head):
    lane = lax.broadcasted_iota(jnp.int32, (SEQ, LANES), 1)
    return (lane // DH) == head


def attend_kernel(query_ref, key_ref, value_ref, *rest):
    out_ref, lse_ref = rest[-2:]
    query = query_ref[...] * LOW(0.125)
    key = key_ref[...]
    value_t = value_ref[...].T
    parts = []
    for head in range(LANES // DH):
        own = jnp.where(head_mask(head), query, jnp.zeros_like(query))
        scores = against(key, own)
        top = jnp.max(scores, axis=0, keepdims=True)
        expo = jnp.exp(scores - top)
        total = jnp.sum(expo, axis=0, keepdims=True)
        mixed = project(value_t[head * DH : (head + 1) * DH], expo.astype(LOW))
        parts.append(mixed * (1.0 / total))
        lse_ref[0, head : head + 1, :] = top + jnp.log(total)
    out_ref[...] = jnp.concatenate(parts, axis=0).T.astype(LOW)


def attend_back_kernel(query_ref, key_ref, value_ref, d_ref, lse_ref, out_ref):
    pair = pl.program_id(1)
    query = query_ref[...] * LOW(0.125)
    key = key_ref[...]
    value = value_ref[...]
    d_out = d_ref[...]
    key_t = key.T
    d_key = None
    d_value = None
    d_query = []
    for head in range(LANES // DH):
        mask = head_mask(head)
        own = jnp.where(mask, query, jnp.zeros_like(query))
        d_own = jnp.where(mask, d_out, jnp.zeros_like(d_out))
        probs = jnp.exp(against(key, own) - lse_ref[0, head : head + 1, :])
        d_probs = against(value, d_own)
        inner = jnp.sum(probs * d_probs, axis=0, keepdims=True)
        d_scores = (probs * (d_probs - inner)).astype(LOW)
        part_value = project(probs.astype(LOW), d_own)
        part_key = project(d_scores, own)
        d_value = part_value if d_value is None else d_value + part_value
        d_key = part_key if d_key is None else d_key + part_key
        d_query.append(project(key_t[head * DH : (head + 1) * DH], d_scores))
    d_query = jnp.concatenate(d_query, axis=0).T * 0.125
    for place, grad in enumerate((d_query, d_key, d_value)):
        start = pl.multiple_of(place * WIDE + pair * LANES, LANES)
        out_ref[:, pl.ds(start, LANES)] = grad.astype(LOW)


def column_block(first):
    return pl.BlockSpec((SEQ, LANES), lambda seq, pair: (seq, first + pair))


LSE_BLOCK = pl.BlockSpec((1, LANES // DH, SEQ), lambda seq, pair: (seq * PAIRS + pair, 0, 0))


def triple():
    return [column_block(place * PAIRS) for place in range(3)]


def attend(qkv, group, before):
    count = qkv.shape[0]
    seqs = count // SEQ
    kept = [] if before is None else [before]
    return pl.pallas_call(
        attend_kernel,
        grid=(seqs, PAIRS),
        in_specs=triple() + [pl.BlockSpec(memory_space=pl.ANY)] * len(kept),
        out_specs=[column_block(group * PAIRS), LSE_BLOCK],
        out_shape=[
            jax.ShapeDtypeStruct((count, D), LOW),
            jax.ShapeDtypeStruct((seqs * PAIRS, LANES // DH, SEQ), FULL),
        ],
        input_output_aliases={3: 0} if kept else {},
        compiler_params=pltpu.CompilerParams(vmem_limit_bytes=32 * 2**20),
        name="attend",
    )(qkv, qkv, qkv, *kept)


def attend_back(qkv, d_attended, lse, group):
    count = qkv.shape[0]
    return pl.pallas_call(
        attend_back_kernel,
        grid=(count // SEQ, PAIRS),
        in_specs=triple() + [column_block(group * PAIRS), LSE_BLOCK],
        out_specs=pl.BlockSpec((SEQ, 3 * WIDE), lambda seq, pair: (seq, 0)),
        out_shape=jax.ShapeDtypeStruct((count, 3 * WIDE), LOW),
        compiler_params=pltpu.CompilerParams(vmem_limit_bytes=40 * 2**20),
        name="attend_back",
    )(qkv, qkv, qkv, d_attended, lse)


def assemble_kernel(moves, align, place_ref, *refs):
    out_ref, sems = refs[-2], refs[-1]
    copies = []
    for i, (which, start, rows) in enumerate(moves):
        place = pl.multiple_of(place_ref[i], align)
        source = refs[which].at[pl.ds(start, rows)]
        copies.append(pltpu.make_async_copy(source, out_ref.at[pl.ds(place, rows)], sems.at[i]))
    for copy in copies:
        copy.start()
    for copy in copies:
        copy.wait()


def assemble(arrays, moves, places, rows):
    align = min(move[2] for move in moves)
    return pl.pallas_call(
        functools.partial(assemble_kernel, moves, align),
        in_specs=[pl.BlockSpec(memory_space=pltpu.SMEM)] + [pl.BlockSpec(memory_space=pl.ANY)] * len(arrays),
        out_specs=pl.BlockSpec(memory_space=pltpu.VMEM),
        out_shape=jax.ShapeDtypeStruct((rows,) + arrays[0].shape[1:], arrays[0].dtype),
        scratch_shapes=[pltpu.SemaphoreType.DMA((len(moves),))],
        compiler_params=pltpu.CompilerParams(vmem_limit_bytes=24 * 2**20),
        name="assemble",
    )(jnp.stack(places).astype(jnp.int32), *arrays)


def tie(*values):
    return lax.optimization_barrier(values)


class Links:
    def __init__(self, mesh):
        self.reps, self.size = mesh.shape["rep"], mesh.shape["shard"]
        size = self.size
        self.direct = size > RING_MOST or size % 2 == 1
        self.order = list(range(0, size, 2)) + list(range(size - 1, 0, -2))
        self.far = size // 2
        self.near = size - 1 - self.far
        rep = lax.axis_index("rep")
        shard = lax.axis_index("shard")
        self.core = rep % 2
        self.sign = 1 - 2 * self.core
        self.place = jnp.where(shard % 2 == 0, shard // 2, size - 1 - shard // 2)

    def owner(self, step):
        place = (self.place + self.sign * step + 2 * self.size) % self.size
        return jnp.where(place < self.size // 2, 2 * place, 2 * (self.size - place) - 1)

    def hop(self, values, sign):
        pairs = []
        for rep in range(self.reps):
            turn = sign if rep % 2 == 0 else -sign
            for i, shard in enumerate(self.order):
                target = self.order[(i + turn) % self.size]
                pairs.append((rep * self.size + shard, rep * self.size + target))
        return lax.ppermute(values, AXES, pairs)

    def swap(self, values, bit):
        pairs = []
        for rep in range(self.reps):
            for shard in range(self.size):
                pairs.append((rep * self.size + shard, (rep ^ bit) * self.size + shard))
        return lax.ppermute(values, AXES, pairs)

    def half_of(self, values):
        half = values.shape[0] // 2
        return lax.dynamic_slice_in_dim(values, self.core * half, half, axis=0)


    def gather_small(self, values):
        if self.direct:
            return lax.all_gather(values, "shard", axis=0, tiled=True)
        rows = values.shape[0]
        found = [(values, 0)]
        ahead = back = values
        for step in range(1, self.far + 1):
            ahead = self.hop(ahead, 1)
            found.append((ahead, -step))
            if step <= self.near:
                back = self.hop(back, -1)
                found.append((back, step))
            ahead, back = yield [ahead, back]
        moves = [(i, 0, rows) for i in range(len(found))]
        places = [self.owner(step) * rows for _, step in found]
        return assemble([chunk for chunk, _ in found], moves, places, self.size * rows)

    def gather(self, values):
        if self.direct:
            return lax.all_gather(values, "shard", axis=0, tiled=True)
        rows = values.shape[0]
        half = rows // 2
        arrays = [values]
        moves = [(0, 0, rows)]
        places = [self.owner(0) * rows]

        def keep(chunk, mine, step):
            moves.append((len(arrays), 0, half))
            arrays.append(chunk)
            core = self.core if mine else 1 - self.core
            places.append(self.owner(step) * rows + core * half)

        ahead = back = self.half_of(values)
        for step in range(1, self.far + 2):
            flight = []
            if step > 1:
                keep(ahead, True, 1 - step)
                flight.append((self.swap(ahead, 1), step - 1))
                if step - 1 <= self.near:
                    keep(back, True, step - 1)
                    flight.append((self.swap(back, 1), 1 - step))
            if step <= self.far:
                ahead = self.hop(ahead, 1)
            if step <= self.near:
                back = self.hop(back, -1)
            ahead, back, *swapped = yield [ahead, back] + [chunk for chunk, _ in flight]
            for chunk, (_, place) in zip(swapped, flight):
                keep(chunk, False, place)
        return assemble(arrays, moves, places, self.size * rows)

    def gather_halves(self, values):
        if self.direct:
            return lax.all_gather(values, "shard", axis=0, tiled=True)
        rows = values.shape[0]
        half = rows // 2
        mine = lax.all_gather(self.half_of(values), "shard", axis=0, tiled=True)
        other = self.swap(mine, 1)
        moves, places = [], []
        for shard in range(self.size):
            moves += [(0, shard * half, half), (1, shard * half, half)]
            places += [shard * rows + self.core * half, shard * rows + (1 - self.core) * half]
        return assemble([mine, other], moves, places, self.size * rows)

    def gather_quarters(self, values):
        rows = values.shape[0] // self.reps
        mine = lax.dynamic_slice_in_dim(values, lax.axis_index("rep") * rows, rows, axis=0)
        return lax.all_gather(mine, ("shard", "rep"), axis=0, tiled=True)

    def reduce_halves(self, values):
        if self.direct:
            own = lax.psum_scatter(values, "shard", scatter_dimension=0, tiled=True)
            return lax.psum(own, "rep").astype(FULL)
        width = values.shape[1]
        half = values.shape[0] // self.size // 2
        split = values.reshape(self.size, 2, half, width)
        other = self.swap(lax.dynamic_index_in_dim(split, 1 - self.core, axis=1, keepdims=False), 1)
        (other,) = yield [other]
        mine = lax.dynamic_index_in_dim(split, self.core, axis=1, keepdims=False)
        total = (mine.astype(FULL) + other.astype(FULL)).astype(LOW)
        total = total.reshape(self.size * half, width)
        return lax.psum_scatter(total, "shard", scatter_dimension=0, tiled=True)

    def finish(self, total):
        total = (total.astype(FULL) + self.swap(total, 2).astype(FULL)).astype(LOW)
        pair = self.swap(total, 1)
        low = jnp.where(self.core == 0, total, pair)
        high = jnp.where(self.core == 0, pair, total)
        return jnp.concatenate([low, high], axis=0).astype(FULL)

    def reduce(self, values):
        if self.direct:
            own = lax.psum_scatter(values, "shard", scatter_dimension=0, tiled=True)
            return lax.psum(own, "rep").astype(FULL)
        width = values.shape[1]
        half = values.shape[0] // self.size // 2
        split = values.reshape(self.size, 2, half, width)
        other = self.swap(lax.dynamic_index_in_dim(split, 1 - self.core, axis=1, keepdims=False), 1)
        (other,) = yield [other]

        def piece(step):
            owner = self.owner(step)
            own = lax.dynamic_slice(split, (owner, self.core, 0, 0), (1, 1, half, width))
            pair = lax.dynamic_slice(other, (owner, 0, 0), (1, half, width))
            return own[0, 0].astype(FULL) + pair[0].astype(FULL)

        ahead = piece(self.far).astype(LOW)
        back = piece(-self.near).astype(LOW)
        for step in range(self.far - 1, -1, -1):
            moving = [self.hop(ahead, 1)]
            if step < self.near:
                moving.append(self.hop(back, -1))
            ahead, *rest = yield moving
            if step > 0:
                ahead = (ahead.astype(FULL) + piece(step)).astype(LOW)
            if rest:
                back = rest[0]
                if step > 0:
                    back = (back.astype(FULL) + piece(-step)).astype(LOW)
        total = (piece(0) + ahead.astype(FULL) + back.astype(FULL)).astype(LOW)
        (cross,) = yield [self.swap(total, 2)]
        total = (total.astype(FULL) + cross.astype(FULL)).astype(LOW)
        (pair,) = yield [self.swap(total, 1)]
        low = jnp.where(self.core == 0, total, pair)
        high = jnp.where(self.core == 0, pair, total)
        return jnp.concatenate([low, high], axis=0).astype(FULL)


class Flow:
    def __init__(self):
        self.running = {}
        self.results = {}

    def start(self, name, steps):
        self._move(name, steps, None)

    def _move(self, name, steps, values):
        try:
            self.running[name] = (steps, steps.send(values))
        except StopIteration as end:
            self.running.pop(name, None)
            self.results[name] = end.value

    def advance(self, *values):
        running = list(self.running.items())
        flat = list(values)
        for _, (_, flight) in running:
            flat += flight
        tied = tie(*flat) if flat else ()
        at = len(values)
        for name, (steps, flight) in running:
            self._move(name, steps, list(tied[at : at + len(flight)]))
            at += len(flight)
        return tied[0] if len(values) == 1 else tuple(tied[: len(values)])

    def take(self, name):
        while name in self.running:
            steps, flight = self.running[name]
            self._move(name, steps, flight)
        return self.results[name]


def shards(
    mesh,
    tokens,
    w_query,
    w_key,
    w_value,
    b_query,
    b_value,
    w_out,
    b_out,
    gain_one,
    shift_one,
    w_inner,
    b_inner,
    w_outer,
    b_outer,
    gain_two,
    shift_two,
    cotangent,
):
    links = Links(mesh)
    size = links.size
    width = D // size
    hidden = b_inner.shape[0]

    vectors = (b_query, b_value, b_out, gain_one, shift_one, b_outer, gain_two, shift_two)
    packed = jnp.concatenate(vectors + (b_inner,))
    used = packed.shape[0]
    room = -(-used // (32 * LANES)) * 32 * LANES
    packed = jnp.pad(packed, (0, room - used)).reshape(room // LANES, LANES)

    own_groups = [
        jnp.concatenate([w[:, g * WIDE : (g + 1) * WIDE] for w in (w_query, w_key, w_value)], axis=1)
        for g in range(GROUPS)
    ]
    flow = Flow()
    flow.start("group0", links.gather(own_groups[0]))
    flow.start("small", links.gather_small(packed))
    own_groups[1], w_out, w_inner, w_outer = flow.advance(own_groups[1], w_out, w_inner, w_outer)
    flow.start("group1", links.gather(own_groups[1]))
    flow.advance()
    w_inner, w_outer = flow.advance(w_inner, w_outer)
    whole_inner = links.gather_halves(w_inner)
    whole_outer = links.gather_quarters(w_outer)
    flow.advance()
    whole_groups = [flow.take("group0")]
    whole_small = flow.take("small").reshape(size, room).astype(FULL)
    (bias_query, bias_value, bias_out, gain_first, shift_first, bias_outer, gain_second, shift_second) = (
        whole_small[:, i * width : (i + 1) * width].reshape(D) for i in range(len(vectors))
    )
    bias_inner = whole_small[:, used - hidden : used].reshape(size * hidden)

    no_bias = jnp.zeros((WIDE,), FULL)
    projected = []
    attended, lse = None, []
    for g in range(GROUPS):
        columns = slice(g * WIDE, (g + 1) * WIDE)
        bias = jnp.concatenate([bias_query[columns], no_bias, bias_value[columns]])
        projected.append((project(tokens, whole_groups[g]) + bias).astype(LOW))
        if g == 0:
            projected[g], w_out = flow.advance(projected[g], w_out)
            flow.start("out", links.gather(w_out))
        else:
            projected[g] = flow.advance(projected[g])
        attended, kept = attend(projected[g], g, attended)
        lse.append(kept)
        attended = flow.advance(attended)
        if g == 0:
            whole_groups.append(flow.take("group1"))
    whole_out = flow.take("out")
    branch = project(attended, whole_out) + bias_out
    unit_one, inverse_one = normal(tokens.astype(FULL) + branch)
    first = unit_one * gain_first + shift_first
    first_low = first.astype(LOW)
    pre = project(first_low, whole_inner) + bias_inner
    below = 0.5 * (1.0 + lax.erf(pre * (0.5**0.5)))
    active = (pre * below).astype(LOW)
    slope = (below + pre * jnp.exp(-0.5 * pre * pre) * 0.3989422804014327).astype(LOW)
    second = first + project(active, whole_outer) + bias_outer
    unit_two, inverse_two = normal(second)
    output = (unit_two * gain_second + shift_second).astype(LOW)

    cot = cotangent.astype(FULL)
    grad_gain_two = jnp.sum(cot * unit_two, axis=0)
    grad_shift_two = jnp.sum(cot, axis=0)
    d_second = normal_back(cot * gain_second, unit_two, inverse_two)
    d_mid = d_second.astype(LOW)
    grad_outer = gram(active, d_mid).astype(LOW)
    grad_outer, d_mid = tie(grad_outer, d_mid)
    flow.start("outer", links.reduce(grad_outer))
    grad_b_outer = column_sum(d_mid)
    d_pre = (against(d_mid, whole_outer) * slope.astype(FULL)).astype(LOW)
    d_pre = flow.advance(d_pre)
    grad_inner = gram(first_low, d_pre).astype(LOW)
    grad_inner, d_pre = flow.advance(grad_inner, d_pre)
    flow.start("inner", links.reduce(grad_inner))
    grad_b_inner = column_sum(d_pre)
    d_first = d_second + against(d_pre, whole_inner)
    d_first = flow.advance(d_first)
    grad_gain_one = jnp.sum(d_first * unit_one, axis=0)
    grad_shift_one = jnp.sum(d_first, axis=0)
    d_inner = normal_back(d_first * gain_first, unit_one, inverse_one)
    d_branch = d_inner.astype(LOW)
    grad_out = gram(attended, d_branch).astype(LOW)
    grad_out, d_branch = flow.advance(grad_out, d_branch)
    flow.start("out_back", links.reduce(grad_out))
    grad_b_out = column_sum(d_branch)
    d_attended = against(d_branch, whole_out).astype(LOW)
    grad_b_groups = []
    d_tokens = d_inner
    for g in range(GROUPS):
        d_group = attend_back(projected[g], d_attended, lse[g], g)
        d_group = flow.advance(d_group)
        grad_group = gram(tokens, d_group).astype(LOW)
        grad_group, d_group, d_attended = flow.advance(grad_group, d_group, d_attended)
        flow.start(f"back{g}", links.reduce(grad_group))
        grad_b_groups.append(column_sum(d_group))
        d_tokens = d_tokens + against(d_group, whole_groups[g])
    d_tokens = d_tokens.astype(LOW)

    def joined(parts, place):
        columns = slice(place * WIDE, (place + 1) * WIDE)
        return jnp.concatenate([part[..., columns] for part in parts], axis=-1)

    grads = (
        joined(grad_b_groups, 0),
        joined(grad_b_groups, 2),
        grad_b_out,
        grad_gain_one,
        grad_shift_one,
        grad_b_outer,
        grad_gain_two,
        grad_shift_two,
    )
    small = jnp.concatenate(
        [grad.reshape(size, width) for grad in grads] + [grad_b_inner.reshape(size, hidden)], axis=1
    )
    small = jnp.pad(small, ((0, 0), (0, room - used))).astype(LOW)
    flow.start("small_back", links.reduce(small.reshape(size * (room // LANES), LANES)))
    own_outer = flow.take("outer")
    own_inner = flow.take("inner")
    own_out = flow.take("out_back")
    own_small = flow.take("small_back").reshape(room)
    own_groups = [flow.take(f"back{g}") for g in range(GROUPS)]
    (
        own_bias_query,
        own_bias_value,
        own_bias_out,
        own_gain_one,
        own_shift_one,
        own_bias_outer,
        own_gain_two,
        own_shift_two,
    ) = (own_small[i * width : (i + 1) * width] for i in range(len(vectors)))
    own_bias_inner = own_small[used - hidden : used]
    return (
        output,
        d_tokens,
        joined(own_groups, 0),
        joined(own_groups, 1),
        joined(own_groups, 2),
        own_bias_query,
        own_bias_value,
        own_out,
        own_bias_out,
        own_gain_one,
        own_shift_one,
        own_inner,
        own_bias_inner,
        own_outer,
        own_bias_outer,
        own_gain_two,
        own_shift_two,
    )


def solution(mesh):
    rows = P(("rep", "shard"), None)
    matrix = P("shard", None)
    vector = P("shard")
    return jax.shard_map(
        functools.partial(shards, mesh),
        mesh=mesh,
        in_specs=(
            rows,
            matrix,
            matrix,
            matrix,
            vector,
            vector,
            matrix,
            vector,
            vector,
            vector,
            matrix,
            vector,
            matrix,
            vector,
            vector,
            vector,
            rows,
        ),
        out_specs=(
            rows,
            rows,
            matrix,
            matrix,
            matrix,
            vector,
            vector,
            matrix,
            vector,
            vector,
            vector,
            matrix,
            vector,
            matrix,
            vector,
            vector,
            vector,
        ),
        check_vma=False,
    )
```

```python
import functools

import jax
import jax.numpy as jnp
from jax import lax
from jax.experimental import pallas as pl
from jax.experimental.pallas import tpu as pltpu
from jax.sharding import PartitionSpec as P

D = 1024
H = 16
DH = 64
SEQ = 512
LANES = 128
GROUPS = 2
PAIRS = D // LANES // GROUPS
WIDE = D // GROUPS
AXES = ("rep", "shard")
RING_MOST = 16
LOW = jnp.bfloat16
FULL = jnp.float32


def project(left, right):
    return jnp.dot(left, right, preferred_element_type=FULL)


def gram(left, right):
    return lax.dot_general(left, right, (((0,), (0,)), ((), ())), preferred_element_type=FULL)


def against(left, right):
    return lax.dot_general(left, right, (((1,), (1,)), ((), ())), preferred_element_type=FULL)


def column_sum(values):
    return jnp.sum(values.astype(FULL), axis=0)


def normal(values):
    centre = values - jnp.mean(values, axis=-1, keepdims=True)
    spread = jnp.mean(centre * centre, axis=-1, keepdims=True)
    inverse = lax.rsqrt(spread + 1e-12)
    return centre * inverse, inverse


def normal_back(scaled, unit, inverse):
    mean = jnp.mean(scaled, axis=-1, keepdims=True)
    along = jnp.mean(scaled * unit, axis=-1, keepdims=True)
    return (scaled - mean - unit * along) * inverse


def head_mask(head):
    lane = lax.broadcasted_iota(jnp.int32, (SEQ, LANES), 1)
    return (lane // DH) == head


def attend_kernel(query_ref, key_ref, value_ref, *rest):
    out_ref, lse_ref = rest[-2:]
    query = query_ref[...] * LOW(0.125)
    key = key_ref[...]
    value_t = value_ref[...].T
    parts = []
    for head in range(LANES // DH):
        own = jnp.where(head_mask(head), query, jnp.zeros_like(query))
        scores = against(key, own)
        top = jnp.max(scores, axis=0, keepdims=True)
        expo = jnp.exp(scores - top)
        total = jnp.sum(expo, axis=0, keepdims=True)
        mixed = project(value_t[head * DH : (head + 1) * DH], expo.astype(LOW))
        parts.append(mixed * (1.0 / total))
        lse_ref[0, head : head + 1, :] = top + jnp.log(total)
    out_ref[...] = jnp.concatenate(parts, axis=0).T.astype(LOW)


def attend_back_kernel(query_ref, key_ref, value_ref, d_ref, lse_ref, out_ref):
    pair = pl.program_id(1)
    query = query_ref[...] * LOW(0.125)
    key = key_ref[...]
    value = value_ref[...]
    d_out = d_ref[...]
    key_t = key.T
    d_key = None
    d_value = None
    d_query = []
    for head in range(LANES // DH):
        mask = head_mask(head)
        own = jnp.where(mask, query, jnp.zeros_like(query))
        d_own = jnp.where(mask, d_out, jnp.zeros_like(d_out))
        probs = jnp.exp(against(key, own) - lse_ref[0, head : head + 1, :])
        d_probs = against(value, d_own)
        inner = jnp.sum(probs * d_probs, axis=0, keepdims=True)
        d_scores = (probs * (d_probs - inner)).astype(LOW)
        part_value = project(probs.astype(LOW), d_own)
        part_key = project(d_scores, own)
        d_value = part_value if d_value is None else d_value + part_value
        d_key = part_key if d_key is None else d_key + part_key
        d_query.append(project(key_t[head * DH : (head + 1) * DH], d_scores))
    d_query = jnp.concatenate(d_query, axis=0).T * 0.125
    for place, grad in enumerate((d_query, d_key, d_value)):
        start = pl.multiple_of(place * WIDE + pair * LANES, LANES)
        out_ref[:, pl.ds(start, LANES)] = grad.astype(LOW)


def column_block(first):
    return pl.BlockSpec((SEQ, LANES), lambda seq, pair: (seq, first + pair))


LSE_BLOCK = pl.BlockSpec((1, LANES // DH, SEQ), lambda seq, pair: (seq * PAIRS + pair, 0, 0))


def triple():
    return [column_block(place * PAIRS) for place in range(3)]


def attend(qkv, group, before):
    count = qkv.shape[0]
    seqs = count // SEQ
    kept = [] if before is None else [before]
    return pl.pallas_call(
        attend_kernel,
        grid=(seqs, PAIRS),
        in_specs=triple() + [pl.BlockSpec(memory_space=pl.ANY)] * len(kept),
        out_specs=[column_block(group * PAIRS), LSE_BLOCK],
        out_shape=[
            jax.ShapeDtypeStruct((count, D), LOW),
            jax.ShapeDtypeStruct((seqs * PAIRS, LANES // DH, SEQ), FULL),
        ],
        input_output_aliases={3: 0} if kept else {},
        compiler_params=pltpu.CompilerParams(vmem_limit_bytes=32 * 2**20),
        name="attend",
    )(qkv, qkv, qkv, *kept)


def attend_back(qkv, d_attended, lse, group):
    count = qkv.shape[0]
    return pl.pallas_call(
        attend_back_kernel,
        grid=(count // SEQ, PAIRS),
        in_specs=triple() + [column_block(group * PAIRS), LSE_BLOCK],
        out_specs=pl.BlockSpec((SEQ, 3 * WIDE), lambda seq, pair: (seq, 0)),
        out_shape=jax.ShapeDtypeStruct((count, 3 * WIDE), LOW),
        compiler_params=pltpu.CompilerParams(vmem_limit_bytes=40 * 2**20),
        name="attend_back",
    )(qkv, qkv, qkv, d_attended, lse)


def assemble_kernel(moves, align, place_ref, *refs):
    out_ref, sems = refs[-2], refs[-1]
    copies = []
    for i, (which, start, rows) in enumerate(moves):
        place = pl.multiple_of(place_ref[i], align)
        source = refs[which].at[pl.ds(start, rows)]
        copies.append(pltpu.make_async_copy(source, out_ref.at[pl.ds(place, rows)], sems.at[i]))
    for copy in copies:
        copy.start()
    for copy in copies:
        copy.wait()


def assemble(arrays, moves, places, rows):
    align = min(move[2] for move in moves)
    return pl.pallas_call(
        functools.partial(assemble_kernel, moves, align),
        in_specs=[pl.BlockSpec(memory_space=pltpu.SMEM)] + [pl.BlockSpec(memory_space=pl.ANY)] * len(arrays),
        out_specs=pl.BlockSpec(memory_space=pltpu.VMEM),
        out_shape=jax.ShapeDtypeStruct((rows,) + arrays[0].shape[1:], arrays[0].dtype),
        scratch_shapes=[pltpu.SemaphoreType.DMA((len(moves),))],
        compiler_params=pltpu.CompilerParams(vmem_limit_bytes=24 * 2**20),
        name="assemble",
    )(jnp.stack(places).astype(jnp.int32), *arrays)


def pack_kernel(size, rows, *refs):
    out_ref = refs[-1]
    out_ref[...] = jnp.zeros_like(out_ref)
    for shard in range(size):
        at = 0
        for ref in refs[:-1]:
            width = ref.shape[1] // size
            for start in range(0, width, LANES):
                count = min(LANES, width - start)
                line = ref[:, shard * width + start : shard * width + start + count]
                out_ref[shard * rows + at : shard * rows + at + 1, :count] = line
                at += 1


def pack(vectors, size, rows):
    if vectors[0].shape[1] // size < LANES:
        small = jnp.concatenate([vector.reshape(size, -1) for vector in vectors], axis=1)
        small = jnp.pad(small, ((0, 0), (0, rows * LANES - small.shape[1])))
        return small.reshape(size * rows, LANES).astype(LOW)
    return pl.pallas_call(
        functools.partial(pack_kernel, size, rows),
        out_shape=jax.ShapeDtypeStruct((size * rows, LANES), FULL),
        name="pack",
    )(*vectors).astype(LOW)


def tie(*values):
    return lax.optimization_barrier(values)


class Links:
    def __init__(self, mesh):
        self.reps, self.size = mesh.shape["rep"], mesh.shape["shard"]
        size = self.size
        self.direct = size > RING_MOST or size % 2 == 1
        self.order = list(range(0, size, 2)) + list(range(size - 1, 0, -2))
        self.far = size // 2
        self.near = size - 1 - self.far
        rep = lax.axis_index("rep")
        shard = lax.axis_index("shard")
        self.core = rep % 2
        self.sign = 1 - 2 * self.core
        self.place = jnp.where(shard % 2 == 0, shard // 2, size - 1 - shard // 2)

    def owner(self, step):
        place = (self.place + self.sign * step + 2 * self.size) % self.size
        return jnp.where(place < self.size // 2, 2 * place, 2 * (self.size - place) - 1)

    def hop(self, values, sign):
        pairs = []
        for rep in range(self.reps):
            turn = sign if rep % 2 == 0 else -sign
            for i, shard in enumerate(self.order):
                target = self.order[(i + turn) % self.size]
                pairs.append((rep * self.size + shard, rep * self.size + target))
        return lax.ppermute(values, AXES, pairs)

    def swap(self, values, bit):
        pairs = []
        for rep in range(self.reps):
            for shard in range(self.size):
                pairs.append((rep * self.size + shard, (rep ^ bit) * self.size + shard))
        return lax.ppermute(values, AXES, pairs)

    def half_of(self, values):
        half = values.shape[0] // 2
        return lax.dynamic_slice_in_dim(values, self.core * half, half, axis=0)


    def gather_small(self, values):
        if self.direct:
            return lax.all_gather(values, "shard", axis=0, tiled=True)
        rows = values.shape[0]
        found = [(values, 0)]
        ahead = back = values
        for step in range(1, self.far + 1):
            ahead = self.hop(ahead, 1)
            found.append((ahead, -step))
            if step <= self.near:
                back = self.hop(back, -1)
                found.append((back, step))
            ahead, back = yield [ahead, back]
        moves = [(i, 0, rows) for i in range(len(found))]
        places = [self.owner(step) * rows for _, step in found]
        return assemble([chunk for chunk, _ in found], moves, places, self.size * rows)

    def gather(self, values):
        if self.direct:
            return lax.all_gather(values, "shard", axis=0, tiled=True)
        rows = values.shape[0]
        half = rows // 2
        arrays = [values]
        moves = [(0, 0, rows)]
        places = [self.owner(0) * rows]

        def keep(chunk, mine, step):
            moves.append((len(arrays), 0, half))
            arrays.append(chunk)
            core = self.core if mine else 1 - self.core
            places.append(self.owner(step) * rows + core * half)

        ahead = back = self.half_of(values)
        for step in range(1, self.far + 2):
            flight = []
            if step > 1:
                keep(ahead, True, 1 - step)
                flight.append((self.swap(ahead, 1), step - 1))
                if step - 1 <= self.near:
                    keep(back, True, step - 1)
                    flight.append((self.swap(back, 1), 1 - step))
            if step <= self.far:
                ahead = self.hop(ahead, 1)
            if step <= self.near:
                back = self.hop(back, -1)
            ahead, back, *swapped = yield [ahead, back] + [chunk for chunk, _ in flight]
            for chunk, (_, place) in zip(swapped, flight):
                keep(chunk, False, place)
        return assemble(arrays, moves, places, self.size * rows)

    def gather_quarters(self, values):
        rows = values.shape[0] // self.reps
        mine = lax.dynamic_slice_in_dim(values, lax.axis_index("rep") * rows, rows, axis=0)
        return lax.all_gather(mine, ("shard", "rep"), axis=0, tiled=True)

    def scatter_quarters(self, values):
        return lax.psum_scatter(values, ("shard", "rep"), scatter_dimension=0, tiled=True)

    def join_quarters(self, values):
        return lax.all_gather(values, "rep", axis=0, tiled=True).astype(FULL)

    def reduce(self, values):
        if self.direct:
            own = lax.psum_scatter(values, "shard", scatter_dimension=0, tiled=True)
            return lax.psum(own, "rep").astype(FULL)
        width = values.shape[1]
        half = values.shape[0] // self.size // 2
        split = values.reshape(self.size, 2, half, width)
        other = self.swap(lax.dynamic_index_in_dim(split, 1 - self.core, axis=1, keepdims=False), 1)
        (other,) = yield [other]

        def piece(step):
            owner = self.owner(step)
            own = lax.dynamic_slice(split, (owner, self.core, 0, 0), (1, 1, half, width))
            pair = lax.dynamic_slice(other, (owner, 0, 0), (1, half, width))
            return own[0, 0].astype(FULL) + pair[0].astype(FULL)

        ahead = piece(self.far).astype(LOW)
        back = piece(-self.near).astype(LOW)
        for step in range(self.far - 1, -1, -1):
            moving = [self.hop(ahead, 1)]
            if step < self.near:
                moving.append(self.hop(back, -1))
            ahead, *rest = yield moving
            if step > 0:
                ahead = (ahead.astype(FULL) + piece(step)).astype(LOW)
            if rest:
                back = rest[0]
                if step > 0:
                    back = (back.astype(FULL) + piece(-step)).astype(LOW)
        total = (piece(0) + ahead.astype(FULL) + back.astype(FULL)).astype(LOW)
        (cross,) = yield [self.swap(total, 2)]
        total = (total.astype(FULL) + cross.astype(FULL)).astype(LOW)
        (pair,) = yield [self.swap(total, 1)]
        low = jnp.where(self.core == 0, total, pair)
        high = jnp.where(self.core == 0, pair, total)
        return jnp.concatenate([low, high], axis=0).astype(FULL)


class Flow:
    def __init__(self):
        self.running = {}
        self.results = {}

    def start(self, name, steps):
        self._move(name, steps, None)

    def _move(self, name, steps, values):
        try:
            self.running[name] = (steps, steps.send(values))
        except StopIteration as end:
            self.running.pop(name, None)
            self.results[name] = end.value

    def advance(self, *values):
        running = list(self.running.items())
        flat = list(values)
        for _, (_, flight) in running:
            flat += flight
        tied = tie(*flat) if flat else ()
        at = len(values)
        for name, (steps, flight) in running:
            self._move(name, steps, list(tied[at : at + len(flight)]))
            at += len(flight)
        return tied[0] if len(values) == 1 else tuple(tied[: len(values)])

    def take(self, name):
        while name in self.running:
            steps, flight = self.running[name]
            self._move(name, steps, flight)
        return self.results[name]


def shards(
    mesh,
    tokens,
    w_query,
    w_key,
    w_value,
    b_query,
    b_value,
    w_out,
    b_out,
    gain_one,
    shift_one,
    w_inner,
    b_inner,
    w_outer,
    b_outer,
    gain_two,
    shift_two,
    cotangent,
):
    links = Links(mesh)
    size = links.size
    width = D // size
    hidden = b_inner.shape[0]

    own_groups = [
        jnp.concatenate([w[:, g * WIDE : (g + 1) * WIDE] for w in (w_query, w_key, w_value)], axis=1)
        for g in range(GROUPS)
    ]
    vectors = (b_query, b_value, b_out, gain_one, shift_one, b_outer, gain_two, shift_two)
    used = len(vectors) * width + hidden
    room = -(-used // (32 * LANES)) * 32 * LANES
    flow = Flow()
    flow.start("group0", links.gather(own_groups[0]))
    *vectors, b_inner, own_groups[1], w_inner, w_outer = flow.advance(
        *vectors, b_inner, own_groups[1], w_inner, w_outer
    )
    whole_inner = links.gather_quarters(w_inner)
    whole_outer = links.gather_quarters(w_outer)
    packed = jnp.pad(jnp.concatenate(vectors + [b_inner]), (0, room - used))
    flow.start("small", links.gather_small(packed.reshape(room // LANES, LANES)))
    flow.advance()
    flow.start("group1", links.gather(own_groups[1]))
    flow.advance()
    flow.advance()
    whole_groups = [flow.take("group0")]
    whole_small = flow.take("small").reshape(size, room).astype(FULL)
    (bias_query, bias_value, bias_out, gain_first, shift_first, bias_outer, gain_second, shift_second) = (
        whole_small[:, i * width : (i + 1) * width].reshape(D) for i in range(len(vectors))
    )
    bias_inner = whole_small[:, used - hidden : used].reshape(size * hidden)

    no_bias = jnp.zeros((WIDE,), FULL)
    projected = []
    attended, lse = None, []
    for g in range(GROUPS):
        columns = slice(g * WIDE, (g + 1) * WIDE)
        bias = jnp.concatenate([bias_query[columns], no_bias, bias_value[columns]])
        projected.append((project(tokens, whole_groups[g]) + bias).astype(LOW))
        if g == 0:
            projected[g], w_out = flow.advance(projected[g], w_out)
            flow.start("out", links.gather(w_out))
        else:
            projected[g] = flow.advance(projected[g])
        attended, kept = attend(projected[g], g, attended)
        lse.append(kept)
        attended = flow.advance(attended)
        if g == 0:
            whole_groups.append(flow.take("group1"))
    whole_out = flow.take("out")
    branch = project(attended, whole_out) + bias_out
    unit_one, inverse_one = normal(tokens.astype(FULL) + branch)
    first = unit_one * gain_first + shift_first
    first_low = first.astype(LOW)
    pre = project(first_low, whole_inner) + bias_inner
    below = 0.5 * (1.0 + lax.erf(pre * (0.5**0.5)))
    active = (pre * below).astype(LOW)
    slope = (below + pre * jnp.exp(-0.5 * pre * pre) * 0.3989422804014327).astype(LOW)
    second = first + project(active, whole_outer) + bias_outer
    unit_two, inverse_two = normal(second)
    output = (unit_two * gain_second + shift_second).astype(LOW)

    cot = cotangent.astype(FULL)
    grad_gain_two = jnp.sum(cot * unit_two, axis=0)
    grad_shift_two = jnp.sum(cot, axis=0)
    d_second = normal_back(cot * gain_second, unit_two, inverse_two)
    d_mid = d_second.astype(LOW)
    grad_outer = gram(active, d_mid).astype(LOW)
    grad_outer, d_mid = tie(grad_outer, d_mid)
    part_outer = links.scatter_quarters(grad_outer)
    grad_b_outer = column_sum(d_mid)
    d_pre = (against(d_mid, whole_outer) * slope.astype(FULL)).astype(LOW)
    grad_inner = gram(first_low, d_pre).astype(LOW)
    grad_inner, d_pre = tie(grad_inner, d_pre)
    part_inner = links.scatter_quarters(grad_inner)
    grad_b_inner = column_sum(d_pre)
    d_first = d_second + against(d_pre, whole_inner)
    grad_gain_one = jnp.sum(d_first * unit_one, axis=0)
    grad_shift_one = jnp.sum(d_first, axis=0)
    d_inner = normal_back(d_first * gain_first, unit_one, inverse_one)
    d_branch = d_inner.astype(LOW)
    grad_out = gram(attended, d_branch).astype(LOW)
    grad_out, d_branch = flow.advance(grad_out, d_branch)
    flow.start("out_back", links.reduce(grad_out))
    grad_b_out = column_sum(d_branch)
    d_attended = against(d_branch, whole_out).astype(LOW)
    def joined(parts, place):
        columns = slice(place * WIDE, (place + 1) * WIDE)
        return jnp.concatenate([part[..., columns] for part in parts], axis=-1)

    grad_b_groups = []
    d_groups = []
    for g in range(GROUPS):
        d_group = attend_back(projected[g], d_attended, lse[g], g)
        if g == 0:
            d_group, part_outer = flow.advance(d_group, part_outer)
            own_outer = links.join_quarters(part_outer)
        else:
            d_group = flow.advance(d_group)
        grad_b_groups.append(column_sum(d_group))
        if g == GROUPS - 1:
            grads = (
                joined(grad_b_groups, 0),
                joined(grad_b_groups, 2),
                grad_b_out,
                grad_gain_one,
                grad_shift_one,
                grad_b_outer,
                grad_gain_two,
                grad_shift_two,
                grad_b_inner,
            )
            small = pack([grad.reshape(1, -1) for grad in grads], size, room // LANES)
            small, d_group = tie(small, d_group)
            flow.start("small_back", links.reduce(small))
        grad_group = gram(tokens, d_group).astype(LOW)
        grad_group, d_group, d_attended = flow.advance(grad_group, d_group, d_attended)
        flow.start(f"back{g}", links.reduce(grad_group))
        d_groups.append(d_group)
    d_groups[0] = flow.advance(d_groups[0])
    d_tokens = d_inner + against(d_groups[0], whole_groups[0])
    d_tokens = flow.advance(d_tokens)
    d_tokens = (d_tokens + against(d_groups[1], whole_groups[1])).astype(LOW)
    d_tokens, part_inner = flow.advance(d_tokens, part_inner)
    own_inner = links.join_quarters(part_inner)
    own_out = flow.take("out_back")
    own_small = flow.take("small_back").reshape(room)
    own_groups = [flow.take(f"back{g}") for g in range(GROUPS)]
    (
        own_bias_query,
        own_bias_value,
        own_bias_out,
        own_gain_one,
        own_shift_one,
        own_bias_outer,
        own_gain_two,
        own_shift_two,
    ) = (own_small[i * width : (i + 1) * width] for i in range(len(vectors)))
    own_bias_inner = own_small[used - hidden : used]
    return (
        output,
        d_tokens,
        joined(own_groups, 0),
        joined(own_groups, 1),
        joined(own_groups, 2),
        own_bias_query,
        own_bias_value,
        own_out,
        own_bias_out,
        own_gain_one,
        own_shift_one,
        own_inner,
        own_bias_inner,
        own_outer,
        own_bias_outer,
        own_gain_two,
        own_shift_two,
    )


def solution(mesh):
    rows = P(("rep", "shard"), None)
    matrix = P("shard", None)
    vector = P("shard")
    return jax.shard_map(
        functools.partial(shards, mesh),
        mesh=mesh,
        in_specs=(
            rows,
            matrix,
            matrix,
            matrix,
            vector,
            vector,
            matrix,
            vector,
            vector,
            vector,
            matrix,
            vector,
            matrix,
            vector,
            vector,
            vector,
            rows,
        ),
        out_specs=(
            rows,
            rows,
            matrix,
            matrix,
            matrix,
            vector,
            vector,
            matrix,
            vector,
            vector,
            vector,
            matrix,
            vector,
            matrix,
            vector,
            vector,
            vector,
        ),
        check_vma=False,
    )
```

```python
import functools

import jax
import jax.numpy as jnp
from jax import lax
from jax.experimental import pallas as pl
from jax.experimental.pallas import tpu as pltpu
from jax.sharding import PartitionSpec as P

D = 1024
H = 16
DH = 64
SEQ = 512
LANES = 128
GROUPS = 2
PAIRS = D // LANES // GROUPS
WIDE = D // GROUPS
AXES = ("rep", "shard")
RING_MOST = 16
LOW = jnp.bfloat16
FULL = jnp.float32


def project(left, right):
    return jnp.dot(left, right, preferred_element_type=FULL)


def gram(left, right):
    return lax.dot_general(left, right, (((0,), (0,)), ((), ())), preferred_element_type=FULL)


def against(left, right):
    return lax.dot_general(left, right, (((1,), (1,)), ((), ())), preferred_element_type=FULL)


def normal(values):
    centre = values - jnp.mean(values, axis=-1, keepdims=True)
    spread = jnp.mean(centre * centre, axis=-1, keepdims=True)
    inverse = lax.rsqrt(spread + 1e-12)
    return centre * inverse, inverse


def normal_back(scaled, unit, inverse):
    mean = jnp.mean(scaled, axis=-1, keepdims=True)
    along = jnp.mean(scaled * unit, axis=-1, keepdims=True)
    return (scaled - mean - unit * along) * inverse


def head_mask(head):
    lane = lax.broadcasted_iota(jnp.int32, (SEQ, LANES), 1)
    return (lane // DH) == head


def attend_kernel(query_ref, key_ref, value_ref, *rest):
    out_ref, lse_ref = rest[-2:]
    query = query_ref[...] * LOW(0.125)
    key = key_ref[...]
    value_t = value_ref[...].T
    parts = []
    for head in range(LANES // DH):
        own = jnp.where(head_mask(head), query, jnp.zeros_like(query))
        scores = against(key, own)
        top = jnp.max(scores, axis=0, keepdims=True)
        expo = jnp.exp(scores - top)
        total = jnp.sum(expo, axis=0, keepdims=True)
        mixed = project(value_t[head * DH : (head + 1) * DH], expo.astype(LOW))
        parts.append(mixed * (1.0 / total))
        lse_ref[0, head : head + 1, :] = top + jnp.log(total)
    out_ref[...] = jnp.concatenate(parts, axis=0).T.astype(LOW)


def attend_back_kernel(query_ref, key_ref, value_ref, d_ref, lse_ref, out_ref, sum_ref):
    seq, pair = pl.program_id(0), pl.program_id(1)
    query = query_ref[...] * LOW(0.125)
    key = key_ref[...]
    value = value_ref[...]
    d_out = d_ref[...]
    key_t = key.T
    d_key = None
    d_value = None
    d_query = []
    for head in range(LANES // DH):
        mask = head_mask(head)
        own = jnp.where(mask, query, jnp.zeros_like(query))
        d_own = jnp.where(mask, d_out, jnp.zeros_like(d_out))
        probs = jnp.exp(against(key, own) - lse_ref[0, head : head + 1, :])
        d_probs = against(value, d_own)
        inner = jnp.sum(probs * d_probs, axis=0, keepdims=True)
        d_scores = (probs * (d_probs - inner)).astype(LOW)
        part_value = project(probs.astype(LOW), d_own)
        part_key = project(d_scores, own)
        d_value = part_value if d_value is None else d_value + part_value
        d_key = part_key if d_key is None else d_key + part_key
        d_query.append(project(key_t[head * DH : (head + 1) * DH], d_scores))
    d_query = jnp.concatenate(d_query, axis=0).T * 0.125
    for place, grad in enumerate((d_query, d_key, d_value)):
        start = pl.multiple_of(place * WIDE + pair * LANES, LANES)
        out_ref[:, pl.ds(start, LANES)] = grad.astype(LOW)
        total = jnp.sum(grad, axis=0, keepdims=True)
        before = sum_ref[0:1, pl.ds(start, LANES)]
        sum_ref[0:1, pl.ds(start, LANES)] = jnp.where(seq == 0, total, before + total)


def column_block(first):
    return pl.BlockSpec((SEQ, LANES), lambda seq, pair: (seq, first + pair))


LSE_BLOCK = pl.BlockSpec((1, LANES // DH, SEQ), lambda seq, pair: (seq * PAIRS + pair, 0, 0))


def triple():
    return [column_block(place * PAIRS) for place in range(3)]


def attend(qkv, group, before):
    count = qkv.shape[0]
    seqs = count // SEQ
    kept = [] if before is None else [before]
    return pl.pallas_call(
        attend_kernel,
        grid=(seqs, PAIRS),
        in_specs=triple() + [pl.BlockSpec(memory_space=pl.ANY)] * len(kept),
        out_specs=[column_block(group * PAIRS), LSE_BLOCK],
        out_shape=[
            jax.ShapeDtypeStruct((count, D), LOW),
            jax.ShapeDtypeStruct((seqs * PAIRS, LANES // DH, SEQ), FULL),
        ],
        input_output_aliases={3: 0} if kept else {},
        compiler_params=pltpu.CompilerParams(vmem_limit_bytes=32 * 2**20),
        name="attend",
    )(qkv, qkv, qkv, *kept)


def attend_back(qkv, d_attended, lse, group):
    count = qkv.shape[0]
    return pl.pallas_call(
        attend_back_kernel,
        grid=(count // SEQ, PAIRS),
        in_specs=triple() + [column_block(group * PAIRS), LSE_BLOCK],
        out_specs=[
            pl.BlockSpec((SEQ, 3 * WIDE), lambda seq, pair: (seq, 0)),
            pl.BlockSpec((8, 3 * WIDE), lambda seq, pair: (0, 0)),
        ],
        out_shape=[
            jax.ShapeDtypeStruct((count, 3 * WIDE), LOW),
            jax.ShapeDtypeStruct((8, 3 * WIDE), FULL),
        ],
        compiler_params=pltpu.CompilerParams(vmem_limit_bytes=40 * 2**20),
        name="attend_back",
    )(qkv, qkv, qkv, d_attended, lse)


ROWS = 256
COLUMNS = 512
PARTS = 2
(QUERY, VALUE, OUT, GAIN_ONE, SHIFT_ONE, OUTER, GAIN_TWO, SHIFT_TWO) = range(8)


def line(ref, row):
    return ref[row : row + 1, :]


def kept(shape):
    return pl.BlockSpec(shape, lambda i: (0,) * len(shape), pipeline_mode=pl.Buffered(1))


def rows_of(width):
    return pl.BlockSpec((ROWS, width), lambda i: (i, 0))


def columns_of(height):
    return pl.BlockSpec((height, COLUMNS), lambda i: (0, i))


def add_line(ref, row, values):
    ref[row : row + 1, :] += jnp.sum(values, axis=0, keepdims=True)


def clear(ref):
    @pl.when(pl.program_id(0) == 0)
    def _():
        ref[...] = jnp.zeros_like(ref)


def pieces(rows):
    step = rows // PARTS
    return [slice(i * step, (i + 1) * step) for i in range(PARTS)]


LIMIT = pltpu.CompilerParams(vmem_limit_bytes=48 * 2**20)


def out_kernel(attended_ref, w_ref, tokens_ref, vec_ref, unit_ref, inverse_ref, low_ref):
    for rows in pieces(ROWS):
        branch = project(attended_ref[rows, :], w_ref[...]) + line(vec_ref, OUT)
        unit, inverse = normal(tokens_ref[rows, :].astype(FULL) + branch)
        unit_ref[rows, :] = unit
        inverse_ref[rows, :] = jnp.broadcast_to(inverse, (inverse.shape[0], LANES))
        low_ref[rows, :] = (unit * line(vec_ref, GAIN_ONE) + line(vec_ref, SHIFT_ONE)).astype(LOW)


def out_norm(attended, w_out, tokens, vec):
    count = tokens.shape[0]
    return pl.pallas_call(
        out_kernel,
        grid=(count // ROWS,),
        in_specs=[rows_of(D), kept((D, D)), rows_of(D), kept((8, D))],
        out_specs=[rows_of(D), rows_of(LANES), rows_of(D)],
        out_shape=[
            jax.ShapeDtypeStruct((count, D), FULL),
            jax.ShapeDtypeStruct((count, LANES), FULL),
            jax.ShapeDtypeStruct((count, D), LOW),
        ],
        compiler_params=LIMIT,
        name="out_norm",
    )(attended, w_out, tokens, vec)


def inner_kernel(low_ref, w_ref, bias_ref, active_ref, slope_ref):
    for rows in pieces(low_ref.shape[0]):
        pre = project(low_ref[rows, :], w_ref[...]) + bias_ref[...]
        below = 0.5 * (1.0 + lax.erf(pre * (0.5**0.5)))
        active_ref[rows, :] = (pre * below).astype(LOW)
        slope_ref[rows, :] = (below + pre * jnp.exp(-0.5 * pre * pre) * 0.3989422804014327).astype(LOW)


def inner_gelu(low, w_inner, bias):
    count, hidden = low.shape[0], w_inner.shape[1]
    return pl.pallas_call(
        inner_kernel,
        grid=(hidden // COLUMNS,),
        in_specs=[kept((count, D)), columns_of(D), columns_of(1)],
        out_specs=[columns_of(count), columns_of(count)],
        out_shape=[jax.ShapeDtypeStruct((count, hidden), LOW)] * 2,
        compiler_params=LIMIT,
        name="inner_gelu",
    )(low, w_inner, bias)


def outer_kernel(active_ref, w_ref, unit_ref, vec_ref, cot_ref, out_ref, d_ref, d_low_ref, sum_ref):
    clear(sum_ref)
    for rows in pieces(ROWS):
        first = unit_ref[rows, :] * line(vec_ref, GAIN_ONE) + line(vec_ref, SHIFT_ONE)
        second = first + project(active_ref[rows, :], w_ref[...]) + line(vec_ref, OUTER)
        unit, inverse = normal(second)
        out_ref[rows, :] = (unit * line(vec_ref, GAIN_TWO) + line(vec_ref, SHIFT_TWO)).astype(LOW)
        cot = cot_ref[rows, :].astype(FULL)
        d_second = normal_back(cot * line(vec_ref, GAIN_TWO), unit, inverse)
        d_ref[rows, :] = d_second
        d_low_ref[rows, :] = d_second.astype(LOW)
        add_line(sum_ref, 0, cot * unit)
        add_line(sum_ref, 1, cot)
        add_line(sum_ref, 2, d_second)


def outer_norms(active, w_outer, unit, vec, cotangent):
    count, hidden = active.shape
    return pl.pallas_call(
        outer_kernel,
        grid=(count // ROWS,),
        in_specs=[rows_of(hidden), kept((hidden, D)), rows_of(D), kept((8, D)), rows_of(D)],
        out_specs=[rows_of(D), rows_of(D), rows_of(D), kept((8, D))],
        out_shape=[
            jax.ShapeDtypeStruct((count, D), LOW),
            jax.ShapeDtypeStruct((count, D), FULL),
            jax.ShapeDtypeStruct((count, D), LOW),
            jax.ShapeDtypeStruct((8, D), FULL),
        ],
        compiler_params=LIMIT,
        name="outer_norms",
    )(active, w_outer, unit, vec, cotangent)


def outer_back_kernel(d_ref, w_ref, slope_ref, out_ref, sum_ref):
    sum_ref[...] = jnp.zeros_like(sum_ref)
    for rows in pieces(d_ref.shape[0]):
        d_pre = against(d_ref[rows, :], w_ref[...]) * slope_ref[rows, :].astype(FULL)
        out_ref[rows, :] = d_pre.astype(LOW)
        add_line(sum_ref, 0, d_pre)


def outer_back(d_mid, w_outer, slope):
    count, hidden = slope.shape
    return pl.pallas_call(
        outer_back_kernel,
        grid=(hidden // COLUMNS,),
        in_specs=[kept((count, D)), pl.BlockSpec((COLUMNS, D), lambda i: (i, 0)), columns_of(count)],
        out_specs=[columns_of(count), columns_of(1)],
        out_shape=[
            jax.ShapeDtypeStruct((count, hidden), LOW),
            jax.ShapeDtypeStruct((1, hidden), FULL),
        ],
        compiler_params=LIMIT,
        name="outer_back",
    )(d_mid, w_outer, slope)


def inner_back_kernel(
    d_pre_ref, w_ref, d_ref, unit_ref, inverse_ref, vec_ref, w_out_ref, out_ref, low_ref, attended_ref, sum_ref
):
    clear(sum_ref)
    for rows in pieces(ROWS):
        d_first = d_ref[rows, :] + against(d_pre_ref[rows, :], w_ref[...])
        unit = unit_ref[rows, :]
        d_inner = normal_back(d_first * line(vec_ref, GAIN_ONE), unit, inverse_ref[rows, 0:1])
        low = d_inner.astype(LOW)
        out_ref[rows, :] = d_inner
        low_ref[rows, :] = low
        attended_ref[rows, :] = against(low, w_out_ref[...]).astype(LOW)
        add_line(sum_ref, 0, d_first * unit)
        add_line(sum_ref, 1, d_first)
        add_line(sum_ref, 2, d_inner)


def inner_back(d_pre, w_inner, d_second, unit, inverse, vec, w_out):
    count, hidden = d_pre.shape
    return pl.pallas_call(
        inner_back_kernel,
        grid=(count // ROWS,),
        in_specs=[
            rows_of(hidden),
            kept((D, hidden)),
            rows_of(D),
            rows_of(D),
            rows_of(LANES),
            kept((8, D)),
            kept((D, D)),
        ],
        out_specs=[rows_of(D), rows_of(D), rows_of(D), kept((8, D))],
        out_shape=[
            jax.ShapeDtypeStruct((count, D), FULL),
            jax.ShapeDtypeStruct((count, D), LOW),
            jax.ShapeDtypeStruct((count, D), LOW),
            jax.ShapeDtypeStruct((8, D), FULL),
        ],
        compiler_params=LIMIT,
        name="inner_back",
    )(d_pre, w_inner, d_second, unit, inverse, vec, w_out)


def tokens_kernel(base_ref, d_ref, w_ref, out_ref):
    out_ref[...] = (base_ref[...] + against(d_ref[...], w_ref[...])).astype(out_ref.dtype)


def tokens_back(base, d_group, w_group, kind):
    count, wide = d_group.shape
    return pl.pallas_call(
        tokens_kernel,
        grid=(count // ROWS,),
        in_specs=[rows_of(D), rows_of(wide), kept((D, wide))],
        out_specs=rows_of(D),
        out_shape=jax.ShapeDtypeStruct((count, D), kind),
        compiler_params=LIMIT,
        name="tokens_back",
    )(base, d_group, w_group)


def turn_kernel(ref, out_ref):
    out_ref[...] = ref[...].T


def turn(values):
    count, width = values.shape
    return pl.pallas_call(
        turn_kernel,
        grid=(count // ROWS,),
        in_specs=[rows_of(width)],
        out_specs=pl.BlockSpec((width, ROWS), lambda i: (0, i)),
        out_shape=jax.ShapeDtypeStruct((width, count), values.dtype),
        name="turn",
    )(values)


def product_kernel(left_ref, right_ref, out_ref):
    out_ref[...] = project(left_ref[...], right_ref[...]).astype(LOW)


def product(left, right):
    height, depth = left.shape
    return pl.pallas_call(
        product_kernel,
        grid=(right.shape[1] // COLUMNS,),
        in_specs=[kept((height, depth)), columns_of(depth)],
        out_specs=columns_of(height),
        out_shape=jax.ShapeDtypeStruct((height, right.shape[1]), LOW),
        compiler_params=LIMIT,
        name="product",
    )(left, right)


def assemble_kernel(moves, align, place_ref, *refs):
    out_ref, sems = refs[-2], refs[-1]
    copies = []
    for i, (which, start, rows) in enumerate(moves):
        place = pl.multiple_of(place_ref[i], align)
        source = refs[which].at[pl.ds(start, rows)]
        copies.append(pltpu.make_async_copy(source, out_ref.at[pl.ds(place, rows)], sems.at[i]))
    for copy in copies:
        copy.start()
    for copy in copies:
        copy.wait()


def assemble(arrays, moves, places, rows):
    align = min(move[2] for move in moves)
    return pl.pallas_call(
        functools.partial(assemble_kernel, moves, align),
        in_specs=[pl.BlockSpec(memory_space=pltpu.SMEM)] + [pl.BlockSpec(memory_space=pl.ANY)] * len(arrays),
        out_specs=pl.BlockSpec(memory_space=pltpu.VMEM),
        out_shape=jax.ShapeDtypeStruct((rows,) + arrays[0].shape[1:], arrays[0].dtype),
        scratch_shapes=[pltpu.SemaphoreType.DMA((len(moves),))],
        compiler_params=pltpu.CompilerParams(vmem_limit_bytes=24 * 2**20),
        name="assemble",
    )(jnp.stack(places).astype(jnp.int32), *arrays)


def pack_kernel(size, rows, vectors, *refs):
    out_ref = refs[-1]
    out_ref[...] = jnp.zeros_like(out_ref)
    for shard in range(size):
        at = shard * rows
        for spans in vectors:
            lines = []
            for which, row, first, length in spans:
                lines += [(which, row, first + i) for i in range(0, length, LANES)]
            share = len(lines) // size
            for which, row, first in lines[shard * share : (shard + 1) * share]:
                out_ref[at : at + 1, :] = refs[which][row : row + 1, first : first + LANES]
                at += 1


def pack(arrays, vectors, size, rows):
    if any(sum(span[3] for span in spans) % (size * LANES) for spans in vectors):
        whole = [
            jnp.concatenate([arrays[which][row, first : first + length] for which, row, first, length in spans])
            for spans in vectors
        ]
        small = jnp.concatenate([vector.reshape(size, -1) for vector in whole], axis=1)
        small = jnp.pad(small, ((0, 0), (0, rows * LANES - small.shape[1])))
        return small.reshape(size * rows, LANES).astype(LOW)
    return pl.pallas_call(
        functools.partial(pack_kernel, size, rows, vectors),
        out_shape=jax.ShapeDtypeStruct((size * rows, LANES), FULL),
        name="pack",
    )(*arrays).astype(LOW)


def unpack_kernel(count, place_ref, *refs):
    vec_ref, bias_ref, group_ref = refs[count:]
    group_ref[...] = jnp.zeros_like(group_ref)
    hidden = bias_ref.shape[1] // count
    for i in range(count):
        chunk = refs[i][...].astype(FULL)
        owner = place_ref[i]
        start = pl.multiple_of(owner * LANES, LANES)
        for row in range(8):
            vec_ref[row : row + 1, pl.ds(start, LANES)] = chunk[row : row + 1, :]
        for row in range(hidden // LANES):
            first = pl.multiple_of(owner * hidden + row * LANES, LANES)
            bias_ref[:, pl.ds(first, LANES)] = chunk[8 + row : 9 + row, :]
        group = owner * LANES // WIDE
        for place, row in ((0, QUERY), (2, VALUE)):
            first = pl.multiple_of(group * 2 * WIDE + place * WIDE + start, LANES)
            group_ref[:, pl.ds(first, LANES)] = chunk[row : row + 1, :]


def unpack(chunks, owners, hidden):
    count = len(chunks)
    return pl.pallas_call(
        functools.partial(unpack_kernel, count),
        in_specs=[pl.BlockSpec(memory_space=pltpu.SMEM)] + [pl.BlockSpec(memory_space=pltpu.VMEM)] * count,
        out_shape=[
            jax.ShapeDtypeStruct((8, D), FULL),
            jax.ShapeDtypeStruct((1, hidden), FULL),
            jax.ShapeDtypeStruct((1, 3 * D), FULL),
        ],
        name="unpack",
    )(jnp.stack(owners).astype(jnp.int32), *chunks)


def tie(*values):
    return lax.optimization_barrier(values)


class Links:
    def __init__(self, mesh):
        self.reps, self.size = mesh.shape["rep"], mesh.shape["shard"]
        size = self.size
        self.direct = size > RING_MOST or size % 2 == 1
        self.order = list(range(0, size, 2)) + list(range(size - 1, 0, -2))
        self.far = size // 2
        self.near = size - 1 - self.far
        rep = lax.axis_index("rep")
        shard = lax.axis_index("shard")
        self.core = rep % 2
        self.sign = 1 - 2 * self.core
        self.place = jnp.where(shard % 2 == 0, shard // 2, size - 1 - shard // 2)

    def owner(self, step):
        place = (self.place + self.sign * step + 2 * self.size) % self.size
        return jnp.where(place < self.size // 2, 2 * place, 2 * (self.size - place) - 1)

    def hop(self, values, sign):
        pairs = []
        for rep in range(self.reps):
            turn = sign if rep % 2 == 0 else -sign
            for i, shard in enumerate(self.order):
                target = self.order[(i + turn) % self.size]
                pairs.append((rep * self.size + shard, rep * self.size + target))
        return lax.ppermute(values, AXES, pairs)

    def swap(self, values, bit):
        pairs = []
        for rep in range(self.reps):
            for shard in range(self.size):
                pairs.append((rep * self.size + shard, (rep ^ bit) * self.size + shard))
        return lax.ppermute(values, AXES, pairs)

    def half_of(self, values):
        half = values.shape[0] // 2
        return lax.dynamic_slice_in_dim(values, self.core * half, half, axis=0)


    def gather_small(self, values, hidden):
        if self.direct:
            small = lax.all_gather(values, "shard", axis=0, tiled=True).reshape(self.size, -1).astype(FULL)
            width, share = D // self.size, hidden // self.size
            vec = small[:, : 8 * width].reshape(self.size, 8, width).swapaxes(0, 1).reshape(8, D)
            bias = small[:, 8 * width : 8 * width + share].reshape(1, hidden)
            none = jnp.zeros((WIDE,), FULL)
            spans = [slice(g * WIDE, (g + 1) * WIDE) for g in range(GROUPS)]
            parts = [part for span in spans for part in (vec[QUERY, span], none, vec[VALUE, span])]
            return vec, bias, jnp.concatenate(parts).reshape(1, 3 * D)
        found = [(values, 0)]
        ahead = back = values
        for step in range(1, self.far + 1):
            ahead = self.hop(ahead, 1)
            found.append((ahead, -step))
            if step <= self.near:
                back = self.hop(back, -1)
                found.append((back, step))
            ahead, back = yield [ahead, back]
        owners = [self.owner(step) for _, step in found]
        return unpack([chunk for chunk, _ in found], owners, hidden)

    def gather(self, values):
        if self.direct:
            return lax.all_gather(values, "shard", axis=0, tiled=True)
        rows = values.shape[0]
        half = rows // 2
        arrays = [values]
        moves = [(0, 0, rows)]
        places = [self.owner(0) * rows]

        def keep(chunk, mine, step):
            moves.append((len(arrays), 0, half))
            arrays.append(chunk)
            core = self.core if mine else 1 - self.core
            places.append(self.owner(step) * rows + core * half)

        ahead = back = self.half_of(values)
        for step in range(1, self.far + 2):
            flight = []
            if step > 1:
                keep(ahead, True, 1 - step)
                flight.append((self.swap(ahead, 1), step - 1))
                if step - 1 <= self.near:
                    keep(back, True, step - 1)
                    flight.append((self.swap(back, 1), 1 - step))
            if step <= self.far:
                ahead = self.hop(ahead, 1)
            if step <= self.near:
                back = self.hop(back, -1)
            ahead, back, *swapped = yield [ahead, back] + [chunk for chunk, _ in flight]
            for chunk, (_, place) in zip(swapped, flight):
                keep(chunk, False, place)
        return assemble(arrays, moves, places, self.size * rows)

    def gather_quarters(self, values):
        rows = values.shape[0] // self.reps
        mine = lax.dynamic_slice_in_dim(values, lax.axis_index("rep") * rows, rows, axis=0)
        return lax.all_gather(mine, ("shard", "rep"), axis=0, tiled=True)

    def reduce_halves(self, values, rounds):
        if self.direct:
            own = lax.psum_scatter(values, "shard", scatter_dimension=0, tiled=True)
            return lax.psum(own, "rep").astype(FULL)
        width = values.shape[1]
        half = values.shape[0] // self.size // 2
        split = values.reshape(self.size, 2, half, width)
        other = self.swap(lax.dynamic_index_in_dim(split, 1 - self.core, axis=1, keepdims=False), 1)
        (other,) = yield [other]
        mine = lax.dynamic_index_in_dim(split, self.core, axis=1, keepdims=False)
        total = (mine.astype(FULL) + other.astype(FULL)).astype(LOW).reshape(self.size * half, width)
        total = lax.psum_scatter(total, "shard", scatter_dimension=0, tiled=True)
        for _ in range(rounds):
            yield []
        (total,) = yield [total]
        return (yield from self.finish(total))

    def finish(self, total):
        (cross,) = yield [self.swap(total, 2)]
        total = (total.astype(FULL) + cross.astype(FULL)).astype(LOW)
        (pair,) = yield [self.swap(total, 1)]
        low = jnp.where(self.core == 0, total, pair)
        high = jnp.where(self.core == 0, pair, total)
        return jnp.concatenate([low, high], axis=0).astype(FULL)

    def reduce(self, values):
        if self.direct:
            own = lax.psum_scatter(values, "shard", scatter_dimension=0, tiled=True)
            return lax.psum(own, "rep").astype(FULL)
        width = values.shape[1]
        half = values.shape[0] // self.size // 2
        split = values.reshape(self.size, 2, half, width)
        other = self.swap(lax.dynamic_index_in_dim(split, 1 - self.core, axis=1, keepdims=False), 1)
        (other,) = yield [other]

        def piece(step):
            owner = self.owner(step)
            own = lax.dynamic_slice(split, (owner, self.core, 0, 0), (1, 1, half, width))
            pair = lax.dynamic_slice(other, (owner, 0, 0), (1, half, width))
            return own[0, 0].astype(FULL) + pair[0].astype(FULL)

        ahead = piece(self.far).astype(LOW)
        back = piece(-self.near).astype(LOW)
        for step in range(self.far - 1, -1, -1):
            moving = [self.hop(ahead, 1)]
            if step < self.near:
                moving.append(self.hop(back, -1))
            ahead, *rest = yield moving
            if step > 0:
                ahead = (ahead.astype(FULL) + piece(step)).astype(LOW)
            if rest:
                back = rest[0]
                if step > 0:
                    back = (back.astype(FULL) + piece(-step)).astype(LOW)
        total = (piece(0) + ahead.astype(FULL) + back.astype(FULL)).astype(LOW)
        return (yield from self.finish(total))


class Flow:
    def __init__(self):
        self.running = {}
        self.results = {}

    def start(self, name, steps):
        self._move(name, steps, None)

    def _move(self, name, steps, values):
        try:
            self.running[name] = (steps, steps.send(values))
        except StopIteration as end:
            self.running.pop(name, None)
            self.results[name] = end.value

    def advance(self, *values):
        running = list(self.running.items())
        flat = list(values)
        for _, (_, flight) in running:
            flat += flight
        tied = tie(*flat) if flat else ()
        at = len(values)
        for name, (steps, flight) in running:
            self._move(name, steps, list(tied[at : at + len(flight)]))
            at += len(flight)
        return tied[0] if len(values) == 1 else tuple(tied[: len(values)])

    def take(self, name):
        while name in self.running:
            steps, flight = self.running[name]
            self._move(name, steps, flight)
        return self.results[name]


def shards(
    mesh,
    tokens,
    w_query,
    w_key,
    w_value,
    b_query,
    b_value,
    w_out,
    b_out,
    gain_one,
    shift_one,
    w_inner,
    b_inner,
    w_outer,
    b_outer,
    gain_two,
    shift_two,
    cotangent,
):
    links = Links(mesh)
    size = links.size
    width = D // size
    hidden = b_inner.shape[0]

    own_groups = [
        jnp.concatenate([w[:, g * WIDE : (g + 1) * WIDE] for w in (w_query, w_key, w_value)], axis=1)
        for g in range(GROUPS)
    ]
    vectors = (b_query, b_value, b_out, gain_one, shift_one, b_outer, gain_two, shift_two)
    used = len(vectors) * width + hidden
    room = -(-used // (32 * LANES)) * 32 * LANES
    flow = Flow()
    flow.start("group0", links.gather(own_groups[0]))
    *vectors, b_inner, own_groups[1], w_inner, w_outer = flow.advance(
        *vectors, b_inner, own_groups[1], w_inner, w_outer
    )
    whole_inner = links.gather_quarters(w_inner)
    whole_outer = links.gather_quarters(w_outer)
    packed = jnp.pad(jnp.concatenate(vectors + [b_inner]), (0, room - used))
    flow.start("small", links.gather_small(packed.reshape(room // LANES, LANES), size * hidden))
    flow.advance()
    tokens_turned, own_groups[1] = tie(turn(tokens), own_groups[1])
    flow.start("group1", links.gather(own_groups[1]))
    flow.advance()
    flow.advance()
    whole_groups = [flow.take("group0")]
    vec, bias_inner, bias_groups = flow.take("small")

    projected = []
    attended, lse = None, []
    for g in range(GROUPS):
        bias = bias_groups[:, g * 3 * WIDE : (g + 1) * 3 * WIDE]
        projected.append((project(tokens, whole_groups[g]) + bias).astype(LOW))
        if g == 0:
            projected[g], w_out = flow.advance(projected[g], w_out)
            flow.start("out", links.gather(w_out))
        else:
            projected[g] = flow.advance(projected[g])
        attended, logs = attend(projected[g], g, attended)
        lse.append(logs)
        attended = flow.advance(attended)
        if g == 0:
            whole_groups.append(flow.take("group1"))
    whole_out = flow.take("out")
    unit_one, inverse_one, first_low = out_norm(attended, whole_out, tokens, vec)
    active, slope = inner_gelu(first_low, whole_inner, bias_inner)
    output, d_second, d_mid, sums_two = outer_norms(active, whole_outer, unit_one, vec, cotangent)

    grad_outer, d_mid = tie(gram(active, d_mid).astype(LOW), d_mid)
    flow.start("outer_back", links.reduce_halves(grad_outer, 5))
    d_pre, sum_inner = outer_back(d_mid, whole_outer, slope)
    d_pre = flow.advance(d_pre)
    grad_inner, d_pre = flow.advance(gram(first_low, d_pre).astype(LOW), d_pre)
    flow.start("inner_back", links.reduce(grad_inner))
    d_inner, d_branch, d_attended, sums_one = inner_back(
        d_pre, whole_inner, d_second, unit_one, inverse_one, vec, whole_out
    )
    d_branch, d_attended = flow.advance(d_branch, d_attended)
    grad_out, d_attended = tie(gram(attended, d_branch).astype(LOW), d_attended)
    flow.start("out_back", links.reduce(grad_out))

    d_groups, sums_group = [], []
    for g in range(GROUPS):
        d_group, sums = attend_back(projected[g], d_attended, lse[g], g)
        d_group, sums = flow.advance(d_group, sums)
        sums_group.append(sums)
        if g == GROUPS - 1:
            arrays = [sums_one, sums_two, sum_inner] + sums_group
            spans = [[(3 + h, 0, place * WIDE, WIDE) for h in range(GROUPS)] for place in (0, 2)]
            spans += [[(i, row, 0, D)] for i, row in ((0, 2), (0, 0), (0, 1), (1, 2), (1, 0), (1, 1))]
            spans += [[(2, 0, 0, size * hidden)]]
            small, d_group = tie(pack(arrays, spans, size, room // LANES), d_group)
            flow.start("small_back", links.reduce(small))
        grad_group, d_group, d_attended = flow.advance(product(tokens_turned, d_group), d_group, d_attended)
        flow.start(f"back{g}", links.reduce(grad_group))
        d_groups.append(d_group)
    d_groups[0] = flow.advance(d_groups[0])
    d_tokens = flow.advance(tokens_back(d_inner, d_groups[0], whole_groups[0], FULL))
    d_tokens = flow.advance(tokens_back(d_tokens, d_groups[1], whole_groups[1], LOW))
    own_inner = flow.take("inner_back")
    own_outer = flow.take("outer_back")
    own_out = flow.take("out_back")
    own_small = flow.take("small_back").reshape(room)
    own_groups = [flow.take(f"back{g}") for g in range(GROUPS)]

    def joined(parts, place):
        columns = slice(place * WIDE, (place + 1) * WIDE)
        return jnp.concatenate([part[..., columns] for part in parts], axis=-1)

    (
        own_bias_query,
        own_bias_value,
        own_bias_out,
        own_gain_one,
        own_shift_one,
        own_bias_outer,
        own_gain_two,
        own_shift_two,
    ) = (own_small[i * width : (i + 1) * width] for i in range(len(vectors)))
    own_bias_inner = own_small[used - hidden : used]
    return (
        output,
        d_tokens,
        joined(own_groups, 0),
        joined(own_groups, 1),
        joined(own_groups, 2),
        own_bias_query,
        own_bias_value,
        own_out,
        own_bias_out,
        own_gain_one,
        own_shift_one,
        own_inner,
        own_bias_inner,
        own_outer,
        own_bias_outer,
        own_gain_two,
        own_shift_two,
    )


def solution(mesh):
    rows = P(("rep", "shard"), None)
    matrix = P("shard", None)
    vector = P("shard")
    return jax.shard_map(
        functools.partial(shards, mesh),
        mesh=mesh,
        in_specs=(
            rows,
            matrix,
            matrix,
            matrix,
            vector,
            vector,
            matrix,
            vector,
            vector,
            vector,
            matrix,
            vector,
            matrix,
            vector,
            vector,
            vector,
            rows,
        ),
        out_specs=(
            rows,
            rows,
            matrix,
            matrix,
            matrix,
            vector,
            vector,
            matrix,
            vector,
            vector,
            vector,
            matrix,
            vector,
            matrix,
            vector,
            vector,
            vector,
        ),
        check_vma=False,
    )
```

```python
import functools

import jax
import jax.numpy as jnp
from jax import lax
from jax.experimental import pallas as pl
from jax.experimental.pallas import tpu as pltpu
from jax.sharding import PartitionSpec as P

D = 1024
H = 16
DH = 64
SEQ = 512
LANES = 128
GROUPS = 2
PAIRS = D // LANES // GROUPS
WIDE = D // GROUPS
AXES = ("cross", "core", "shard")
RING_MOST = 16
LOW = jnp.bfloat16
FULL = jnp.float32


def project(left, right):
    return jnp.dot(left, right, preferred_element_type=FULL)


def gram(left, right):
    return lax.dot_general(left, right, (((0,), (0,)), ((), ())), preferred_element_type=FULL)


def against(left, right):
    return lax.dot_general(left, right, (((1,), (1,)), ((), ())), preferred_element_type=FULL)


def normal(values):
    centre = values - jnp.mean(values, axis=-1, keepdims=True)
    spread = jnp.mean(centre * centre, axis=-1, keepdims=True)
    inverse = lax.rsqrt(spread + 1e-12)
    return centre * inverse, inverse


def normal_back(scaled, unit, inverse):
    mean = jnp.mean(scaled, axis=-1, keepdims=True)
    along = jnp.mean(scaled * unit, axis=-1, keepdims=True)
    return (scaled - mean - unit * along) * inverse


def head_mask(head):
    lane = lax.broadcasted_iota(jnp.int32, (SEQ, LANES), 1)
    return (lane // DH) == head


def attend_kernel(query_ref, key_ref, value_ref, *rest):
    out_ref, lse_ref = rest[-2:]
    query = query_ref[...] * LOW(0.125)
    key = key_ref[...]
    value_t = value_ref[...].T
    parts = []
    for head in range(LANES // DH):
        own = jnp.where(head_mask(head), query, jnp.zeros_like(query))
        scores = against(key, own)
        top = jnp.max(scores, axis=0, keepdims=True)
        expo = jnp.exp(scores - top)
        total = jnp.sum(expo, axis=0, keepdims=True)
        mixed = project(value_t[head * DH : (head + 1) * DH], expo.astype(LOW))
        parts.append(mixed * (1.0 / total))
        lse_ref[0, head : head + 1, :] = top + jnp.log(total)
    out_ref[...] = jnp.concatenate(parts, axis=0).T.astype(LOW)


def attend_back_kernel(query_ref, key_ref, value_ref, d_ref, lse_ref, out_ref, sum_ref):
    seq, pair = pl.program_id(0), pl.program_id(1)
    query = query_ref[...] * LOW(0.125)
    key = key_ref[...]
    value = value_ref[...]
    d_out = d_ref[...]
    key_t = key.T
    d_key = None
    d_value = None
    d_query = []
    for head in range(LANES // DH):
        mask = head_mask(head)
        own = jnp.where(mask, query, jnp.zeros_like(query))
        d_own = jnp.where(mask, d_out, jnp.zeros_like(d_out))
        probs = jnp.exp(against(key, own) - lse_ref[0, head : head + 1, :])
        d_probs = against(value, d_own)
        inner = jnp.sum(probs * d_probs, axis=0, keepdims=True)
        d_scores = (probs * (d_probs - inner)).astype(LOW)
        part_value = project(probs.astype(LOW), d_own)
        part_key = project(d_scores, own)
        d_value = part_value if d_value is None else d_value + part_value
        d_key = part_key if d_key is None else d_key + part_key
        d_query.append(project(key_t[head * DH : (head + 1) * DH], d_scores))
    d_query = jnp.concatenate(d_query, axis=0).T * 0.125
    for place, grad in enumerate((d_query, d_key, d_value)):
        start = pl.multiple_of(place * WIDE + pair * LANES, LANES)
        out_ref[:, pl.ds(start, LANES)] = grad.astype(LOW)
        total = jnp.sum(grad, axis=0, keepdims=True)
        before = sum_ref[0:1, pl.ds(start, LANES)]
        sum_ref[0:1, pl.ds(start, LANES)] = jnp.where(seq == 0, total, before + total)


def column_block(first):
    return pl.BlockSpec((SEQ, LANES), lambda seq, pair: (seq, first + pair))


LSE_BLOCK = pl.BlockSpec((1, LANES // DH, SEQ), lambda seq, pair: (seq * PAIRS + pair, 0, 0))


def triple():
    return [column_block(place * PAIRS) for place in range(3)]


def attend(qkv, group, before):
    count = qkv.shape[0]
    seqs = count // SEQ
    kept = [] if before is None else [before]
    return pl.pallas_call(
        attend_kernel,
        grid=(seqs, PAIRS),
        in_specs=triple() + [pl.BlockSpec(memory_space=pl.ANY)] * len(kept),
        out_specs=[column_block(group * PAIRS), LSE_BLOCK],
        out_shape=[
            jax.ShapeDtypeStruct((count, D), LOW),
            jax.ShapeDtypeStruct((seqs * PAIRS, LANES // DH, SEQ), FULL),
        ],
        input_output_aliases={3: 0} if kept else {},
        compiler_params=pltpu.CompilerParams(vmem_limit_bytes=32 * 2**20),
        name="attend",
    )(qkv, qkv, qkv, *kept)


def attend_back(qkv, d_attended, lse, group):
    count = qkv.shape[0]
    return pl.pallas_call(
        attend_back_kernel,
        grid=(count // SEQ, PAIRS),
        in_specs=triple() + [column_block(group * PAIRS), LSE_BLOCK],
        out_specs=[
            pl.BlockSpec((SEQ, 3 * WIDE), lambda seq, pair: (seq, 0)),
            pl.BlockSpec((8, 3 * WIDE), lambda seq, pair: (0, 0)),
        ],
        out_shape=[
            jax.ShapeDtypeStruct((count, 3 * WIDE), LOW),
            jax.ShapeDtypeStruct((8, 3 * WIDE), FULL),
        ],
        compiler_params=pltpu.CompilerParams(vmem_limit_bytes=40 * 2**20),
        name="attend_back",
    )(qkv, qkv, qkv, d_attended, lse)


ROWS = 256
COLUMNS = 512
PARTS = 2
(QUERY, VALUE, OUT, GAIN_ONE, SHIFT_ONE, OUTER, GAIN_TWO, SHIFT_TWO) = range(8)


def line(ref, row):
    return ref[row : row + 1, :]


def kept(shape):
    return pl.BlockSpec(shape, lambda i: (0,) * len(shape), pipeline_mode=pl.Buffered(1))


def rows_of(width):
    return pl.BlockSpec((ROWS, width), lambda i: (i, 0))


def columns_of(height):
    return pl.BlockSpec((height, COLUMNS), lambda i: (0, i))


def add_line(ref, row, values):
    ref[row : row + 1, :] += jnp.sum(values, axis=0, keepdims=True)


def clear(ref):
    @pl.when(pl.program_id(0) == 0)
    def _():
        ref[...] = jnp.zeros_like(ref)


def pieces(rows, count=PARTS):
    step = rows // count
    return [slice(i * step, (i + 1) * step) for i in range(count)]


LIMIT = pltpu.CompilerParams(vmem_limit_bytes=48 * 2**20)


def out_kernel(attended_ref, w_ref, tokens_ref, vec_ref, unit_ref, inverse_ref, low_ref):
    for rows in pieces(ROWS):
        branch = project(attended_ref[rows, :], w_ref[...]) + line(vec_ref, OUT)
        unit, inverse = normal(tokens_ref[rows, :].astype(FULL) + branch)
        unit_ref[rows, :] = unit
        inverse_ref[rows, :] = jnp.broadcast_to(inverse, (inverse.shape[0], LANES))
        low_ref[rows, :] = (unit * line(vec_ref, GAIN_ONE) + line(vec_ref, SHIFT_ONE)).astype(LOW)


def out_norm(attended, w_out, tokens, vec):
    count = tokens.shape[0]
    return pl.pallas_call(
        out_kernel,
        grid=(count // ROWS,),
        in_specs=[rows_of(D), kept((D, D)), rows_of(D), kept((8, D))],
        out_specs=[rows_of(D), rows_of(LANES), rows_of(D)],
        out_shape=[
            jax.ShapeDtypeStruct((count, D), FULL),
            jax.ShapeDtypeStruct((count, LANES), FULL),
            jax.ShapeDtypeStruct((count, D), LOW),
        ],
        compiler_params=LIMIT,
        name="out_norm",
    )(attended, w_out, tokens, vec)


def inner_kernel(low_ref, w_ref, bias_ref, active_ref, slope_ref):
    for rows in pieces(low_ref.shape[0], 4):
        pre = project(low_ref[rows, :], w_ref[...]) + bias_ref[...]
        below = 0.5 * (1.0 + lax.erf(pre * (0.5**0.5)))
        active_ref[rows, :] = (pre * below).astype(LOW)
        slope_ref[rows, :] = (below + pre * jnp.exp(-0.5 * pre * pre) * 0.3989422804014327).astype(LOW)


def inner_gelu(low, w_inner, bias):
    count, hidden = low.shape[0], w_inner.shape[1]
    return pl.pallas_call(
        inner_kernel,
        grid=(hidden // COLUMNS,),
        in_specs=[kept((count, D)), columns_of(D), columns_of(1)],
        out_specs=[columns_of(count), columns_of(count)],
        out_shape=[jax.ShapeDtypeStruct((count, hidden), LOW)] * 2,
        compiler_params=LIMIT,
        name="inner_gelu",
    )(low, w_inner, bias)


def outer_kernel(active_ref, w_ref, unit_ref, vec_ref, cot_ref, out_ref, d_ref, d_low_ref, sum_ref):
    clear(sum_ref)
    for rows in pieces(ROWS):
        first = unit_ref[rows, :] * line(vec_ref, GAIN_ONE) + line(vec_ref, SHIFT_ONE)
        second = first + project(active_ref[rows, :], w_ref[...]) + line(vec_ref, OUTER)
        unit, inverse = normal(second)
        out_ref[rows, :] = (unit * line(vec_ref, GAIN_TWO) + line(vec_ref, SHIFT_TWO)).astype(LOW)
        cot = cot_ref[rows, :].astype(FULL)
        d_second = normal_back(cot * line(vec_ref, GAIN_TWO), unit, inverse)
        d_ref[rows, :] = d_second
        d_low_ref[rows, :] = d_second.astype(LOW)
        add_line(sum_ref, 0, cot * unit)
        add_line(sum_ref, 1, cot)
        add_line(sum_ref, 2, d_second)


def outer_norms(active, w_outer, unit, vec, cotangent):
    count, hidden = active.shape
    return pl.pallas_call(
        outer_kernel,
        grid=(count // ROWS,),
        in_specs=[rows_of(hidden), kept((hidden, D)), rows_of(D), kept((8, D)), rows_of(D)],
        out_specs=[rows_of(D), rows_of(D), rows_of(D), kept((8, D))],
        out_shape=[
            jax.ShapeDtypeStruct((count, D), LOW),
            jax.ShapeDtypeStruct((count, D), FULL),
            jax.ShapeDtypeStruct((count, D), LOW),
            jax.ShapeDtypeStruct((8, D), FULL),
        ],
        compiler_params=LIMIT,
        name="outer_norms",
    )(active, w_outer, unit, vec, cotangent)


def outer_back_kernel(d_ref, w_ref, slope_ref, out_ref, sum_ref):
    sum_ref[...] = jnp.zeros_like(sum_ref)
    turned = w_ref[...].T
    for rows in pieces(d_ref.shape[0], 4):
        d_pre = project(d_ref[rows, :], turned) * slope_ref[rows, :].astype(FULL)
        out_ref[rows, :] = d_pre.astype(LOW)
        add_line(sum_ref, 0, d_pre)


def outer_back(d_mid, w_outer, slope):
    count, hidden = slope.shape
    return pl.pallas_call(
        outer_back_kernel,
        grid=(hidden // COLUMNS,),
        in_specs=[kept((count, D)), pl.BlockSpec((COLUMNS, D), lambda i: (i, 0)), columns_of(count)],
        out_specs=[columns_of(count), columns_of(1)],
        out_shape=[
            jax.ShapeDtypeStruct((count, hidden), LOW),
            jax.ShapeDtypeStruct((1, hidden), FULL),
        ],
        compiler_params=LIMIT,
        name="outer_back",
    )(d_mid, w_outer, slope)


def inner_back_kernel(
    d_pre_ref, w_ref, d_ref, unit_ref, inverse_ref, vec_ref, w_out_ref, out_ref, low_ref, attended_ref, sum_ref, total_ref
):
    step = pl.program_id(0)
    turned = w_ref[...].T
    for rows in pieces(total_ref.shape[0], 4):
        part = project(d_pre_ref[rows, :], turned)

        @pl.when(step == 0)
        def _():
            total_ref[rows, :] = d_ref[rows, :] + part

        @pl.when(step > 0)
        def _():
            total_ref[rows, :] += part

    @pl.when(step == pl.num_programs(0) - 1)
    def _():
        sum_ref[...] = jnp.zeros_like(sum_ref)
        w_out_turned = w_out_ref[...].T
        for rows in pieces(total_ref.shape[0], 8):
            d_first = total_ref[rows, :]
            unit = unit_ref[rows, :]
            d_inner = normal_back(d_first * line(vec_ref, GAIN_ONE), unit, inverse_ref[rows, 0:1])
            low = d_inner.astype(LOW)
            out_ref[rows, :] = d_inner
            low_ref[rows, :] = low
            attended_ref[rows, :] = project(low, w_out_turned).astype(LOW)
            add_line(sum_ref, 0, d_first * unit)
            add_line(sum_ref, 1, d_first)
            add_line(sum_ref, 2, d_inner)


def inner_back(d_pre, w_inner, d_second, unit, inverse, vec, w_out):
    count, hidden = d_pre.shape
    return pl.pallas_call(
        inner_back_kernel,
        grid=(hidden // COLUMNS,),
        in_specs=[
            columns_of(count),
            columns_of(D),
            kept((count, D)),
            kept((count, D)),
            kept((count, LANES)),
            kept((8, D)),
            kept((D, D)),
        ],
        out_specs=[kept((count, D)), kept((count, D)), kept((count, D)), kept((8, D))],
        out_shape=[
            jax.ShapeDtypeStruct((count, D), FULL),
            jax.ShapeDtypeStruct((count, D), LOW),
            jax.ShapeDtypeStruct((count, D), LOW),
            jax.ShapeDtypeStruct((8, D), FULL),
        ],
        scratch_shapes=[pltpu.VMEM((count, D), FULL)],
        compiler_params=LIMIT,
        name="inner_back",
    )(d_pre, w_inner, d_second, unit, inverse, vec, w_out)


def tokens_kernel(base_ref, d_ref, w_ref, out_ref):
    out_ref[...] = (base_ref[...] + against(d_ref[...], w_ref[...])).astype(out_ref.dtype)


def tokens_back(base, d_group, w_group, kind):
    count, wide = d_group.shape
    return pl.pallas_call(
        tokens_kernel,
        grid=(count // ROWS,),
        in_specs=[rows_of(D), rows_of(wide), kept((D, wide))],
        out_specs=rows_of(D),
        out_shape=jax.ShapeDtypeStruct((count, D), kind),
        compiler_params=LIMIT,
        name="tokens_back",
    )(base, d_group, w_group)


def turn_kernel(ref, out_ref):
    out_ref[...] = ref[...].T


def turn(values):
    count, width = values.shape
    return pl.pallas_call(
        turn_kernel,
        grid=(count // ROWS,),
        in_specs=[rows_of(width)],
        out_specs=pl.BlockSpec((width, ROWS), lambda i: (0, i)),
        out_shape=jax.ShapeDtypeStruct((width, count), values.dtype),
        name="turn",
    )(values)


def product_kernel(left_ref, right_ref, out_ref):
    out_ref[...] = project(left_ref[...], right_ref[...]).astype(LOW)


def product(left, right):
    height, depth = left.shape
    return pl.pallas_call(
        product_kernel,
        grid=(right.shape[1] // COLUMNS,),
        in_specs=[kept((height, depth)), columns_of(depth)],
        out_specs=columns_of(height),
        out_shape=jax.ShapeDtypeStruct((height, right.shape[1]), LOW),
        compiler_params=LIMIT,
        name="product",
    )(left, right)


def assemble_kernel(moves, align, place_ref, *refs):
    out_ref, sems = refs[-2], refs[-1]
    copies = []
    for i, (which, start, rows) in enumerate(moves):
        place = pl.multiple_of(place_ref[i], align)
        source = refs[which].at[pl.ds(start, rows)]
        copies.append(pltpu.make_async_copy(source, out_ref.at[pl.ds(place, rows)], sems.at[i]))
    for copy in copies:
        copy.start()
    for copy in copies:
        copy.wait()


def assemble(arrays, moves, places, rows):
    align = min(move[2] for move in moves)
    return pl.pallas_call(
        functools.partial(assemble_kernel, moves, align),
        in_specs=[pl.BlockSpec(memory_space=pltpu.SMEM)] + [pl.BlockSpec(memory_space=pl.ANY)] * len(arrays),
        out_specs=pl.BlockSpec(memory_space=pltpu.VMEM),
        out_shape=jax.ShapeDtypeStruct((rows,) + arrays[0].shape[1:], arrays[0].dtype),
        scratch_shapes=[pltpu.SemaphoreType.DMA((len(moves),))],
        compiler_params=pltpu.CompilerParams(vmem_limit_bytes=24 * 2**20),
        name="assemble",
    )(jnp.stack(places).astype(jnp.int32), *arrays)


def pack_kernel(size, rows, vectors, *refs):
    out_ref = refs[-1]
    out_ref[...] = jnp.zeros_like(out_ref)
    for shard in range(size):
        at = shard * rows
        for spans in vectors:
            lines = []
            for which, row, first, length in spans:
                lines += [(which, row, first + i) for i in range(0, length, LANES)]
            share = len(lines) // size
            for which, row, first in lines[shard * share : (shard + 1) * share]:
                out_ref[at : at + 1, :] = refs[which][row : row + 1, first : first + LANES]
                at += 1


def pack(arrays, vectors, size, rows):
    if any(sum(span[3] for span in spans) % (size * LANES) for spans in vectors):
        whole = [
            jnp.concatenate([arrays[which][row, first : first + length] for which, row, first, length in spans])
            for spans in vectors
        ]
        small = jnp.concatenate([vector.reshape(size, -1) for vector in whole], axis=1)
        small = jnp.pad(small, ((0, 0), (0, rows * LANES - small.shape[1])))
        return small.reshape(size * rows, LANES).astype(LOW)
    return pl.pallas_call(
        functools.partial(pack_kernel, size, rows, vectors),
        out_shape=jax.ShapeDtypeStruct((size * rows, LANES), FULL),
        name="pack",
    )(*arrays).astype(LOW)


def unpack_kernel(count, place_ref, *refs):
    vec_ref, bias_ref, group_ref = refs[count:]
    group_ref[...] = jnp.zeros_like(group_ref)
    hidden = bias_ref.shape[1] // count
    for i in range(count):
        chunk = refs[i][...].astype(FULL)
        owner = place_ref[i]
        start = pl.multiple_of(owner * LANES, LANES)
        for row in range(8):
            vec_ref[row : row + 1, pl.ds(start, LANES)] = chunk[row : row + 1, :]
        for row in range(hidden // LANES):
            first = pl.multiple_of(owner * hidden + row * LANES, LANES)
            bias_ref[:, pl.ds(first, LANES)] = chunk[8 + row : 9 + row, :]
        group = owner * LANES // WIDE
        for place, row in ((0, QUERY), (2, VALUE)):
            first = pl.multiple_of(group * 2 * WIDE + place * WIDE + start, LANES)
            group_ref[:, pl.ds(first, LANES)] = chunk[row : row + 1, :]


def unpack(chunks, owners, hidden):
    count = len(chunks)
    return pl.pallas_call(
        functools.partial(unpack_kernel, count),
        in_specs=[pl.BlockSpec(memory_space=pltpu.SMEM)] + [pl.BlockSpec(memory_space=pltpu.VMEM)] * count,
        out_shape=[
            jax.ShapeDtypeStruct((8, D), FULL),
            jax.ShapeDtypeStruct((1, hidden), FULL),
            jax.ShapeDtypeStruct((1, 3 * D), FULL),
        ],
        name="unpack",
    )(jnp.stack(owners).astype(jnp.int32), *chunks)


def tie(*values):
    return lax.optimization_barrier(values)


class Links:
    def __init__(self, mesh):
        self.reps, self.size = mesh.shape["cross"] * mesh.shape["core"], mesh.shape["shard"]
        size = self.size
        self.direct = size > RING_MOST or size % 2 == 1
        self.order = list(range(0, size, 2)) + list(range(size - 1, 0, -2))
        self.far = size // 2
        self.near = size - 1 - self.far
        shard = lax.axis_index("shard")
        self.core = lax.axis_index("core")
        self.sign = 1 - 2 * self.core
        self.place = jnp.where(shard % 2 == 0, shard // 2, size - 1 - shard // 2)

    def owner(self, step):
        place = (self.place + self.sign * step + 2 * self.size) % self.size
        return jnp.where(place < self.size // 2, 2 * place, 2 * (self.size - place) - 1)

    def hop(self, values, sign):
        pairs = []
        for rep in range(self.reps):
            turn = sign if rep % 2 == 0 else -sign
            for i, shard in enumerate(self.order):
                target = self.order[(i + turn) % self.size]
                pairs.append((rep * self.size + shard, rep * self.size + target))
        return lax.ppermute(values, AXES, pairs)

    def swap(self, values, bit):
        pairs = []
        for rep in range(self.reps):
            for shard in range(self.size):
                pairs.append((rep * self.size + shard, (rep ^ bit) * self.size + shard))
        return lax.ppermute(values, AXES, pairs)

    def half_of(self, values):
        half = values.shape[0] // 2
        return lax.dynamic_slice_in_dim(values, self.core * half, half, axis=0)


    def gather_small(self, values, hidden):
        if self.direct:
            small = lax.all_gather(values, "shard", axis=0, tiled=True).reshape(self.size, -1).astype(FULL)
            width, share = D // self.size, hidden // self.size
            vec = small[:, : 8 * width].reshape(self.size, 8, width).swapaxes(0, 1).reshape(8, D)
            bias = small[:, 8 * width : 8 * width + share].reshape(1, hidden)
            none = jnp.zeros((WIDE,), FULL)
            spans = [slice(g * WIDE, (g + 1) * WIDE) for g in range(GROUPS)]
            parts = [part for span in spans for part in (vec[QUERY, span], none, vec[VALUE, span])]
            return vec, bias, jnp.concatenate(parts).reshape(1, 3 * D)
        found = [(values, 0)]
        ahead = back = values
        for step in range(1, self.far + 1):
            ahead = self.hop(ahead, 1)
            found.append((ahead, -step))
            if step <= self.near:
                back = self.hop(back, -1)
                found.append((back, step))
            ahead, back = yield [ahead, back]
        owners = [self.owner(step) for _, step in found]
        return unpack([chunk for chunk, _ in found], owners, hidden)

    def gather(self, values):
        if self.direct:
            return lax.all_gather(values, "shard", axis=0, tiled=True)
        rows = values.shape[0]
        half = rows // 2
        arrays = [values]
        moves = [(0, 0, rows)]
        places = [self.owner(0) * rows]

        def keep(chunk, mine, step):
            moves.append((len(arrays), 0, half))
            arrays.append(chunk)
            core = self.core if mine else 1 - self.core
            places.append(self.owner(step) * rows + core * half)

        ahead = back = self.half_of(values)
        for step in range(1, self.far + 2):
            flight = []
            if step > 1:
                keep(ahead, True, 1 - step)
                flight.append((self.swap(ahead, 1), step - 1))
                if step - 1 <= self.near:
                    keep(back, True, step - 1)
                    flight.append((self.swap(back, 1), 1 - step))
            if step <= self.far:
                ahead = self.hop(ahead, 1)
            if step <= self.near:
                back = self.hop(back, -1)
            ahead, back, *swapped = yield [ahead, back] + [chunk for chunk, _ in flight]
            for chunk, (_, place) in zip(swapped, flight):
                keep(chunk, False, place)
        return assemble(arrays, moves, places, self.size * rows)

    def gather_quarters(self, values):
        if self.direct:
            return lax.all_gather(values, "shard", axis=0, tiled=True)
        rows = values.shape[0]
        half, part = rows // 2, rows // 4
        place = self.core * half + lax.axis_index("cross") * part
        mine = lax.dynamic_slice_in_dim(values, place, part, axis=0)
        mine = lax.all_gather(mine, ("shard", "cross"), axis=0, tiled=True)
        (mine,) = yield [mine]
        (other,) = yield [self.swap(mine, 1)]
        moves, places = [], []
        for shard in range(self.size):
            moves += [(0, shard * half, half), (1, shard * half, half)]
            places += [shard * rows + self.core * half, shard * rows + (1 - self.core) * half]
        return assemble([mine, other], moves, places, self.size * rows)

    def reduce_halves(self, values, rounds):
        if self.direct:
            own = lax.psum_scatter(values, "shard", scatter_dimension=0, tiled=True)
            return lax.psum(own, ("cross", "core")).astype(FULL)
        width = values.shape[1]
        half = values.shape[0] // self.size // 2
        split = values.reshape(self.size, 2, half, width)
        other = self.swap(lax.dynamic_index_in_dim(split, 1 - self.core, axis=1, keepdims=False), 1)
        (other,) = yield [other]
        mine = lax.dynamic_index_in_dim(split, self.core, axis=1, keepdims=False)
        total = (mine.astype(FULL) + other.astype(FULL)).astype(LOW).reshape(self.size * half, width)
        (total,) = yield [total]
        total = lax.psum_scatter(total, "shard", scatter_dimension=0, tiled=True)
        for _ in range(rounds):
            yield []
        (total,) = yield [total]
        return (yield from self.finish(total))

    def finish(self, total):
        (cross,) = yield [self.swap(total, 2)]
        total = (total.astype(FULL) + cross.astype(FULL)).astype(LOW)
        (pair,) = yield [self.swap(total, 1)]
        low = jnp.where(self.core == 0, total, pair)
        high = jnp.where(self.core == 0, pair, total)
        return jnp.concatenate([low, high], axis=0).astype(FULL)

    def reduce(self, values):
        if self.direct:
            own = lax.psum_scatter(values, "shard", scatter_dimension=0, tiled=True)
            return lax.psum(own, ("cross", "core")).astype(FULL)
        width = values.shape[1]
        half = values.shape[0] // self.size // 2
        split = values.reshape(self.size, 2, half, width)
        other = self.swap(lax.dynamic_index_in_dim(split, 1 - self.core, axis=1, keepdims=False), 1)
        (other,) = yield [other]

        def piece(step):
            owner = self.owner(step)
            own = lax.dynamic_slice(split, (owner, self.core, 0, 0), (1, 1, half, width))
            pair = lax.dynamic_slice(other, (owner, 0, 0), (1, half, width))
            return own[0, 0].astype(FULL) + pair[0].astype(FULL)

        ahead = piece(self.far).astype(LOW)
        back = piece(-self.near).astype(LOW)
        for step in range(self.far - 1, -1, -1):
            moving = [self.hop(ahead, 1)]
            if step < self.near:
                moving.append(self.hop(back, -1))
            ahead, *rest = yield moving
            if step > 0:
                ahead = (ahead.astype(FULL) + piece(step)).astype(LOW)
            if rest:
                back = rest[0]
                if step > 0:
                    back = (back.astype(FULL) + piece(-step)).astype(LOW)
        total = (piece(0) + ahead.astype(FULL) + back.astype(FULL)).astype(LOW)
        return (yield from self.finish(total))


class Flow:
    def __init__(self):
        self.running = {}
        self.results = {}

    def start(self, name, steps):
        self._move(name, steps, None)

    def _move(self, name, steps, values):
        try:
            self.running[name] = (steps, steps.send(values))
        except StopIteration as end:
            self.running.pop(name, None)
            self.results[name] = end.value

    def advance(self, *values, near=None):
        running = [item for item in self.running.items() if near is None or item[0] in near]
        flat = list(values)
        for _, (_, flight) in running:
            flat += flight
        tied = tie(*flat) if flat else ()
        at = len(values)
        for name, (steps, flight) in running:
            self._move(name, steps, list(tied[at : at + len(flight)]))
            at += len(flight)
        return tied[0] if len(values) == 1 else tuple(tied[: len(values)])

    def take(self, name):
        while name in self.running:
            steps, flight = self.running[name]
            self._move(name, steps, flight)
        return self.results[name]


def shards(
    mesh,
    tokens,
    w_query,
    w_key,
    w_value,
    b_query,
    b_value,
    w_out,
    b_out,
    gain_one,
    shift_one,
    w_inner,
    b_inner,
    w_outer,
    b_outer,
    gain_two,
    shift_two,
    cotangent,
):
    links = Links(mesh)
    size = links.size
    width = D // size
    hidden = b_inner.shape[0]

    own_groups = [
        jnp.concatenate([w[:, g * WIDE : (g + 1) * WIDE] for w in (w_query, w_key, w_value)], axis=1)
        for g in range(GROUPS)
    ]
    vectors = (b_query, b_value, b_out, gain_one, shift_one, b_outer, gain_two, shift_two)
    used = len(vectors) * width + hidden
    room = -(-used // (32 * LANES)) * 32 * LANES
    flow = Flow()
    flow.start("group0", links.gather(own_groups[0]))
    w_inner = flow.advance(w_inner)
    flow.start("inner", links.gather_quarters(w_inner))
    own_groups[1], w_outer, *own_vectors = flow.advance(
        own_groups[1], w_outer, *vectors, b_inner, near=("group0",)
    )
    flow.start("outer", links.gather_quarters(w_outer))
    flow.start("group1", links.gather(own_groups[1]))
    packed = jnp.pad(jnp.concatenate(own_vectors), (0, room - used))
    flow.start("small", links.gather_small(packed.reshape(room // LANES, LANES), size * hidden))
    tokens_turned, w_out = flow.advance(turn(tokens), w_out, near=("group0", "group1", "small"))
    flow.start("out", links.gather(w_out))
    flow.advance(near=("group0", "group1", "small"))
    whole_groups = [flow.take("group0")]

    projected = []
    attended, lse = None, []
    for g in range(GROUPS):
        part = project(tokens, whole_groups[g])
        if g == 0:
            vec, bias_inner, bias_groups = flow.take("small")
        bias = bias_groups[:, g * 3 * WIDE : (g + 1) * 3 * WIDE]
        projected.append((part + bias).astype(LOW))
        if g == 0:
            projected[g] = flow.advance(projected[g], near=("group1", "out"))
            attended, logs = attend(projected[g], g, attended)
            attended = flow.advance(attended, near=("group1", "out", "inner"))
            whole_groups.append(flow.take("group1"))
        else:
            projected[g] = flow.advance(projected[g], near=("inner", "out"))
            attended, logs = attend(projected[g], g, attended)
            attended = flow.advance(attended, near=("inner", "out"))
        lse.append(logs)
    whole_out = flow.take("out")
    whole_inner = flow.take("inner")
    unit_one, inverse_one, first_low = out_norm(attended, whole_out, tokens, vec)
    first_low = flow.advance(first_low, near=("outer",))
    active, slope = inner_gelu(first_low, whole_inner, bias_inner)
    whole_outer = flow.take("outer")
    output, d_second, d_mid, sums_two = outer_norms(active, whole_outer, unit_one, vec, cotangent)

    grad_outer, d_mid = tie(gram(active, d_mid).astype(LOW), d_mid)
    flow.start("outer_back", links.reduce_halves(grad_outer, 4))
    d_pre, sum_inner = outer_back(d_mid, whole_outer, slope)
    d_pre = flow.advance(d_pre)
    grad_inner, d_pre = flow.advance(gram(first_low, d_pre).astype(LOW), d_pre)
    flow.start("inner_back", links.reduce(grad_inner))
    d_inner, d_branch, d_attended, sums_one = inner_back(
        d_pre, whole_inner, d_second, unit_one, inverse_one, vec, whole_out
    )
    d_branch, d_attended = flow.advance(d_branch, d_attended)
    grad_out, d_attended = tie(gram(attended, d_branch).astype(LOW), d_attended)
    flow.start("out_back", links.reduce(grad_out))

    d_groups, sums_group = [], []
    for g in range(GROUPS):
        d_group, sums = attend_back(projected[g], d_attended, lse[g], g)
        d_group, sums = flow.advance(d_group, sums)
        sums_group.append(sums)
        if g == GROUPS - 1:
            arrays = [sums_one, sums_two, sum_inner] + sums_group
            spans = [[(3 + h, 0, place * WIDE, WIDE) for h in range(GROUPS)] for place in (0, 2)]
            spans += [[(i, row, 0, D)] for i, row in ((0, 2), (0, 0), (0, 1), (1, 2), (1, 0), (1, 1))]
            spans += [[(2, 0, 0, size * hidden)]]
            small, d_group = tie(pack(arrays, spans, size, room // LANES), d_group)
            flow.start("small_back", links.reduce(small))
        grad_group, d_group, d_attended = flow.advance(product(tokens_turned, d_group), d_group, d_attended)
        flow.start(f"back{g}", links.reduce(grad_group))
        d_groups.append(d_group)
    d_groups[0] = flow.advance(d_groups[0])
    d_tokens = flow.advance(tokens_back(d_inner, d_groups[0], whole_groups[0], FULL))
    d_tokens = flow.advance(tokens_back(d_tokens, d_groups[1], whole_groups[1], LOW))
    own_inner = flow.take("inner_back")
    own_outer = flow.take("outer_back")
    own_out = flow.take("out_back")
    own_small = flow.take("small_back").reshape(room)
    own_groups = [flow.take(f"back{g}") for g in range(GROUPS)]

    def joined(parts, place):
        columns = slice(place * WIDE, (place + 1) * WIDE)
        return jnp.concatenate([part[..., columns] for part in parts], axis=-1)

    (
        own_bias_query,
        own_bias_value,
        own_bias_out,
        own_gain_one,
        own_shift_one,
        own_bias_outer,
        own_gain_two,
        own_shift_two,
    ) = (own_small[i * width : (i + 1) * width] for i in range(len(vectors)))
    own_bias_inner = own_small[used - hidden : used]
    return (
        output,
        d_tokens,
        joined(own_groups, 0),
        joined(own_groups, 1),
        joined(own_groups, 2),
        own_bias_query,
        own_bias_value,
        own_out,
        own_bias_out,
        own_gain_one,
        own_shift_one,
        own_inner,
        own_bias_inner,
        own_outer,
        own_bias_outer,
        own_gain_two,
        own_shift_two,
    )


def solution(mesh):
    reps, size = mesh.shape["rep"], mesh.shape["shard"]
    mesh = jax.sharding.Mesh(mesh.devices.reshape(reps // 2, 2, size), AXES)
    rows = P(AXES, None)
    matrix = P("shard", None)
    vector = P("shard")
    return jax.shard_map(
        functools.partial(shards, mesh),
        mesh=mesh,
        in_specs=(
            rows,
            matrix,
            matrix,
            matrix,
            vector,
            vector,
            matrix,
            vector,
            vector,
            vector,
            matrix,
            vector,
            matrix,
            vector,
            vector,
            vector,
            rows,
        ),
        out_specs=(
            rows,
            rows,
            matrix,
            matrix,
            matrix,
            vector,
            vector,
            matrix,
            vector,
            vector,
            vector,
            matrix,
            vector,
            matrix,
            vector,
            vector,
            vector,
        ),
        check_vma=False,
    )
```

```python
import functools

import jax
import jax.numpy as jnp
from jax import lax
from jax.experimental import pallas as pl
from jax.experimental.pallas import tpu as pltpu
from jax.sharding import PartitionSpec as P

D = 1024
H = 16
DH = 64
SEQ = 512
LANES = 128
GROUPS = 2
PAIRS = D // LANES // GROUPS
WIDE = D // GROUPS
AXES = ("cross", "core", "shard")
RING_MOST = 16
LOW = jnp.bfloat16
FULL = jnp.float32


def project(left, right):
    return jnp.dot(left, right, preferred_element_type=FULL)


def gram(left, right):
    return lax.dot_general(left, right, (((0,), (0,)), ((), ())), preferred_element_type=FULL)


def against(left, right):
    return lax.dot_general(left, right, (((1,), (1,)), ((), ())), preferred_element_type=FULL)


def normal(values):
    centre = values - jnp.mean(values, axis=-1, keepdims=True)
    spread = jnp.mean(centre * centre, axis=-1, keepdims=True)
    inverse = lax.rsqrt(spread + 1e-12)
    return centre * inverse, inverse


def normal_back(scaled, unit, inverse):
    mean = jnp.mean(scaled, axis=-1, keepdims=True)
    along = jnp.mean(scaled * unit, axis=-1, keepdims=True)
    return (scaled - mean - unit * along) * inverse


def head_mask(head):
    lane = lax.broadcasted_iota(jnp.int32, (SEQ, LANES), 1)
    return (lane // DH) == head


def attend_kernel(query_ref, key_ref, value_ref, *rest):
    out_ref, lse_ref = rest[-2:]
    query = query_ref[...] * LOW(0.125)
    key = key_ref[...]
    value_t = value_ref[...].T
    parts = []
    for head in range(LANES // DH):
        own = jnp.where(head_mask(head), query, jnp.zeros_like(query))
        scores = against(key, own)
        top = jnp.max(scores, axis=0, keepdims=True)
        expo = jnp.exp(scores - top)
        total = jnp.sum(expo, axis=0, keepdims=True)
        mixed = project(value_t[head * DH : (head + 1) * DH], expo.astype(LOW))
        parts.append(mixed * (1.0 / total))
        lse_ref[0, head : head + 1, :] = top + jnp.log(total)
    out_ref[...] = jnp.concatenate(parts, axis=0).T.astype(LOW)


def attend_back_kernel(query_ref, key_ref, value_ref, d_ref, lse_ref, out_ref, sum_ref):
    seq, pair = pl.program_id(0), pl.program_id(1)
    query = query_ref[...] * LOW(0.125)
    key = key_ref[...]
    value = value_ref[...]
    d_out = d_ref[...]
    key_t = key.T
    d_key = None
    d_value = None
    d_query = []
    for head in range(LANES // DH):
        mask = head_mask(head)
        own = jnp.where(mask, query, jnp.zeros_like(query))
        d_own = jnp.where(mask, d_out, jnp.zeros_like(d_out))
        probs = jnp.exp(against(key, own) - lse_ref[0, head : head + 1, :])
        d_probs = against(value, d_own)
        inner = jnp.sum(probs * d_probs, axis=0, keepdims=True)
        d_scores = (probs * (d_probs - inner)).astype(LOW)
        part_value = project(probs.astype(LOW), d_own)
        part_key = project(d_scores, own)
        d_value = part_value if d_value is None else d_value + part_value
        d_key = part_key if d_key is None else d_key + part_key
        d_query.append(project(key_t[head * DH : (head + 1) * DH], d_scores))
    d_query = jnp.concatenate(d_query, axis=0).T * 0.125
    for place, grad in enumerate((d_query, d_key, d_value)):
        start = pl.multiple_of(place * WIDE + pair * LANES, LANES)
        out_ref[:, pl.ds(start, LANES)] = grad.astype(LOW)
        total = jnp.sum(grad, axis=0, keepdims=True)
        before = sum_ref[0:1, pl.ds(start, LANES)]
        sum_ref[0:1, pl.ds(start, LANES)] = jnp.where(seq == 0, total, before + total)


def column_block(first):
    return pl.BlockSpec((SEQ, LANES), lambda seq, pair: (seq, first + pair))


LSE_BLOCK = pl.BlockSpec((1, LANES // DH, SEQ), lambda seq, pair: (seq * PAIRS + pair, 0, 0))


def triple():
    return [column_block(place * PAIRS) for place in range(3)]


def attend(qkv, group, before):
    count = qkv.shape[0]
    seqs = count // SEQ
    kept = [] if before is None else [before]
    return pl.pallas_call(
        attend_kernel,
        grid=(seqs, PAIRS),
        in_specs=triple() + [pl.BlockSpec(memory_space=pl.ANY)] * len(kept),
        out_specs=[column_block(group * PAIRS), LSE_BLOCK],
        out_shape=[
            jax.ShapeDtypeStruct((count, D), LOW),
            jax.ShapeDtypeStruct((seqs * PAIRS, LANES // DH, SEQ), FULL),
        ],
        input_output_aliases={3: 0} if kept else {},
        compiler_params=pltpu.CompilerParams(vmem_limit_bytes=32 * 2**20),
        name="attend",
    )(qkv, qkv, qkv, *kept)


def attend_back(qkv, d_attended, lse, group):
    count = qkv.shape[0]
    return pl.pallas_call(
        attend_back_kernel,
        grid=(count // SEQ, PAIRS),
        in_specs=triple() + [column_block(group * PAIRS), LSE_BLOCK],
        out_specs=[
            pl.BlockSpec((SEQ, 3 * WIDE), lambda seq, pair: (seq, 0)),
            pl.BlockSpec((8, 3 * WIDE), lambda seq, pair: (0, 0)),
        ],
        out_shape=[
            jax.ShapeDtypeStruct((count, 3 * WIDE), LOW),
            jax.ShapeDtypeStruct((8, 3 * WIDE), FULL),
        ],
        compiler_params=pltpu.CompilerParams(vmem_limit_bytes=40 * 2**20),
        name="attend_back",
    )(qkv, qkv, qkv, d_attended, lse)


ROWS = 256
COLUMNS = 512
EXTRA = 16
PARTS = 2
(QUERY, VALUE, OUT, GAIN_ONE, SHIFT_ONE, OUTER, GAIN_TWO, SHIFT_TWO) = range(8)


def line(ref, row):
    return ref[row : row + 1, :]


def kept(shape):
    return pl.BlockSpec(shape, lambda i: (0,) * len(shape), pipeline_mode=pl.Buffered(1))


def rows_of(width):
    return pl.BlockSpec((ROWS, width), lambda i: (i, 0))


def columns_of(height):
    return pl.BlockSpec((height, COLUMNS), lambda i: (0, i))


def add_line(ref, row, values):
    ref[row : row + 1, :] += jnp.sum(values, axis=0, keepdims=True)


def clear(ref):
    @pl.when(pl.program_id(0) == 0)
    def _():
        ref[...] = jnp.zeros_like(ref)


def pieces(rows, count=PARTS):
    step = rows // count
    return [slice(i * step, (i + 1) * step) for i in range(count)]


LIMIT = pltpu.CompilerParams(vmem_limit_bytes=48 * 2**20)


def out_kernel(attended_ref, w_ref, tokens_ref, vec_ref, unit_ref, inverse_ref, low_ref):
    for rows in pieces(ROWS):
        branch = project(attended_ref[rows, :], w_ref[...]) + line(vec_ref, OUT)
        unit, inverse = normal(tokens_ref[rows, :].astype(FULL) + branch)
        unit_ref[rows, :] = unit
        inverse_ref[rows, :] = jnp.broadcast_to(inverse, (inverse.shape[0], LANES))
        low_ref[rows, :] = (unit * line(vec_ref, GAIN_ONE) + line(vec_ref, SHIFT_ONE)).astype(LOW)


def out_norm(attended, w_out, tokens, vec):
    count = tokens.shape[0]
    return pl.pallas_call(
        out_kernel,
        grid=(count // ROWS,),
        in_specs=[rows_of(D), kept((D, D)), rows_of(D), kept((8, D))],
        out_specs=[rows_of(D), rows_of(LANES), rows_of(D)],
        out_shape=[
            jax.ShapeDtypeStruct((count, D), FULL),
            jax.ShapeDtypeStruct((count, LANES), FULL),
            jax.ShapeDtypeStruct((count, D), LOW),
        ],
        compiler_params=LIMIT,
        name="out_norm",
    )(attended, w_out, tokens, vec)


def inner_kernel(low_ref, w_ref, bias_ref, active_ref, slope_ref):
    for rows in pieces(low_ref.shape[0], 4):
        pre = project(low_ref[rows, :], w_ref[...]) + bias_ref[...]
        below = 0.5 * (1.0 + lax.erf(pre * (0.5**0.5)))
        active_ref[rows, :] = (pre * below).astype(LOW)
        slope_ref[rows, :] = (below + pre * jnp.exp(-0.5 * pre * pre) * 0.3989422804014327).astype(LOW)


def inner_gelu(low, w_inner, bias):
    count, hidden = low.shape[0], w_inner.shape[1]
    return pl.pallas_call(
        inner_kernel,
        grid=(hidden // COLUMNS,),
        in_specs=[kept((count, D)), columns_of(D), columns_of(1)],
        out_specs=[columns_of(count), columns_of(count)],
        out_shape=[jax.ShapeDtypeStruct((count, hidden), LOW)] * 2,
        compiler_params=LIMIT,
        name="inner_gelu",
    )(low, w_inner, bias)


def outer_kernel(active_ref, w_ref, unit_ref, vec_ref, cot_ref, out_ref, d_ref, d_low_ref, sum_ref):
    clear(sum_ref)
    for rows in pieces(ROWS):
        first = unit_ref[rows, :] * line(vec_ref, GAIN_ONE) + line(vec_ref, SHIFT_ONE)
        second = first + project(active_ref[rows, :], w_ref[...]) + line(vec_ref, OUTER)
        unit, inverse = normal(second)
        out_ref[rows, :] = (unit * line(vec_ref, GAIN_TWO) + line(vec_ref, SHIFT_TWO)).astype(LOW)
        cot = cot_ref[rows, :].astype(FULL)
        d_second = normal_back(cot * line(vec_ref, GAIN_TWO), unit, inverse)
        d_ref[rows, :] = d_second
        d_low_ref[rows, :] = d_second.astype(LOW)
        add_line(sum_ref, 0, cot * unit)
        add_line(sum_ref, 1, cot)
        add_line(sum_ref, 2, d_second)


def outer_norms(active, w_outer, unit, vec, cotangent):
    count, hidden = active.shape
    return pl.pallas_call(
        outer_kernel,
        grid=(count // ROWS,),
        in_specs=[rows_of(hidden), kept((hidden, D)), rows_of(D), kept((8, D)), rows_of(D)],
        out_specs=[rows_of(D), rows_of(D), rows_of(D), kept((8, D))],
        out_shape=[
            jax.ShapeDtypeStruct((count, D), LOW),
            jax.ShapeDtypeStruct((count, D), FULL),
            jax.ShapeDtypeStruct((count, D), LOW),
            jax.ShapeDtypeStruct((8, D), FULL),
        ],
        compiler_params=LIMIT,
        name="outer_norms",
    )(active, w_outer, unit, vec, cotangent)


def outer_back_kernel(d_ref, w_ref, slope_ref, out_ref, sum_ref):
    sum_ref[...] = jnp.zeros_like(sum_ref)
    for rows in pieces(d_ref.shape[0]):
        d_pre = against(d_ref[rows, :], w_ref[...]) * slope_ref[rows, :].astype(FULL)
        out_ref[rows, :] = d_pre.astype(LOW)
        add_line(sum_ref, 0, d_pre)


def outer_back(d_mid, w_outer, slope):
    count, hidden = slope.shape
    return pl.pallas_call(
        outer_back_kernel,
        grid=(hidden // COLUMNS,),
        in_specs=[kept((count, D)), pl.BlockSpec((COLUMNS, D), lambda i: (i, 0)), columns_of(count)],
        out_specs=[columns_of(count), columns_of(1)],
        out_shape=[
            jax.ShapeDtypeStruct((count, hidden), LOW),
            jax.ShapeDtypeStruct((1, hidden), FULL),
        ],
        compiler_params=LIMIT,
        name="outer_back",
    )(d_mid, w_outer, slope)


def inner_back_kernel(
    d_pre_ref, w_ref, d_ref, unit_ref, inverse_ref, vec_ref, w_out_ref, before_ref, *refs
):
    out_ref, low_ref, attended_ref, sum_ref, total_ref = refs[-5:]
    step = pl.program_id(0)
    part = against(d_pre_ref[...], w_ref[...])

    @pl.when(step == 0)
    def _():
        total_ref[...] = d_ref[...] + part

    @pl.when(step > 0)
    def _():
        total_ref[...] += part

    @pl.when(step == pl.num_programs(0) - 1)
    def _():
        sum_ref[...] = before_ref[...]
        for rows in pieces(total_ref.shape[0], 2):
            d_first = total_ref[rows, :]
            unit = unit_ref[rows, :]
            d_inner = normal_back(d_first * line(vec_ref, GAIN_ONE), unit, inverse_ref[rows, 0:1])
            low = d_inner.astype(LOW)
            out_ref[rows, :] = d_inner
            low_ref[rows, :] = low
            attended_ref[rows, :] = against(low, w_out_ref[...]).astype(LOW)
            add_line(sum_ref, 0, d_first * unit)
            add_line(sum_ref, 1, d_first)
            add_line(sum_ref, 2, d_inner)


def inner_back(part, d_pre, w_inner, d_second, unit, inverse, vec, w_out, sums, before):
    count, hidden = d_pre.shape
    rows = count // 2

    def own(width):
        return pl.BlockSpec((rows, width), lambda i: (part, 0), pipeline_mode=pl.Buffered(1))

    return pl.pallas_call(
        inner_back_kernel,
        grid=(hidden // COLUMNS,),
        in_specs=[
            pl.BlockSpec((rows, COLUMNS), lambda i: (part, i)),
            columns_of(D),
            own(D),
            own(D),
            own(LANES),
            kept((8, D)),
            kept((D, D)),
            kept((8, D)),
        ]
        + [pl.BlockSpec(memory_space=pl.ANY)] * len(before),
        out_specs=[own(D), own(D), own(D), kept((8, D))],
        out_shape=[
            jax.ShapeDtypeStruct((count, D), FULL),
            jax.ShapeDtypeStruct((count, D), LOW),
            jax.ShapeDtypeStruct((count, D), LOW),
            jax.ShapeDtypeStruct((8, D), FULL),
        ],
        input_output_aliases={8 + i: i for i in range(len(before))},
        scratch_shapes=[pltpu.VMEM((rows, D), FULL)],
        compiler_params=LIMIT,
        name="inner_back",
    )(d_pre, w_inner, d_second, unit, inverse, vec, w_out, sums, *before)


def tokens_kernel(base_ref, d_ref, w_ref, out_ref):
    out_ref[...] = (base_ref[...] + against(d_ref[...], w_ref[...])).astype(out_ref.dtype)


def tokens_back(base, d_group, w_group, kind):
    count, wide = d_group.shape
    return pl.pallas_call(
        tokens_kernel,
        grid=(count // ROWS,),
        in_specs=[rows_of(D), rows_of(wide), kept((D, wide))],
        out_specs=rows_of(D),
        out_shape=jax.ShapeDtypeStruct((count, D), kind),
        compiler_params=LIMIT,
        name="tokens_back",
    )(base, d_group, w_group)


def turn_kernel(ref, out_ref):
    out_ref[...] = ref[...].T


def turn(values):
    count, width = values.shape
    return pl.pallas_call(
        turn_kernel,
        grid=(count // ROWS,),
        in_specs=[rows_of(width)],
        out_specs=pl.BlockSpec((width, ROWS), lambda i: (0, i)),
        out_shape=jax.ShapeDtypeStruct((width, count), values.dtype),
        name="turn",
    )(values)


def product_kernel(left_ref, right_ref, out_ref):
    out_ref[...] = project(left_ref[...], right_ref[...]).astype(LOW)


def product_extra_kernel(size, left_ref, right_ref, small_ref, out_ref):
    found = project(left_ref[...], right_ref[...]).astype(LOW)
    body = found.shape[0] // size // 2
    for shard in range(size):
        extra = jnp.broadcast_to(small_ref[shard : shard + 1, :], (EXTRA, found.shape[1])).astype(LOW)
        for core in range(2):
            half = 2 * shard + core
            at = half * (body + EXTRA)
            out_ref[at : at + body, :] = found[half * body : (half + 1) * body]
            out_ref[at + body : at + body + EXTRA, :] = extra


def product(left, right, small=None, size=1):
    height, depth = left.shape
    rows = height if small is None else height + 2 * EXTRA * size
    return pl.pallas_call(
        product_kernel if small is None else functools.partial(product_extra_kernel, size),
        grid=(right.shape[1] // COLUMNS,),
        in_specs=[kept((height, depth)), columns_of(depth)] + ([] if small is None else [columns_of(size)]),
        out_specs=columns_of(rows),
        out_shape=jax.ShapeDtypeStruct((rows, right.shape[1]), LOW),
        compiler_params=LIMIT,
        name="product",
    )(left, right, *([] if small is None else [small]))


def assemble_kernel(moves, align, place_ref, *refs):
    out_ref, sems = refs[-2], refs[-1]
    copies = []
    for i, (which, start, rows) in enumerate(moves):
        place = pl.multiple_of(place_ref[i], align)
        source = refs[which].at[pl.ds(start, rows)]
        copies.append(pltpu.make_async_copy(source, out_ref.at[pl.ds(place, rows)], sems.at[i]))
    for copy in copies:
        copy.start()
    for copy in copies:
        copy.wait()


def assemble(arrays, moves, places, rows):
    align = min(move[2] for move in moves)
    return pl.pallas_call(
        functools.partial(assemble_kernel, moves, align),
        in_specs=[pl.BlockSpec(memory_space=pltpu.SMEM)] + [pl.BlockSpec(memory_space=pl.ANY)] * len(arrays),
        out_specs=pl.BlockSpec(memory_space=pltpu.VMEM),
        out_shape=jax.ShapeDtypeStruct((rows,) + arrays[0].shape[1:], arrays[0].dtype),
        scratch_shapes=[pltpu.SemaphoreType.DMA((len(moves),))],
        compiler_params=pltpu.CompilerParams(vmem_limit_bytes=24 * 2**20),
        name="assemble",
    )(jnp.stack(places).astype(jnp.int32), *arrays)


def pack_kernel(size, vectors, *refs):
    out_ref = refs[-1]
    for shard in range(size):
        at = 0
        for spans in vectors:
            lines = []
            for which, row, first, length in spans:
                lines += [(which, row, first + i) for i in range(0, length, LANES)]
            share = len(lines) // size
            for which, row, first in lines[shard * share : (shard + 1) * share]:
                out_ref[shard : shard + 1, at : at + LANES] = refs[which][row : row + 1, first : first + LANES]
                at += LANES


def pack(arrays, vectors, size):
    lengths = [sum(span[3] for span in spans) for spans in vectors]
    if any(length % (size * LANES) for length in lengths):
        whole = [
            jnp.concatenate([arrays[which][row, first : first + length] for which, row, first, length in spans])
            for spans in vectors
        ]
        return jnp.concatenate([vector.reshape(size, -1) for vector in whole], axis=1)
    return pl.pallas_call(
        functools.partial(pack_kernel, size, vectors),
        out_shape=jax.ShapeDtypeStruct((size, sum(lengths) // size), FULL),
        name="pack",
    )(*arrays)


def unpack_kernel(count, body, place_ref, *refs):
    vec_ref, bias_ref, group_ref = refs[count:]
    group_ref[...] = jnp.zeros_like(group_ref)
    hidden = bias_ref.shape[1] // count
    for i in range(count):
        packed = refs[i][body : body + EXTRA, :].astype(FULL)[0:1, :]
        owner = place_ref[i]
        start = pl.multiple_of(owner * LANES, LANES)
        for row in range(8):
            vec_ref[row : row + 1, pl.ds(start, LANES)] = packed[:, row * LANES : (row + 1) * LANES]
        first = pl.multiple_of(owner * hidden, LANES)
        bias_ref[:, pl.ds(first, hidden)] = packed[:, 8 * LANES : 8 * LANES + hidden]
        group = owner * LANES // WIDE
        for place, row in ((0, QUERY), (2, VALUE)):
            first = pl.multiple_of(group * 2 * WIDE + place * WIDE + start, LANES)
            group_ref[:, pl.ds(first, LANES)] = packed[:, row * LANES : (row + 1) * LANES]


def unpack(chunks, owners, body, hidden):
    count = len(chunks)
    return pl.pallas_call(
        functools.partial(unpack_kernel, count, body),
        in_specs=[pl.BlockSpec(memory_space=pltpu.SMEM)] + [pl.BlockSpec(memory_space=pltpu.VMEM)] * count,
        out_shape=[
            jax.ShapeDtypeStruct((8, D), FULL),
            jax.ShapeDtypeStruct((1, hidden), FULL),
            jax.ShapeDtypeStruct((1, 3 * D), FULL),
        ],
        compiler_params=LIMIT,
        name="unpack",
    )(jnp.stack(owners).astype(jnp.int32), *chunks)


def tie(*values):
    return lax.optimization_barrier(values)


class Links:
    def __init__(self, mesh):
        self.reps, self.size = mesh.shape["cross"] * mesh.shape["core"], mesh.shape["shard"]
        size = self.size
        self.direct = size > RING_MOST or size % 2 == 1
        self.order = list(range(0, size, 2)) + list(range(size - 1, 0, -2))
        self.far = size // 2
        self.near = size - 1 - self.far
        shard = lax.axis_index("shard")
        self.core = lax.axis_index("core")
        self.sign = 1 - 2 * self.core
        self.place = jnp.where(shard % 2 == 0, shard // 2, size - 1 - shard // 2)

    def owner(self, step):
        place = (self.place + self.sign * step + 2 * self.size) % self.size
        return jnp.where(place < self.size // 2, 2 * place, 2 * (self.size - place) - 1)

    def hop(self, values, sign):
        pairs = []
        for rep in range(self.reps):
            turn = sign if rep % 2 == 0 else -sign
            for i, shard in enumerate(self.order):
                target = self.order[(i + turn) % self.size]
                pairs.append((rep * self.size + shard, rep * self.size + target))
        return lax.ppermute(values, AXES, pairs)

    def swap(self, values, bit):
        pairs = []
        for rep in range(self.reps):
            for shard in range(self.size):
                pairs.append((rep * self.size + shard, (rep ^ bit) * self.size + shard))
        return lax.ppermute(values, AXES, pairs)

    def half_of(self, values):
        half = values.shape[0] // 2
        return lax.dynamic_slice_in_dim(values, self.core * half, half, axis=0)


    def vectors(self, packed, hidden):
        small = lax.all_gather(packed, "shard", axis=0).astype(FULL)
        width, share = D // self.size, hidden // self.size
        vec = small[:, : 8 * width].reshape(self.size, 8, width).swapaxes(0, 1).reshape(8, D)
        bias = small[:, 8 * width : 8 * width + share].reshape(1, hidden)
        none = jnp.zeros((WIDE,), FULL)
        spans = [slice(g * WIDE, (g + 1) * WIDE) for g in range(GROUPS)]
        parts = [part for span in spans for part in (vec[QUERY, span], none, vec[VALUE, span])]
        return vec, bias, jnp.concatenate(parts).reshape(1, 3 * D)

    def gather(self, values, extra=0):
        if self.direct:
            return lax.all_gather(values, "shard", axis=0, tiled=True)
        half = values.shape[0] // 2
        body = half - extra
        rows = 2 * body
        arrays = [values]
        moves = [(0, 0, body), (0, half, body)]
        places = [self.owner(0) * rows, self.owner(0) * rows + body]
        chunks, owners = [values], [self.owner(0)]

        def keep(chunk, mine, step):
            moves.append((len(arrays), 0, body))
            arrays.append(chunk)
            core = self.core if mine else 1 - self.core
            places.append(self.owner(step) * rows + core * body)
            if mine:
                chunks.append(chunk)
                owners.append(self.owner(step))

        ahead = back = lax.dynamic_slice_in_dim(values, self.core * half, half, axis=0)
        for step in range(1, self.far + 2):
            flight = []
            if step > 1:
                keep(ahead, True, 1 - step)
                flight.append((self.swap(ahead, 1), step - 1))
                if step - 1 <= self.near:
                    keep(back, True, step - 1)
                    flight.append((self.swap(back, 1), 1 - step))
            if step <= self.far:
                ahead = self.hop(ahead, 1)
            if step <= self.near:
                back = self.hop(back, -1)
            ahead, back, *swapped = yield [ahead, back] + [chunk for chunk, _ in flight]
            for chunk, (_, place) in zip(swapped, flight):
                keep(chunk, False, place)
        whole = assemble(arrays, moves, places, self.size * rows)
        return (whole, chunks, owners) if extra else whole

    def gather_quarters(self, values):
        rows = values.shape[0] // self.reps
        index = lax.axis_index("cross") * 2 + self.core
        mine = lax.dynamic_slice_in_dim(values, index * rows, rows, axis=0)
        return lax.all_gather(mine, ("shard", "cross", "core"), axis=0, tiled=True)

    def finish(self, total):
        (cross,) = yield [self.swap(total, 2)]
        total = (total.astype(FULL) + cross.astype(FULL)).astype(LOW)
        (pair,) = yield [self.swap(total, 1)]
        low = jnp.where(self.core == 0, total, pair)
        high = jnp.where(self.core == 0, pair, total)
        return jnp.concatenate([low, high], axis=0).astype(FULL)

    def reduce(self, values):
        if self.direct:
            own = lax.psum_scatter(values, "shard", scatter_dimension=0, tiled=True)
            return lax.psum(own, ("cross", "core")).astype(FULL)
        width = values.shape[1]
        half = values.shape[0] // self.size // 2
        split = values.reshape(self.size, 2, half, width)
        other = self.swap(lax.dynamic_index_in_dim(split, 1 - self.core, axis=1, keepdims=False), 1)
        (other,) = yield [other]

        def piece(step):
            owner = self.owner(step)
            own = lax.dynamic_slice(split, (owner, self.core, 0, 0), (1, 1, half, width))
            pair = lax.dynamic_slice(other, (owner, 0, 0), (1, half, width))
            return own[0, 0].astype(FULL) + pair[0].astype(FULL)

        ahead = piece(self.far).astype(LOW)
        back = piece(-self.near).astype(LOW)
        for step in range(self.far - 1, -1, -1):
            moving = [self.hop(ahead, 1)]
            if step < self.near:
                moving.append(self.hop(back, -1))
            ahead, *rest = yield moving
            if step > 0:
                ahead = (ahead.astype(FULL) + piece(step)).astype(LOW)
            if rest:
                back = rest[0]
                if step > 0:
                    back = (back.astype(FULL) + piece(-step)).astype(LOW)
        total = (piece(0) + ahead.astype(FULL) + back.astype(FULL)).astype(LOW)
        return (yield from self.finish(total))


class Flow:
    def __init__(self):
        self.running = {}
        self.results = {}

    def start(self, name, steps):
        self._move(name, steps, None)

    def _move(self, name, steps, values):
        try:
            self.running[name] = (steps, steps.send(values))
        except StopIteration as end:
            self.running.pop(name, None)
            self.results[name] = end.value

    def advance(self, *values, near=None):
        running = [item for item in self.running.items() if near is None or item[0] in near]
        flat = list(values)
        for _, (_, flight) in running:
            flat += flight
        tied = tie(*flat) if flat else ()
        at = len(values)
        for name, (steps, flight) in running:
            self._move(name, steps, list(tied[at : at + len(flight)]))
            at += len(flight)
        return tied[0] if len(values) == 1 else tuple(tied[: len(values)])

    def take(self, name):
        while name in self.running:
            steps, flight = self.running[name]
            self._move(name, steps, flight)
        return self.results[name]


def shards(
    mesh,
    tokens,
    w_query,
    w_key,
    w_value,
    b_query,
    b_value,
    w_out,
    b_out,
    gain_one,
    shift_one,
    w_inner,
    b_inner,
    w_outer,
    b_outer,
    gain_two,
    shift_two,
    cotangent,
):
    links = Links(mesh)
    size = links.size
    width = D // size
    hidden = b_inner.shape[0]

    own_groups = [
        jnp.concatenate([w[:, g * WIDE : (g + 1) * WIDE] for w in (w_query, w_key, w_value)], axis=1)
        for g in range(GROUPS)
    ]
    vectors = (b_query, b_value, b_out, gain_one, shift_one, b_outer, gain_two, shift_two)
    used = len(vectors) * width + hidden
    ride = not links.direct and used <= 3 * WIDE and width == LANES
    packed = jnp.concatenate(vectors + (b_inner,))
    if ride:
        row = jnp.pad(packed, (0, 3 * WIDE - used)).reshape(1, 3 * WIDE)
        extra = jnp.broadcast_to(row, (EXTRA, 3 * WIDE))
        body = width // 2
        own_groups[0] = jnp.concatenate([own_groups[0][:body], extra, own_groups[0][body:], extra], axis=0)
    flow = Flow()
    whole_inner = links.gather_quarters(w_inner)
    flow.start("group0", links.gather(own_groups[0], EXTRA if ride else 0))
    flow.advance()
    own_groups[1] = flow.advance(own_groups[1])
    flow.start("group1", links.gather(own_groups[1]))
    tokens_turned, w_out = flow.advance(turn(tokens), w_out)
    flow.start("out", links.gather(w_out))
    flow.advance(near=("group0", "group1"))
    if ride:
        first_group, chunks, owners = flow.take("group0")
        vec, bias_inner, bias_groups = unpack(chunks, owners, body, size * hidden)
    else:
        first_group = flow.take("group0")
        vec, bias_inner, bias_groups = links.vectors(packed, size * hidden)
    whole_groups = [first_group]

    projected = []
    attended, lse = None, []
    for g in range(GROUPS):
        bias = bias_groups[:, g * 3 * WIDE : (g + 1) * 3 * WIDE]
        projected.append((project(tokens, whole_groups[g]) + bias).astype(LOW))
        if g == 0:
            projected[g], w_outer = flow.advance(projected[g], w_outer)
            flow.start("outer", links.gather(w_outer))
            attended, logs = attend(projected[g], g, attended)
            attended = flow.advance(attended)
            whole_groups.append(flow.take("group1"))
        else:
            projected[g] = flow.advance(projected[g])
            attended, logs = attend(projected[g], g, attended)
            attended = flow.advance(attended)
        lse.append(logs)
    whole_out = flow.take("out")
    unit_one, inverse_one, first_low = out_norm(attended, whole_out, tokens, vec)
    first_low = flow.advance(first_low)
    active, slope = inner_gelu(first_low, whole_inner, bias_inner)
    active = flow.advance(active)
    whole_outer = flow.take("outer")
    output, d_second, d_mid, sums_two = outer_norms(active, whole_outer, unit_one, vec, cotangent)

    grad_outer, d_mid = tie(gram(active, d_mid).astype(LOW), d_mid)
    flow.start("outer_back", links.reduce(grad_outer))
    d_pre, sum_inner = outer_back(d_mid, whole_outer, slope)
    d_pre = flow.advance(d_pre)
    grad_inner, d_pre = flow.advance(gram(first_low, d_pre).astype(LOW), d_pre)
    flow.start("inner_back", links.reduce(grad_inner))
    sums_one, before = jnp.zeros((8, D), FULL), []
    for part in range(2):
        *before, sums_one = inner_back(
            part, d_pre, whole_inner, d_second, unit_one, inverse_one, vec, whole_out, sums_one, before
        )
        before[0], sums_one = flow.advance(before[0], sums_one)
    d_inner, d_branch, d_attended = before
    grad_out, d_attended = tie(gram(attended, d_branch).astype(LOW), d_attended)
    flow.start("out_back", links.reduce(grad_out))

    d_groups, sums_group = [], []
    for g in range(GROUPS):
        d_group, sums = attend_back(projected[g], d_attended, lse[g], g)
        d_group, sums, d_attended = flow.advance(d_group, sums, d_attended)
        sums_group.append(sums)
        small = None
        if g == GROUPS - 1:
            arrays = [sums_one, sums_two, sum_inner] + sums_group
            spans = [[(3 + h, 0, place * WIDE, WIDE) for h in range(GROUPS)] for place in (0, 2)]
            spans += [[(i, row, 0, D)] for i, row in ((0, 2), (0, 0), (0, 1), (1, 2), (1, 0), (1, 1))]
            spans += [[(2, 0, 0, size * hidden)]]
            small = pack(arrays, spans, size)
        if ride and g == GROUPS - 1:
            small = jnp.pad(small, ((0, 0), (0, 3 * WIDE - used)))
            grad_group = product(tokens_turned, d_group, small, size)
        else:
            grad_group = product(tokens_turned, d_group)
        if g == 0:
            grad_group, d_attended = tie(grad_group, d_attended)
        else:
            grad_group, d_group = flow.advance(grad_group, d_group)
        flow.start(f"back{g}", links.reduce(grad_group))
        d_groups.append(d_group)
    d_tokens = flow.advance(tokens_back(d_inner, d_groups[0], whole_groups[0], FULL))
    d_tokens = flow.advance(tokens_back(d_tokens, d_groups[1], whole_groups[1], LOW))
    own_outer = flow.take("outer_back")
    own_inner = flow.take("inner_back")
    own_out = flow.take("out_back")
    own_groups = [flow.take(f"back{g}") for g in range(GROUPS)]
    if ride:
        last = own_groups[1]
        own_small = last[body]
        own_groups[1] = jnp.concatenate([last[:body], last[body + EXTRA : 2 * body + EXTRA]], axis=0)
    else:
        own_small = lax.psum_scatter(small, "shard", scatter_dimension=0)
        own_small = lax.psum(own_small, ("cross", "core"))

    def joined(parts, place):
        columns = slice(place * WIDE, (place + 1) * WIDE)
        return jnp.concatenate([part[..., columns] for part in parts], axis=-1)

    (
        own_bias_query,
        own_bias_value,
        own_bias_out,
        own_gain_one,
        own_shift_one,
        own_bias_outer,
        own_gain_two,
        own_shift_two,
    ) = (own_small[i * width : (i + 1) * width] for i in range(len(vectors)))
    own_bias_inner = own_small[used - hidden : used]
    return (
        output,
        d_tokens,
        joined(own_groups, 0),
        joined(own_groups, 1),
        joined(own_groups, 2),
        own_bias_query,
        own_bias_value,
        own_out,
        own_bias_out,
        own_gain_one,
        own_shift_one,
        own_inner,
        own_bias_inner,
        own_outer,
        own_bias_outer,
        own_gain_two,
        own_shift_two,
    )


def solution(mesh):
    reps, size = mesh.shape["rep"], mesh.shape["shard"]
    mesh = jax.sharding.Mesh(mesh.devices.reshape(reps // 2, 2, size), AXES)
    rows = P(AXES, None)
    matrix = P("shard", None)
    vector = P("shard")
    return jax.shard_map(
        functools.partial(shards, mesh),
        mesh=mesh,
        in_specs=(
            rows,
            matrix,
            matrix,
            matrix,
            vector,
            vector,
            matrix,
            vector,
            vector,
            vector,
            matrix,
            vector,
            matrix,
            vector,
            vector,
            vector,
            rows,
        ),
        out_specs=(
            rows,
            rows,
            matrix,
            matrix,
            matrix,
            vector,
            vector,
            matrix,
            vector,
            vector,
            vector,
            matrix,
            vector,
            matrix,
            vector,
            vector,
            vector,
        ),
        check_vma=False,
    )
```

```python
import functools

import jax
import jax.numpy as jnp
from jax import lax
from jax.experimental import pallas as pl
from jax.experimental.pallas import tpu as pltpu
from jax.sharding import PartitionSpec as P

D = 1024
H = 16
DH = 64
SEQ = 512
LANES = 128
GROUPS = 2
PAIRS = D // LANES // GROUPS
WIDE = D // GROUPS
AXES = ("cross", "core", "shard")
RING_MOST = 16
LOW = jnp.bfloat16
FULL = jnp.float32


def project(left, right):
    return jnp.dot(left, right, preferred_element_type=FULL)


def gram(left, right):
    return lax.dot_general(left, right, (((0,), (0,)), ((), ())), preferred_element_type=FULL)


def against(left, right):
    return lax.dot_general(left, right, (((1,), (1,)), ((), ())), preferred_element_type=FULL)


def normal(values):
    centre = values - jnp.mean(values, axis=-1, keepdims=True)
    spread = jnp.mean(centre * centre, axis=-1, keepdims=True)
    inverse = lax.rsqrt(spread + 1e-12)
    return centre * inverse, inverse


def normal_back(scaled, unit, inverse):
    mean = jnp.mean(scaled, axis=-1, keepdims=True)
    along = jnp.mean(scaled * unit, axis=-1, keepdims=True)
    return (scaled - mean - unit * along) * inverse


def head_mask(head):
    lane = lax.broadcasted_iota(jnp.int32, (SEQ, LANES), 1)
    return (lane // DH) == head


def attend_kernel(query_ref, key_ref, value_ref, *rest):
    out_ref, lse_ref = rest[-2:]
    query = query_ref[...] * LOW(0.125)
    key = key_ref[...]
    value_t = value_ref[...].T
    parts = []
    for head in range(LANES // DH):
        own = jnp.where(head_mask(head), query, jnp.zeros_like(query))
        scores = against(key, own)
        top = jnp.max(scores, axis=0, keepdims=True)
        expo = jnp.exp(scores - top)
        total = jnp.sum(expo, axis=0, keepdims=True)
        mixed = project(value_t[head * DH : (head + 1) * DH], expo.astype(LOW))
        parts.append(mixed * (1.0 / total))
        lse_ref[0, head : head + 1, :] = top + jnp.log(total)
    out_ref[...] = jnp.concatenate(parts, axis=0).T.astype(LOW)


def attend_back_kernel(query_ref, key_ref, value_ref, d_ref, lse_ref, out_ref, sum_ref):
    seq, pair = pl.program_id(0), pl.program_id(1)
    query = query_ref[...] * LOW(0.125)
    key = key_ref[...]
    value = value_ref[...]
    d_out = d_ref[...]
    key_t = key.T
    d_key = None
    d_value = None
    d_query = []
    for head in range(LANES // DH):
        mask = head_mask(head)
        own = jnp.where(mask, query, jnp.zeros_like(query))
        d_own = jnp.where(mask, d_out, jnp.zeros_like(d_out))
        probs = jnp.exp(against(key, own) - lse_ref[0, head : head + 1, :])
        d_probs = against(value, d_own)
        inner = jnp.sum(probs * d_probs, axis=0, keepdims=True)
        d_scores = (probs * (d_probs - inner)).astype(LOW)
        part_value = project(probs.astype(LOW), d_own)
        part_key = project(d_scores, own)
        d_value = part_value if d_value is None else d_value + part_value
        d_key = part_key if d_key is None else d_key + part_key
        d_query.append(project(key_t[head * DH : (head + 1) * DH], d_scores))
    d_query = jnp.concatenate(d_query, axis=0).T * 0.125
    for place, grad in enumerate((d_query, d_key, d_value)):
        start = pl.multiple_of(place * WIDE + pair * LANES, LANES)
        out_ref[:, pl.ds(start, LANES)] = grad.astype(LOW)
        total = jnp.sum(grad, axis=0, keepdims=True)
        before = sum_ref[0:1, pl.ds(start, LANES)]
        sum_ref[0:1, pl.ds(start, LANES)] = jnp.where(seq == 0, total, before + total)


def column_block(first):
    return pl.BlockSpec((SEQ, LANES), lambda seq, pair: (seq, first + pair))


LSE_BLOCK = pl.BlockSpec((1, LANES // DH, SEQ), lambda seq, pair: (seq * PAIRS + pair, 0, 0))


def triple():
    return [column_block(place * PAIRS) for place in range(3)]


def attend(qkv, group, before):
    count = qkv.shape[0]
    seqs = count // SEQ
    kept = [] if before is None else [before]
    return pl.pallas_call(
        attend_kernel,
        grid=(seqs, PAIRS),
        in_specs=triple() + [pl.BlockSpec(memory_space=pl.ANY)] * len(kept),
        out_specs=[column_block(group * PAIRS), LSE_BLOCK],
        out_shape=[
            jax.ShapeDtypeStruct((count, D), LOW),
            jax.ShapeDtypeStruct((seqs * PAIRS, LANES // DH, SEQ), FULL),
        ],
        input_output_aliases={3: 0} if kept else {},
        compiler_params=pltpu.CompilerParams(vmem_limit_bytes=32 * 2**20),
        name="attend",
    )(qkv, qkv, qkv, *kept)


def attend_back(qkv, d_attended, lse, group):
    count = qkv.shape[0]
    return pl.pallas_call(
        attend_back_kernel,
        grid=(count // SEQ, PAIRS),
        in_specs=triple() + [column_block(group * PAIRS), LSE_BLOCK],
        out_specs=[
            pl.BlockSpec((SEQ, 3 * WIDE), lambda seq, pair: (seq, 0)),
            pl.BlockSpec((8, 3 * WIDE), lambda seq, pair: (0, 0)),
        ],
        out_shape=[
            jax.ShapeDtypeStruct((count, 3 * WIDE), LOW),
            jax.ShapeDtypeStruct((8, 3 * WIDE), FULL),
        ],
        compiler_params=pltpu.CompilerParams(vmem_limit_bytes=40 * 2**20),
        name="attend_back",
    )(qkv, qkv, qkv, d_attended, lse)


ROWS = 256
COLUMNS = 512
EXTRA = 16
PARTS = 2
(QUERY, VALUE, OUT, GAIN_ONE, SHIFT_ONE, OUTER, GAIN_TWO, SHIFT_TWO) = range(8)


def line(ref, row):
    return ref[row : row + 1, :]


def kept(shape):
    return pl.BlockSpec(shape, lambda i: (0,) * len(shape), pipeline_mode=pl.Buffered(1))


def rows_of(width):
    return pl.BlockSpec((ROWS, width), lambda i: (i, 0))


def columns_of(height):
    return pl.BlockSpec((height, COLUMNS), lambda i: (0, i))


def add_line(ref, row, values):
    ref[row : row + 1, :] += jnp.sum(values, axis=0, keepdims=True)


def clear(ref):
    @pl.when(pl.program_id(0) == 0)
    def _():
        ref[...] = jnp.zeros_like(ref)


def pieces(rows, count=PARTS):
    step = rows // count
    return [slice(i * step, (i + 1) * step) for i in range(count)]


LIMIT = pltpu.CompilerParams(vmem_limit_bytes=48 * 2**20)


def out_kernel(attended_ref, w_ref, tokens_ref, vec_ref, unit_ref, inverse_ref, low_ref):
    for rows in pieces(ROWS):
        branch = project(attended_ref[rows, :], w_ref[...]) + line(vec_ref, OUT)
        unit, inverse = normal(tokens_ref[rows, :].astype(FULL) + branch)
        unit_ref[rows, :] = unit
        inverse_ref[rows, :] = jnp.broadcast_to(inverse, (inverse.shape[0], LANES))
        low_ref[rows, :] = (unit * line(vec_ref, GAIN_ONE) + line(vec_ref, SHIFT_ONE)).astype(LOW)


def out_norm(attended, w_out, tokens, vec):
    count = tokens.shape[0]
    return pl.pallas_call(
        out_kernel,
        grid=(count // ROWS,),
        in_specs=[rows_of(D), kept((D, D)), rows_of(D), kept((8, D))],
        out_specs=[rows_of(D), rows_of(LANES), rows_of(D)],
        out_shape=[
            jax.ShapeDtypeStruct((count, D), FULL),
            jax.ShapeDtypeStruct((count, LANES), FULL),
            jax.ShapeDtypeStruct((count, D), LOW),
        ],
        compiler_params=LIMIT,
        name="out_norm",
    )(attended, w_out, tokens, vec)


def inner_kernel(low_ref, w_ref, bias_ref, active_ref, slope_ref):
    for rows in pieces(low_ref.shape[0], 4):
        pre = project(low_ref[rows, :], w_ref[...]) + bias_ref[...]
        below = 0.5 * (1.0 + lax.erf(pre * (0.5**0.5)))
        active_ref[rows, :] = (pre * below).astype(LOW)
        slope_ref[rows, :] = (below + pre * jnp.exp(-0.5 * pre * pre) * 0.3989422804014327).astype(LOW)


def inner_gelu(low, w_inner, bias):
    count, hidden = low.shape[0], w_inner.shape[1]
    return pl.pallas_call(
        inner_kernel,
        grid=(hidden // COLUMNS,),
        in_specs=[kept((count, D)), columns_of(D), columns_of(1)],
        out_specs=[columns_of(count), columns_of(count)],
        out_shape=[jax.ShapeDtypeStruct((count, hidden), LOW)] * 2,
        compiler_params=LIMIT,
        name="inner_gelu",
    )(low, w_inner, bias)


def outer_kernel(active_ref, w_ref, unit_ref, vec_ref, cot_ref, out_ref, d_ref, d_low_ref, sum_ref):
    clear(sum_ref)
    for rows in pieces(ROWS):
        first = unit_ref[rows, :] * line(vec_ref, GAIN_ONE) + line(vec_ref, SHIFT_ONE)
        second = first + project(active_ref[rows, :], w_ref[...]) + line(vec_ref, OUTER)
        unit, inverse = normal(second)
        out_ref[rows, :] = (unit * line(vec_ref, GAIN_TWO) + line(vec_ref, SHIFT_TWO)).astype(LOW)
        cot = cot_ref[rows, :].astype(FULL)
        d_second = normal_back(cot * line(vec_ref, GAIN_TWO), unit, inverse)
        d_ref[rows, :] = d_second
        d_low_ref[rows, :] = d_second.astype(LOW)
        add_line(sum_ref, 0, cot * unit)
        add_line(sum_ref, 1, cot)
        add_line(sum_ref, 2, d_second)


def outer_norms(active, w_outer, unit, vec, cotangent):
    count, hidden = active.shape
    return pl.pallas_call(
        outer_kernel,
        grid=(count // ROWS,),
        in_specs=[rows_of(hidden), kept((hidden, D)), rows_of(D), kept((8, D)), rows_of(D)],
        out_specs=[rows_of(D), rows_of(D), rows_of(D), kept((8, D))],
        out_shape=[
            jax.ShapeDtypeStruct((count, D), LOW),
            jax.ShapeDtypeStruct((count, D), FULL),
            jax.ShapeDtypeStruct((count, D), LOW),
            jax.ShapeDtypeStruct((8, D), FULL),
        ],
        compiler_params=LIMIT,
        name="outer_norms",
    )(active, w_outer, unit, vec, cotangent)


def outer_back_kernel(d_ref, w_ref, slope_ref, out_ref, sum_ref):
    sum_ref[...] = jnp.zeros_like(sum_ref)
    for rows in pieces(d_ref.shape[0]):
        d_pre = against(d_ref[rows, :], w_ref[...]) * slope_ref[rows, :].astype(FULL)
        out_ref[rows, :] = d_pre.astype(LOW)
        add_line(sum_ref, 0, d_pre)


def outer_back(d_mid, w_outer, slope):
    count, hidden = slope.shape
    return pl.pallas_call(
        outer_back_kernel,
        grid=(hidden // COLUMNS,),
        in_specs=[kept((count, D)), pl.BlockSpec((COLUMNS, D), lambda i: (i, 0)), columns_of(count)],
        out_specs=[columns_of(count), columns_of(1)],
        out_shape=[
            jax.ShapeDtypeStruct((count, hidden), LOW),
            jax.ShapeDtypeStruct((1, hidden), FULL),
        ],
        compiler_params=LIMIT,
        name="outer_back",
    )(d_mid, w_outer, slope)


def inner_back_kernel(
    d_pre_ref, w_ref, d_ref, unit_ref, inverse_ref, vec_ref, w_out_ref, before_ref, *refs
):
    out_ref, low_ref, attended_ref, sum_ref, total_ref = refs[-5:]
    step = pl.program_id(0)
    part = against(d_pre_ref[...], w_ref[...])

    @pl.when(step == 0)
    def _():
        total_ref[...] = d_ref[...] + part

    @pl.when(step > 0)
    def _():
        total_ref[...] += part

    @pl.when(step == pl.num_programs(0) - 1)
    def _():
        sum_ref[...] = before_ref[...]
        for rows in pieces(total_ref.shape[0], 2):
            d_first = total_ref[rows, :]
            unit = unit_ref[rows, :]
            d_inner = normal_back(d_first * line(vec_ref, GAIN_ONE), unit, inverse_ref[rows, 0:1])
            low = d_inner.astype(LOW)
            out_ref[rows, :] = d_inner
            low_ref[rows, :] = low
            attended_ref[rows, :] = against(low, w_out_ref[...]).astype(LOW)
            add_line(sum_ref, 0, d_first * unit)
            add_line(sum_ref, 1, d_first)
            add_line(sum_ref, 2, d_inner)


def inner_back(part, d_pre, w_inner, d_second, unit, inverse, vec, w_out, sums, before):
    count, hidden = d_pre.shape
    rows = count // 2

    def own(width):
        return pl.BlockSpec((rows, width), lambda i: (part, 0), pipeline_mode=pl.Buffered(1))

    return pl.pallas_call(
        inner_back_kernel,
        grid=(hidden // COLUMNS,),
        in_specs=[
            pl.BlockSpec((rows, COLUMNS), lambda i: (part, i)),
            columns_of(D),
            own(D),
            own(D),
            own(LANES),
            kept((8, D)),
            kept((D, D)),
            kept((8, D)),
        ]
        + [pl.BlockSpec(memory_space=pl.ANY)] * len(before),
        out_specs=[own(D), own(D), own(D), kept((8, D))],
        out_shape=[
            jax.ShapeDtypeStruct((count, D), FULL),
            jax.ShapeDtypeStruct((count, D), LOW),
            jax.ShapeDtypeStruct((count, D), LOW),
            jax.ShapeDtypeStruct((8, D), FULL),
        ],
        input_output_aliases={8 + i: i for i in range(len(before))},
        scratch_shapes=[pltpu.VMEM((rows, D), FULL)],
        compiler_params=LIMIT,
        name="inner_back",
    )(d_pre, w_inner, d_second, unit, inverse, vec, w_out, sums, *before)


def tokens_kernel(base_ref, d_ref, w_ref, out_ref):
    out_ref[...] = (base_ref[...] + against(d_ref[...], w_ref[...])).astype(out_ref.dtype)


def tokens_back(base, d_group, w_group, kind):
    count, wide = d_group.shape
    rows = count // 2
    return pl.pallas_call(
        tokens_kernel,
        grid=(2,),
        in_specs=[
            pl.BlockSpec((rows, D), lambda i: (i, 0)),
            pl.BlockSpec((rows, wide), lambda i: (i, 0)),
            kept((D, wide)),
        ],
        out_specs=pl.BlockSpec((rows, D), lambda i: (i, 0)),
        out_shape=jax.ShapeDtypeStruct((count, D), kind),
        compiler_params=LIMIT,
        name="tokens_back",
    )(base, d_group, w_group)


def turn_kernel(ref, out_ref):
    out_ref[...] = ref[...].T


def turn(values):
    count, width = values.shape
    return pl.pallas_call(
        turn_kernel,
        grid=(count // ROWS,),
        in_specs=[rows_of(width)],
        out_specs=pl.BlockSpec((width, ROWS), lambda i: (0, i)),
        out_shape=jax.ShapeDtypeStruct((width, count), values.dtype),
        name="turn",
    )(values)


def product_kernel(left_ref, right_ref, out_ref):
    out_ref[...] = project(left_ref[...], right_ref[...]).astype(LOW)


def product_extra_kernel(size, left_ref, right_ref, small_ref, out_ref):
    found = project(left_ref[...], right_ref[...]).astype(LOW)
    body = found.shape[0] // size // 2
    for shard in range(size):
        extra = jnp.broadcast_to(small_ref[shard : shard + 1, :], (EXTRA, found.shape[1])).astype(LOW)
        for core in range(2):
            half = 2 * shard + core
            at = half * (body + EXTRA)
            out_ref[at : at + body, :] = found[half * body : (half + 1) * body]
            out_ref[at + body : at + body + EXTRA, :] = extra


def product(left, right, small=None, size=1):
    height, depth = left.shape
    rows = height if small is None else height + 2 * EXTRA * size
    return pl.pallas_call(
        product_kernel if small is None else functools.partial(product_extra_kernel, size),
        grid=(right.shape[1] // COLUMNS,),
        in_specs=[kept((height, depth)), columns_of(depth)] + ([] if small is None else [columns_of(size)]),
        out_specs=columns_of(rows),
        out_shape=jax.ShapeDtypeStruct((rows, right.shape[1]), LOW),
        compiler_params=LIMIT,
        name="product",
    )(left, right, *([] if small is None else [small]))


def assemble_kernel(moves, align, place_ref, *refs):
    out_ref, sems = refs[-2], refs[-1]
    copies = []
    for i, (which, start, rows) in enumerate(moves):
        place = pl.multiple_of(place_ref[i], align)
        source = refs[which].at[pl.ds(start, rows)]
        copies.append(pltpu.make_async_copy(source, out_ref.at[pl.ds(place, rows)], sems.at[i]))
    for copy in copies:
        copy.start()
    for copy in copies:
        copy.wait()


def assemble(arrays, moves, places, rows):
    align = min(move[2] for move in moves)
    return pl.pallas_call(
        functools.partial(assemble_kernel, moves, align),
        in_specs=[pl.BlockSpec(memory_space=pltpu.SMEM)] + [pl.BlockSpec(memory_space=pl.ANY)] * len(arrays),
        out_specs=pl.BlockSpec(memory_space=pltpu.VMEM),
        out_shape=jax.ShapeDtypeStruct((rows,) + arrays[0].shape[1:], arrays[0].dtype),
        scratch_shapes=[pltpu.SemaphoreType.DMA((len(moves),))],
        compiler_params=pltpu.CompilerParams(vmem_limit_bytes=24 * 2**20),
        name="assemble",
    )(jnp.stack(places).astype(jnp.int32), *arrays)


def pack_kernel(size, vectors, *refs):
    out_ref = refs[-1]
    for shard in range(size):
        at = 0
        for spans in vectors:
            lines = []
            for which, row, first, length in spans:
                lines += [(which, row, first + i) for i in range(0, length, LANES)]
            share = len(lines) // size
            for which, row, first in lines[shard * share : (shard + 1) * share]:
                out_ref[shard : shard + 1, at : at + LANES] = refs[which][row : row + 1, first : first + LANES]
                at += LANES


def pack(arrays, vectors, size):
    lengths = [sum(span[3] for span in spans) for spans in vectors]
    if any(length % (size * LANES) for length in lengths):
        whole = [
            jnp.concatenate([arrays[which][row, first : first + length] for which, row, first, length in spans])
            for spans in vectors
        ]
        return jnp.concatenate([vector.reshape(size, -1) for vector in whole], axis=1)
    return pl.pallas_call(
        functools.partial(pack_kernel, size, vectors),
        out_shape=jax.ShapeDtypeStruct((size, sum(lengths) // size), FULL),
        name="pack",
    )(*arrays)


def lay_kernel(*refs):
    row = jnp.concatenate([ref[...].astype(FULL) for ref in refs[:-1]], axis=1)
    refs[-1][...] = jnp.broadcast_to(row, refs[-1].shape).astype(LOW)


def lay(vectors):
    total = sum(vector.shape[1] for vector in vectors)
    return pl.pallas_call(
        lay_kernel,
        out_shape=jax.ShapeDtypeStruct((EXTRA, total), LOW),
        name="lay",
    )(*vectors)


def unpack_kernel(count, body, place_ref, *refs):
    vec_ref, bias_ref, group_ref = refs[count:]
    group_ref[...] = jnp.zeros_like(group_ref)
    hidden = bias_ref.shape[1] // count
    for i in range(count):
        packed = refs[i][body : body + EXTRA, :].astype(FULL)[0:1, :]
        owner = place_ref[i]
        start = pl.multiple_of(owner * LANES, LANES)
        for row in range(8):
            vec_ref[row : row + 1, pl.ds(start, LANES)] = packed[:, row * LANES : (row + 1) * LANES]
        first = pl.multiple_of(owner * hidden, LANES)
        bias_ref[:, pl.ds(first, hidden)] = packed[:, 8 * LANES : 8 * LANES + hidden]
        group = owner * LANES // WIDE
        for place, row in ((0, QUERY), (2, VALUE)):
            first = pl.multiple_of(group * 2 * WIDE + place * WIDE + start, LANES)
            group_ref[:, pl.ds(first, LANES)] = packed[:, row * LANES : (row + 1) * LANES]


def unpack(chunks, owners, body, hidden):
    count = len(chunks)
    return pl.pallas_call(
        functools.partial(unpack_kernel, count, body),
        in_specs=[pl.BlockSpec(memory_space=pltpu.SMEM)] + [pl.BlockSpec(memory_space=pltpu.VMEM)] * count,
        out_shape=[
            jax.ShapeDtypeStruct((8, D), FULL),
            jax.ShapeDtypeStruct((1, hidden), FULL),
            jax.ShapeDtypeStruct((1, 3 * D), FULL),
        ],
        compiler_params=LIMIT,
        name="unpack",
    )(jnp.stack(owners).astype(jnp.int32), *chunks)


def tie(*values):
    return lax.optimization_barrier(values)


class Links:
    def __init__(self, mesh):
        self.reps, self.size = mesh.shape["cross"] * mesh.shape["core"], mesh.shape["shard"]
        size = self.size
        self.direct = size > RING_MOST or size % 2 == 1
        self.order = list(range(0, size, 2)) + list(range(size - 1, 0, -2))
        self.far = size // 2
        self.near = size - 1 - self.far
        shard = lax.axis_index("shard")
        self.core = lax.axis_index("core")
        self.sign = 1 - 2 * self.core
        self.place = jnp.where(shard % 2 == 0, shard // 2, size - 1 - shard // 2)

    def owner(self, step):
        place = (self.place + self.sign * step + 2 * self.size) % self.size
        return jnp.where(place < self.size // 2, 2 * place, 2 * (self.size - place) - 1)

    def hop(self, values, sign):
        pairs = []
        for rep in range(self.reps):
            turn = sign if rep % 2 == 0 else -sign
            for i, shard in enumerate(self.order):
                target = self.order[(i + turn) % self.size]
                pairs.append((rep * self.size + shard, rep * self.size + target))
        return lax.ppermute(values, AXES, pairs)

    def swap(self, values, bit):
        pairs = []
        for rep in range(self.reps):
            for shard in range(self.size):
                pairs.append((rep * self.size + shard, (rep ^ bit) * self.size + shard))
        return lax.ppermute(values, AXES, pairs)

    def half_of(self, values):
        half = values.shape[0] // 2
        return lax.dynamic_slice_in_dim(values, self.core * half, half, axis=0)


    def vectors(self, packed, hidden):
        small = lax.all_gather(packed, "shard", axis=0).astype(FULL)
        width, share = D // self.size, hidden // self.size
        vec = small[:, : 8 * width].reshape(self.size, 8, width).swapaxes(0, 1).reshape(8, D)
        bias = small[:, 8 * width : 8 * width + share].reshape(1, hidden)
        none = jnp.zeros((WIDE,), FULL)
        spans = [slice(g * WIDE, (g + 1) * WIDE) for g in range(GROUPS)]
        parts = [part for span in spans for part in (vec[QUERY, span], none, vec[VALUE, span])]
        return vec, bias, jnp.concatenate(parts).reshape(1, 3 * D)

    def half_of(self, values):
        half = values.shape[0] // 2
        return lax.dynamic_slice_in_dim(values, self.core * half, half, axis=0)

    def gather(self, values, sent=None):
        if self.direct:
            return lax.all_gather(values, "shard", axis=0, tiled=True)
        rows = values.shape[0]
        body = rows // 2
        arrays = [values]
        moves = [(0, 0, rows)]
        places = [self.owner(0) * rows]
        chunks, owners = [sent], [self.owner(0)]

        def keep(chunk, mine, step):
            moves.append((len(arrays), 0, body))
            arrays.append(chunk)
            core = self.core if mine else 1 - self.core
            places.append(self.owner(step) * rows + core * body)
            if mine:
                chunks.append(chunk)
                owners.append(self.owner(step))

        ahead = back = self.half_of(values) if sent is None else sent
        for step in range(1, self.far + 2):
            flight = []
            if step > 1:
                keep(ahead, True, 1 - step)
                flight.append((self.swap(ahead, 1), step - 1))
                if step - 1 <= self.near:
                    keep(back, True, step - 1)
                    flight.append((self.swap(back, 1), 1 - step))
            if step <= self.far:
                ahead = self.hop(ahead, 1)
            if step <= self.near:
                back = self.hop(back, -1)
            ahead, back, *swapped = yield [ahead, back] + [chunk for chunk, _ in flight]
            for chunk, (_, place) in zip(swapped, flight):
                keep(chunk, False, place)
        whole = assemble(arrays, moves, places, self.size * rows)
        return whole if sent is None else (whole, chunks, owners)

    def gather_quarters(self, values):
        rows = values.shape[0] // self.reps
        index = lax.axis_index("cross") * 2 + self.core
        mine = lax.dynamic_slice_in_dim(values, index * rows, rows, axis=0)
        return lax.all_gather(mine, ("shard", "cross", "core"), axis=0, tiled=True)

    def finish(self, total):
        (cross,) = yield [self.swap(total, 2)]
        total = (total.astype(FULL) + cross.astype(FULL)).astype(LOW)
        (pair,) = yield [self.swap(total, 1)]
        low = jnp.where(self.core == 0, total, pair)
        high = jnp.where(self.core == 0, pair, total)
        return jnp.concatenate([low, high], axis=0).astype(FULL)

    def reduce(self, values):
        if self.direct:
            own = lax.psum_scatter(values, "shard", scatter_dimension=0, tiled=True)
            return lax.psum(own, ("cross", "core")).astype(FULL)
        width = values.shape[1]
        half = values.shape[0] // self.size // 2
        split = values.reshape(self.size, 2, half, width)
        other = self.swap(lax.dynamic_index_in_dim(split, 1 - self.core, axis=1, keepdims=False), 1)
        (other,) = yield [other]

        def piece(step):
            owner = self.owner(step)
            own = lax.dynamic_slice(split, (owner, self.core, 0, 0), (1, 1, half, width))
            pair = lax.dynamic_slice(other, (owner, 0, 0), (1, half, width))
            return own[0, 0].astype(FULL) + pair[0].astype(FULL)

        ahead = piece(self.far).astype(LOW)
        back = piece(-self.near).astype(LOW)
        for step in range(self.far - 1, -1, -1):
            moving = [self.hop(ahead, 1)]
            if step < self.near:
                moving.append(self.hop(back, -1))
            ahead, *rest = yield moving
            if step > 0:
                ahead = (ahead.astype(FULL) + piece(step)).astype(LOW)
            if rest:
                back = rest[0]
                if step > 0:
                    back = (back.astype(FULL) + piece(-step)).astype(LOW)
        total = (piece(0) + ahead.astype(FULL) + back.astype(FULL)).astype(LOW)
        return (yield from self.finish(total))


class Flow:
    def __init__(self):
        self.running = {}
        self.results = {}

    def start(self, name, steps):
        self._move(name, steps, None)

    def _move(self, name, steps, values):
        try:
            self.running[name] = (steps, steps.send(values))
        except StopIteration as end:
            self.running.pop(name, None)
            self.results[name] = end.value

    def advance(self, *values, near=None):
        running = [item for item in self.running.items() if near is None or item[0] in near]
        flat = list(values)
        for _, (_, flight) in running:
            flat += flight
        tied = tie(*flat) if flat else ()
        at = len(values)
        for name, (steps, flight) in running:
            self._move(name, steps, list(tied[at : at + len(flight)]))
            at += len(flight)
        return tied[0] if len(values) == 1 else tuple(tied[: len(values)])

    def take(self, name):
        while name in self.running:
            steps, flight = self.running[name]
            self._move(name, steps, flight)
        return self.results[name]


def shards(
    mesh,
    tokens,
    w_query,
    w_key,
    w_value,
    b_query,
    b_value,
    w_out,
    b_out,
    gain_one,
    shift_one,
    w_inner,
    b_inner,
    w_outer,
    b_outer,
    gain_two,
    shift_two,
    cotangent,
):
    links = Links(mesh)
    size = links.size
    width = D // size
    hidden = b_inner.shape[0]

    own_groups = [
        jnp.concatenate([w[:, g * WIDE : (g + 1) * WIDE] for w in (w_query, w_key, w_value)], axis=1)
        for g in range(GROUPS)
    ]
    vectors = (b_query, b_value, b_out, gain_one, shift_one, b_outer, gain_two, shift_two)
    used = len(vectors) * width + hidden
    ride = not links.direct and used <= 3 * WIDE and width == LANES
    rows_in = [v.reshape(1, -1) for v in vectors + (b_inner,)]
    packed = jnp.concatenate(rows_in, axis=1)
    sent = None
    if ride:
        extra = jnp.pad(lay(rows_in), ((0, 0), (0, 3 * WIDE - used)))
        halves = [links.half_of(w[:, :WIDE]) for w in (w_query, w_key, w_value)]
        sent = jnp.concatenate([jnp.concatenate(halves, axis=1), extra], axis=0)
        sent, w_inner, w_outer = tie(sent, w_inner, w_outer)
    flow = Flow()
    flow.start("group0", links.gather(own_groups[0], sent))
    whole_inner = links.gather_quarters(w_inner)
    whole_outer = links.gather_quarters(w_outer)
    flow.advance()
    own_groups[1] = flow.advance(own_groups[1])
    flow.start("group1", links.gather(own_groups[1]))
    tokens_turned, w_out = flow.advance(turn(tokens), w_out)
    flow.start("out", links.gather(w_out))
    flow.advance()
    if ride:
        first_group, chunks, owners = flow.take("group0")
        vec, bias_inner, bias_groups = unpack(chunks, owners, width // 2, size * hidden)
    else:
        first_group = flow.take("group0")
        vec, bias_inner, bias_groups = links.vectors(packed[0], size * hidden)
    whole_groups = [first_group]

    projected = []
    attended, lse = None, []
    for g in range(GROUPS):
        bias = bias_groups[:, g * 3 * WIDE : (g + 1) * 3 * WIDE]
        projected.append((project(tokens, whole_groups[g]) + bias).astype(LOW))
        if g == 0:
            projected[g] = flow.advance(projected[g])
            attended, logs = attend(projected[g], g, attended)
            attended = flow.advance(attended)
            whole_groups.append(flow.take("group1"))
        else:
            projected[g] = flow.advance(projected[g])
            attended, logs = attend(projected[g], g, attended)
            attended = flow.advance(attended)
        lse.append(logs)
    whole_out = flow.take("out")
    unit_one, inverse_one, first_low = out_norm(attended, whole_out, tokens, vec)
    active, slope = inner_gelu(first_low, whole_inner, bias_inner)
    output, d_second, d_mid, sums_two = outer_norms(active, whole_outer, unit_one, vec, cotangent)

    grad_outer, d_mid = tie(gram(active, d_mid).astype(LOW), d_mid)
    flow.start("outer_back", links.reduce(grad_outer))
    d_pre, sum_inner = outer_back(d_mid, whole_outer, slope)
    d_pre = flow.advance(d_pre)
    grad_inner, d_pre = flow.advance(gram(first_low, d_pre).astype(LOW), d_pre)
    flow.start("inner_back", links.reduce(grad_inner))
    sums_one, before = jnp.zeros((8, D), FULL), []
    for part in range(2):
        *before, sums_one = inner_back(
            part, d_pre, whole_inner, d_second, unit_one, inverse_one, vec, whole_out, sums_one, before
        )
        before[0], sums_one = flow.advance(before[0], sums_one)
    d_inner, d_branch, d_attended = before
    grad_out, d_attended = tie(gram(attended, d_branch).astype(LOW), d_attended)

    d_groups, sums_group = [], []
    for g in range(GROUPS):
        d_group, sums = attend_back(projected[g], d_attended, lse[g], g)
        d_group, sums, d_attended = flow.advance(d_group, sums, d_attended)
        sums_group.append(sums)
        small = None
        if g == GROUPS - 1:
            arrays = [sums_one, sums_two, sum_inner] + sums_group
            spans = [[(3 + h, 0, place * WIDE, WIDE) for h in range(GROUPS)] for place in (0, 2)]
            spans += [[(i, row, 0, D)] for i, row in ((0, 2), (0, 0), (0, 1), (1, 2), (1, 0), (1, 1))]
            spans += [[(2, 0, 0, size * hidden)]]
            small = pack(arrays, spans, size)
        if ride and g == GROUPS - 1:
            small = jnp.pad(small, ((0, 0), (0, 3 * WIDE - used)))
            grad_group = product(tokens_turned, d_group, small, size)
        else:
            grad_group = product(tokens_turned, d_group)
        if g == 0:
            grad_group = jnp.concatenate([grad_group, grad_out], axis=1)
            grad_group, d_attended = tie(grad_group, d_attended)
        else:
            grad_group, d_group = flow.advance(grad_group, d_group)
        flow.start(f"back{g}", links.reduce(grad_group))
        d_groups.append(d_group)
    d_tokens = flow.advance(tokens_back(d_inner, d_groups[0], whole_groups[0], FULL))
    d_tokens = flow.advance(tokens_back(d_tokens, d_groups[1], whole_groups[1], LOW))
    own_outer = flow.take("outer_back")
    own_inner = flow.take("inner_back")
    own_groups = [flow.take(f"back{g}") for g in range(GROUPS)]
    own_out = own_groups[0][:, 3 * WIDE :]
    if ride:
        body = width // 2
        last = own_groups[1]
        own_small = last[body]
        own_groups[1] = jnp.concatenate([last[:body], last[body + EXTRA : 2 * body + EXTRA]], axis=0)
    else:
        own_small = lax.psum_scatter(small, "shard", scatter_dimension=0)
        own_small = lax.psum(own_small, ("cross", "core"))

    def joined(parts, place):
        columns = slice(place * WIDE, (place + 1) * WIDE)
        return jnp.concatenate([part[..., columns] for part in parts], axis=-1)

    (
        own_bias_query,
        own_bias_value,
        own_bias_out,
        own_gain_one,
        own_shift_one,
        own_bias_outer,
        own_gain_two,
        own_shift_two,
    ) = (own_small[i * width : (i + 1) * width] for i in range(len(vectors)))
    own_bias_inner = own_small[used - hidden : used]
    return (
        output,
        d_tokens,
        joined(own_groups, 0),
        joined(own_groups, 1),
        joined(own_groups, 2),
        own_bias_query,
        own_bias_value,
        own_out,
        own_bias_out,
        own_gain_one,
        own_shift_one,
        own_inner,
        own_bias_inner,
        own_outer,
        own_bias_outer,
        own_gain_two,
        own_shift_two,
    )


def solution(mesh):
    reps, size = mesh.shape["rep"], mesh.shape["shard"]
    mesh = jax.sharding.Mesh(mesh.devices.reshape(reps // 2, 2, size), AXES)
    rows = P(AXES, None)
    matrix = P("shard", None)
    vector = P("shard")
    return jax.shard_map(
        functools.partial(shards, mesh),
        mesh=mesh,
        in_specs=(
            rows,
            matrix,
            matrix,
            matrix,
            vector,
            vector,
            matrix,
            vector,
            vector,
            vector,
            matrix,
            vector,
            matrix,
            vector,
            vector,
            vector,
            rows,
        ),
        out_specs=(
            rows,
            rows,
            matrix,
            matrix,
            matrix,
            vector,
            vector,
            matrix,
            vector,
            vector,
            vector,
            matrix,
            vector,
            matrix,
            vector,
            vector,
            vector,
        ),
        check_vma=False,
    )
```

```python
import functools

import jax
import jax.numpy as jnp
from jax import lax
from jax.experimental import pallas as pl
from jax.experimental.pallas import tpu as pltpu
from jax.sharding import PartitionSpec as P

D = 1024
H = 16
DH = 64
SEQ = 512
LANES = 128
GROUPS = 2
PAIRS = D // LANES // GROUPS
WIDE = D // GROUPS
AXES = ("cross", "core", "shard")
RING_MOST = 16
LOW = jnp.bfloat16
FULL = jnp.float32


def project(left, right):
    return jnp.dot(left, right, preferred_element_type=FULL)


def gram(left, right):
    return lax.dot_general(left, right, (((0,), (0,)), ((), ())), preferred_element_type=FULL)


def against(left, right):
    return lax.dot_general(left, right, (((1,), (1,)), ((), ())), preferred_element_type=FULL)


def normal(values):
    centre = values - jnp.mean(values, axis=-1, keepdims=True)
    spread = jnp.mean(centre * centre, axis=-1, keepdims=True)
    inverse = lax.rsqrt(spread + 1e-12)
    return centre * inverse, inverse


def normal_back(scaled, unit, inverse):
    mean = jnp.mean(scaled, axis=-1, keepdims=True)
    along = jnp.mean(scaled * unit, axis=-1, keepdims=True)
    return (scaled - mean - unit * along) * inverse


def head_mask(head):
    lane = lax.broadcasted_iota(jnp.int32, (SEQ, LANES), 1)
    return (lane // DH) == head


def attend_kernel(query_ref, key_ref, value_ref, *rest):
    out_ref, lse_ref = rest[-2:]
    query = query_ref[...] * LOW(0.125)
    key = key_ref[...]
    value_t = value_ref[...].T
    parts = []
    for head in range(LANES // DH):
        own = jnp.where(head_mask(head), query, jnp.zeros_like(query))
        scores = against(key, own)
        top = jnp.max(scores, axis=0, keepdims=True)
        expo = jnp.exp(scores - top)
        total = jnp.sum(expo, axis=0, keepdims=True)
        mixed = project(value_t[head * DH : (head + 1) * DH], expo.astype(LOW))
        parts.append(mixed * (1.0 / total))
        lse_ref[0, head : head + 1, :] = top + jnp.log(total)
    out_ref[...] = jnp.concatenate(parts, axis=0).T.astype(LOW)


def attend_back_kernel(query_ref, key_ref, value_ref, d_ref, lse_ref, out_ref, sum_ref):
    seq, pair = pl.program_id(0), pl.program_id(1)
    query = query_ref[...] * LOW(0.125)
    key = key_ref[...]
    value = value_ref[...]
    d_out = d_ref[...]
    key_t = key.T
    d_key = None
    d_value = None
    d_query = []
    for head in range(LANES // DH):
        mask = head_mask(head)
        own = jnp.where(mask, query, jnp.zeros_like(query))
        d_own = jnp.where(mask, d_out, jnp.zeros_like(d_out))
        probs = jnp.exp(against(key, own) - lse_ref[0, head : head + 1, :])
        d_probs = against(value, d_own)
        inner = jnp.sum(probs * d_probs, axis=0, keepdims=True)
        d_scores = (probs * (d_probs - inner)).astype(LOW)
        part_value = project(probs.astype(LOW), d_own)
        part_key = project(d_scores, own)
        d_value = part_value if d_value is None else d_value + part_value
        d_key = part_key if d_key is None else d_key + part_key
        d_query.append(project(key_t[head * DH : (head + 1) * DH], d_scores))
    d_query = jnp.concatenate(d_query, axis=0).T * 0.125
    for place, grad in enumerate((d_query, d_key, d_value)):
        start = pl.multiple_of(place * WIDE + pair * LANES, LANES)
        out_ref[:, pl.ds(start, LANES)] = grad.astype(LOW)
        total = jnp.sum(grad, axis=0, keepdims=True)
        before = sum_ref[0:1, pl.ds(start, LANES)]
        sum_ref[0:1, pl.ds(start, LANES)] = jnp.where(seq == 0, total, before + total)


def column_block(first):
    return pl.BlockSpec((SEQ, LANES), lambda seq, pair: (seq, first + pair))


LSE_BLOCK = pl.BlockSpec((1, LANES // DH, SEQ), lambda seq, pair: (seq * PAIRS + pair, 0, 0))


def triple():
    return [column_block(place * PAIRS) for place in range(3)]


def attend(qkv, group, before):
    count = qkv.shape[0]
    seqs = count // SEQ
    kept = [] if before is None else [before]
    return pl.pallas_call(
        attend_kernel,
        grid=(seqs, PAIRS),
        in_specs=triple() + [pl.BlockSpec(memory_space=pl.ANY)] * len(kept),
        out_specs=[column_block(group * PAIRS), LSE_BLOCK],
        out_shape=[
            jax.ShapeDtypeStruct((count, D), LOW),
            jax.ShapeDtypeStruct((seqs * PAIRS, LANES // DH, SEQ), FULL),
        ],
        input_output_aliases={3: 0} if kept else {},
        compiler_params=pltpu.CompilerParams(vmem_limit_bytes=32 * 2**20),
        name="attend",
    )(qkv, qkv, qkv, *kept)


def attend_back(qkv, d_attended, lse, group):
    count = qkv.shape[0]
    return pl.pallas_call(
        attend_back_kernel,
        grid=(count // SEQ, PAIRS),
        in_specs=triple() + [column_block(group * PAIRS), LSE_BLOCK],
        out_specs=[
            pl.BlockSpec((SEQ, 3 * WIDE), lambda seq, pair: (seq, 0)),
            pl.BlockSpec((8, 3 * WIDE), lambda seq, pair: (0, 0)),
        ],
        out_shape=[
            jax.ShapeDtypeStruct((count, 3 * WIDE), LOW),
            jax.ShapeDtypeStruct((8, 3 * WIDE), FULL),
        ],
        compiler_params=pltpu.CompilerParams(vmem_limit_bytes=40 * 2**20),
        name="attend_back",
    )(qkv, qkv, qkv, d_attended, lse)


ROWS = 512
COLUMNS = 512
EXTRA = 16
PARTS = 2
(QUERY, VALUE, OUT, GAIN_ONE, SHIFT_ONE, OUTER, GAIN_TWO, SHIFT_TWO) = range(8)


def line(ref, row):
    return ref[row : row + 1, :]


def kept(shape):
    return pl.BlockSpec(shape, lambda i: (0,) * len(shape), pipeline_mode=pl.Buffered(1))


def rows_of(width):
    return pl.BlockSpec((ROWS, width), lambda i: (i, 0))


def columns_of(height):
    return pl.BlockSpec((height, COLUMNS), lambda i: (0, i))


def add_line(ref, row, values):
    ref[row : row + 1, :] += jnp.sum(values, axis=0, keepdims=True)


def clear(ref):
    @pl.when(pl.program_id(0) == 0)
    def _():
        ref[...] = jnp.zeros_like(ref)


def pieces(rows, count=PARTS):
    step = rows // count
    return [slice(i * step, (i + 1) * step) for i in range(count)]


LIMIT = pltpu.CompilerParams(vmem_limit_bytes=48 * 2**20)


def out_kernel(attended_ref, w_ref, tokens_ref, vec_ref, unit_ref, inverse_ref, low_ref):
    for rows in pieces(ROWS):
        branch = project(attended_ref[rows, :], w_ref[...]) + line(vec_ref, OUT)
        unit, inverse = normal(tokens_ref[rows, :].astype(FULL) + branch)
        unit_ref[rows, :] = unit
        inverse_ref[rows, :] = jnp.broadcast_to(inverse, (inverse.shape[0], LANES))
        low_ref[rows, :] = (unit * line(vec_ref, GAIN_ONE) + line(vec_ref, SHIFT_ONE)).astype(LOW)


def out_norm(attended, w_out, tokens, vec):
    count = tokens.shape[0]
    return pl.pallas_call(
        out_kernel,
        grid=(count // ROWS,),
        in_specs=[rows_of(D), kept((D, D)), rows_of(D), kept((8, D))],
        out_specs=[rows_of(D), rows_of(LANES), rows_of(D)],
        out_shape=[
            jax.ShapeDtypeStruct((count, D), FULL),
            jax.ShapeDtypeStruct((count, LANES), FULL),
            jax.ShapeDtypeStruct((count, D), LOW),
        ],
        compiler_params=LIMIT,
        name="out_norm",
    )(attended, w_out, tokens, vec)


def inner_kernel(low_ref, w_ref, bias_ref, active_ref, slope_ref):
    for rows in pieces(low_ref.shape[0], 4):
        pre = project(low_ref[rows, :], w_ref[...]) + bias_ref[...]
        below = 0.5 * (1.0 + lax.erf(pre * (0.5**0.5)))
        active_ref[rows, :] = (pre * below).astype(LOW)
        slope_ref[rows, :] = (below + pre * jnp.exp(-0.5 * pre * pre) * 0.3989422804014327).astype(LOW)


def inner_gelu(low, w_inner, bias):
    count, hidden = low.shape[0], w_inner.shape[1]
    return pl.pallas_call(
        inner_kernel,
        grid=(hidden // COLUMNS,),
        in_specs=[kept((count, D)), columns_of(D), columns_of(1)],
        out_specs=[columns_of(count), columns_of(count)],
        out_shape=[jax.ShapeDtypeStruct((count, hidden), LOW)] * 2,
        compiler_params=LIMIT,
        name="inner_gelu",
    )(low, w_inner, bias)


def outer_kernel(active_ref, w_ref, unit_ref, vec_ref, cot_ref, out_ref, d_ref, d_low_ref, sum_ref):
    clear(sum_ref)
    for rows in pieces(ROWS):
        first = unit_ref[rows, :] * line(vec_ref, GAIN_ONE) + line(vec_ref, SHIFT_ONE)
        second = first + project(active_ref[rows, :], w_ref[...]) + line(vec_ref, OUTER)
        unit, inverse = normal(second)
        out_ref[rows, :] = (unit * line(vec_ref, GAIN_TWO) + line(vec_ref, SHIFT_TWO)).astype(LOW)
        cot = cot_ref[rows, :].astype(FULL)
        d_second = normal_back(cot * line(vec_ref, GAIN_TWO), unit, inverse)
        d_ref[rows, :] = d_second
        d_low_ref[rows, :] = d_second.astype(LOW)
        add_line(sum_ref, 0, cot * unit)
        add_line(sum_ref, 1, cot)
        add_line(sum_ref, 2, d_second)


def outer_norms(active, w_outer, unit, vec, cotangent):
    count, hidden = active.shape
    return pl.pallas_call(
        outer_kernel,
        grid=(count // ROWS,),
        in_specs=[rows_of(hidden), kept((hidden, D)), rows_of(D), kept((8, D)), rows_of(D)],
        out_specs=[rows_of(D), rows_of(D), rows_of(D), kept((8, D))],
        out_shape=[
            jax.ShapeDtypeStruct((count, D), LOW),
            jax.ShapeDtypeStruct((count, D), FULL),
            jax.ShapeDtypeStruct((count, D), LOW),
            jax.ShapeDtypeStruct((8, D), FULL),
        ],
        compiler_params=LIMIT,
        name="outer_norms",
    )(active, w_outer, unit, vec, cotangent)


def outer_back_kernel(d_ref, w_ref, slope_ref, out_ref, sum_ref):
    sum_ref[...] = jnp.zeros_like(sum_ref)
    for rows in pieces(d_ref.shape[0]):
        d_pre = against(d_ref[rows, :], w_ref[...]) * slope_ref[rows, :].astype(FULL)
        out_ref[rows, :] = d_pre.astype(LOW)
        add_line(sum_ref, 0, d_pre)


def outer_back(d_mid, w_outer, slope):
    count, hidden = slope.shape
    return pl.pallas_call(
        outer_back_kernel,
        grid=(hidden // COLUMNS,),
        in_specs=[kept((count, D)), pl.BlockSpec((COLUMNS, D), lambda i: (i, 0)), columns_of(count)],
        out_specs=[columns_of(count), columns_of(1)],
        out_shape=[
            jax.ShapeDtypeStruct((count, hidden), LOW),
            jax.ShapeDtypeStruct((1, hidden), FULL),
        ],
        compiler_params=LIMIT,
        name="outer_back",
    )(d_mid, w_outer, slope)


def inner_back_kernel(
    d_pre_ref, w_ref, d_ref, unit_ref, inverse_ref, vec_ref, w_out_ref, out_ref, low_ref, attended_ref, sum_ref, total_ref
):
    step = pl.program_id(0)
    part = against(d_pre_ref[...], w_ref[...])

    @pl.when(step == 0)
    def _():
        total_ref[...] = d_ref[...] + part

    @pl.when(step > 0)
    def _():
        total_ref[...] += part

    @pl.when(step == pl.num_programs(0) - 1)
    def _():
        sum_ref[...] = jnp.zeros_like(sum_ref)
        for rows in pieces(total_ref.shape[0], 4):
            d_first = total_ref[rows, :]
            unit = unit_ref[rows, :]
            d_inner = normal_back(d_first * line(vec_ref, GAIN_ONE), unit, inverse_ref[rows, 0:1])
            low = d_inner.astype(LOW)
            out_ref[rows, :] = d_inner
            low_ref[rows, :] = low
            attended_ref[rows, :] = against(low, w_out_ref[...]).astype(LOW)
            add_line(sum_ref, 0, d_first * unit)
            add_line(sum_ref, 1, d_first)
            add_line(sum_ref, 2, d_inner)


def inner_back(d_pre, w_inner, d_second, unit, inverse, vec, w_out):
    count, hidden = d_pre.shape
    return pl.pallas_call(
        inner_back_kernel,
        grid=(hidden // D,),
        in_specs=[
            pl.BlockSpec((count, D), lambda i: (0, i)),
            pl.BlockSpec((D, D), lambda i: (0, i)),
            kept((count, D)),
            kept((count, D)),
            kept((count, LANES)),
            kept((8, D)),
            kept((D, D)),
        ],
        out_specs=[kept((count, D)), kept((count, D)), kept((count, D)), kept((8, D))],
        out_shape=[
            jax.ShapeDtypeStruct((count, D), FULL),
            jax.ShapeDtypeStruct((count, D), LOW),
            jax.ShapeDtypeStruct((count, D), LOW),
            jax.ShapeDtypeStruct((8, D), FULL),
        ],
        scratch_shapes=[pltpu.VMEM((count, D), FULL)],
        compiler_params=LIMIT,
        name="inner_back",
    )(d_pre, w_inner, d_second, unit, inverse, vec, w_out)


def tokens_kernel(base_ref, d_ref, w_ref, out_ref):
    out_ref[...] = (base_ref[...] + against(d_ref[...], w_ref[...])).astype(out_ref.dtype)


def tokens_back(base, d_group, w_group, kind):
    count, wide = d_group.shape
    rows = count // 2
    return pl.pallas_call(
        tokens_kernel,
        grid=(2,),
        in_specs=[
            pl.BlockSpec((rows, D), lambda i: (i, 0)),
            pl.BlockSpec((rows, wide), lambda i: (i, 0)),
            kept((D, wide)),
        ],
        out_specs=pl.BlockSpec((rows, D), lambda i: (i, 0)),
        out_shape=jax.ShapeDtypeStruct((count, D), kind),
        compiler_params=LIMIT,
        name="tokens_back",
    )(base, d_group, w_group)


def turn_kernel(ref, out_ref):
    out_ref[...] = ref[...].T


def turn(values):
    count, width = values.shape
    return pl.pallas_call(
        turn_kernel,
        grid=(count // ROWS,),
        in_specs=[rows_of(width)],
        out_specs=pl.BlockSpec((width, ROWS), lambda i: (0, i)),
        out_shape=jax.ShapeDtypeStruct((width, count), values.dtype),
        name="turn",
    )(values)


def product_kernel(left_ref, right_ref, out_ref):
    out_ref[...] = project(left_ref[...], right_ref[...]).astype(LOW)


def product_extra_kernel(size, left_ref, right_ref, small_ref, out_ref):
    found = project(left_ref[...], right_ref[...]).astype(LOW)
    body = found.shape[0] // size // 2
    for shard in range(size):
        extra = jnp.broadcast_to(small_ref[shard : shard + 1, :], (EXTRA, found.shape[1])).astype(LOW)
        for core in range(2):
            half = 2 * shard + core
            at = half * (body + EXTRA)
            out_ref[at : at + body, :] = found[half * body : (half + 1) * body]
            out_ref[at + body : at + body + EXTRA, :] = extra


def product(left, right, small=None, size=1):
    height, depth = left.shape
    rows = height if small is None else height + 2 * EXTRA * size
    return pl.pallas_call(
        product_kernel if small is None else functools.partial(product_extra_kernel, size),
        grid=(right.shape[1] // COLUMNS,),
        in_specs=[kept((height, depth)), columns_of(depth)] + ([] if small is None else [columns_of(size)]),
        out_specs=columns_of(rows),
        out_shape=jax.ShapeDtypeStruct((rows, right.shape[1]), LOW),
        compiler_params=LIMIT,
        name="product",
    )(left, right, *([] if small is None else [small]))


def assemble_kernel(moves, align, place_ref, *refs):
    out_ref, sems = refs[-2], refs[-1]
    copies = []
    for i, (which, start, rows) in enumerate(moves):
        place = pl.multiple_of(place_ref[i], align)
        source = refs[which].at[pl.ds(start, rows)]
        copies.append(pltpu.make_async_copy(source, out_ref.at[pl.ds(place, rows)], sems.at[i]))
    for copy in copies:
        copy.start()
    for copy in copies:
        copy.wait()


def assemble(arrays, moves, places, rows):
    align = min(move[2] for move in moves)
    return pl.pallas_call(
        functools.partial(assemble_kernel, moves, align),
        in_specs=[pl.BlockSpec(memory_space=pltpu.SMEM)] + [pl.BlockSpec(memory_space=pl.ANY)] * len(arrays),
        out_specs=pl.BlockSpec(memory_space=pltpu.VMEM),
        out_shape=jax.ShapeDtypeStruct((rows,) + arrays[0].shape[1:], arrays[0].dtype),
        scratch_shapes=[pltpu.SemaphoreType.DMA((len(moves),))],
        compiler_params=pltpu.CompilerParams(vmem_limit_bytes=24 * 2**20),
        name="assemble",
    )(jnp.stack(places).astype(jnp.int32), *arrays)


def pack_kernel(size, vectors, *refs):
    out_ref = refs[-1]
    for shard in range(size):
        at = 0
        for spans in vectors:
            lines = []
            for which, row, first, length in spans:
                lines += [(which, row, first + i) for i in range(0, length, LANES)]
            share = len(lines) // size
            for which, row, first in lines[shard * share : (shard + 1) * share]:
                out_ref[shard : shard + 1, at : at + LANES] = refs[which][row : row + 1, first : first + LANES]
                at += LANES


def pack(arrays, vectors, size):
    lengths = [sum(span[3] for span in spans) for spans in vectors]
    if any(length % (size * LANES) for length in lengths):
        whole = [
            jnp.concatenate([arrays[which][row, first : first + length] for which, row, first, length in spans])
            for spans in vectors
        ]
        return jnp.concatenate([vector.reshape(size, -1) for vector in whole], axis=1)
    return pl.pallas_call(
        functools.partial(pack_kernel, size, vectors),
        out_shape=jax.ShapeDtypeStruct((size, sum(lengths) // size), FULL),
        name="pack",
    )(*arrays)


def lay_kernel(*refs):
    out_ref = refs[-1]
    lines = []
    for ref in refs[:-1]:
        row = ref[...].astype(FULL)
        lines += [row[:, first : first + LANES] for first in range(0, row.shape[1], LANES)]
    spare = out_ref.shape[0] - len(lines)
    out_ref[...] = jnp.concatenate(lines + [jnp.zeros((spare, LANES), FULL)], axis=0).astype(LOW)


def lay(vectors, rows):
    return pl.pallas_call(
        lay_kernel,
        out_shape=jax.ShapeDtypeStruct((rows, LANES), LOW),
        name="lay",
    )(*vectors)


def unpack_kernel(size, ref, vec_ref, bias_ref, group_ref):
    group_ref[...] = jnp.zeros_like(group_ref)
    share = D // size
    for shard in range(size):
        packed = ref[shard * share : shard * share + EXTRA, :].astype(FULL)
        start = shard * LANES
        vec_ref[:, start : start + LANES] = packed[0:8, :]
        lines = bias_ref.shape[1] // size // LANES
        for i in range(lines):
            first = (shard * lines + i) * LANES
            bias_ref[:, first : first + LANES] = packed[8 + i : 9 + i, :]
        group = start // WIDE
        for place, row in ((0, QUERY), (2, VALUE)):
            first = group * 2 * WIDE + place * WIDE + start
            group_ref[:, first : first + LANES] = packed[row : row + 1, :]


def unpack(lines, size, hidden):
    return pl.pallas_call(
        functools.partial(unpack_kernel, size),
        out_shape=[
            jax.ShapeDtypeStruct((8, D), FULL),
            jax.ShapeDtypeStruct((1, hidden), FULL),
            jax.ShapeDtypeStruct((1, 3 * D), FULL),
        ],
        compiler_params=LIMIT,
        name="unpack",
    )(lines)


def tie(*values):
    return lax.optimization_barrier(values)


class Links:
    def __init__(self, mesh):
        self.reps, self.size = mesh.shape["cross"] * mesh.shape["core"], mesh.shape["shard"]
        size = self.size
        self.direct = size > RING_MOST or size % 2 == 1
        self.order = list(range(0, size, 2)) + list(range(size - 1, 0, -2))
        self.far = size // 2
        self.near = size - 1 - self.far
        shard = lax.axis_index("shard")
        self.core = lax.axis_index("core")
        self.sign = 1 - 2 * self.core
        self.place = jnp.where(shard % 2 == 0, shard // 2, size - 1 - shard // 2)

    def owner(self, step):
        place = (self.place + self.sign * step + 2 * self.size) % self.size
        return jnp.where(place < self.size // 2, 2 * place, 2 * (self.size - place) - 1)

    def hop(self, values, sign):
        pairs = []
        for rep in range(self.reps):
            turn = sign if rep % 2 == 0 else -sign
            for i, shard in enumerate(self.order):
                target = self.order[(i + turn) % self.size]
                pairs.append((rep * self.size + shard, rep * self.size + target))
        return lax.ppermute(values, AXES, pairs)

    def swap(self, values, bit):
        pairs = []
        for rep in range(self.reps):
            for shard in range(self.size):
                pairs.append((rep * self.size + shard, (rep ^ bit) * self.size + shard))
        return lax.ppermute(values, AXES, pairs)

    def half_of(self, values):
        half = values.shape[0] // 2
        return lax.dynamic_slice_in_dim(values, self.core * half, half, axis=0)


    def vectors(self, packed, hidden):
        small = lax.all_gather(packed, "shard", axis=0).astype(FULL)
        width, share = D // self.size, hidden // self.size
        vec = small[:, : 8 * width].reshape(self.size, 8, width).swapaxes(0, 1).reshape(8, D)
        bias = small[:, 8 * width : 8 * width + share].reshape(1, hidden)
        none = jnp.zeros((WIDE,), FULL)
        spans = [slice(g * WIDE, (g + 1) * WIDE) for g in range(GROUPS)]
        parts = [part for span in spans for part in (vec[QUERY, span], none, vec[VALUE, span])]
        return vec, bias, jnp.concatenate(parts).reshape(1, 3 * D)

    def half_of(self, values):
        half = values.shape[0] // 2
        return lax.dynamic_slice_in_dim(values, self.core * half, half, axis=0)

    def gather(self, values):
        if self.direct:
            return lax.all_gather(values, "shard", axis=0, tiled=True)
        rows = values.shape[0]
        body = rows // 2
        arrays = [values]
        moves = [(0, 0, rows)]
        places = [self.owner(0) * rows]

        def keep(chunk, mine, step):
            moves.append((len(arrays), 0, body))
            arrays.append(chunk)
            core = self.core if mine else 1 - self.core
            places.append(self.owner(step) * rows + core * body)

        ahead = back = self.half_of(values)
        for step in range(1, self.far + 2):
            flight = []
            if step > 1:
                keep(ahead, True, 1 - step)
                flight.append((self.swap(ahead, 1), step - 1))
                if step - 1 <= self.near:
                    keep(back, True, step - 1)
                    flight.append((self.swap(back, 1), 1 - step))
            if step <= self.far:
                ahead = self.hop(ahead, 1)
            if step <= self.near:
                back = self.hop(back, -1)
            ahead, back, *swapped = yield [ahead, back] + [chunk for chunk, _ in flight]
            for chunk, (_, place) in zip(swapped, flight):
                keep(chunk, False, place)
        return assemble(arrays, moves, places, self.size * rows)

    def quarter_of(self, values):
        rows = values.shape[0] // self.reps
        index = lax.axis_index("cross") * 2 + self.core
        return lax.dynamic_slice_in_dim(values, index * rows, rows, axis=0)

    def gather_quarters(self, mine):
        return lax.all_gather(mine, ("shard", "cross", "core"), axis=0, tiled=True)

    def finish(self, total):
        (cross,) = yield [self.swap(total, 2)]
        total = (total.astype(FULL) + cross.astype(FULL)).astype(LOW)
        (pair,) = yield [self.swap(total, 1)]
        low = jnp.where(self.core == 0, total, pair)
        high = jnp.where(self.core == 0, pair, total)
        return jnp.concatenate([low, high], axis=0).astype(FULL)

    def reduce(self, values):
        if self.direct:
            own = lax.psum_scatter(values, "shard", scatter_dimension=0, tiled=True)
            return lax.psum(own, ("cross", "core")).astype(FULL)
        width = values.shape[1]
        half = values.shape[0] // self.size // 2
        split = values.reshape(self.size, 2, half, width)
        other = self.swap(lax.dynamic_index_in_dim(split, 1 - self.core, axis=1, keepdims=False), 1)
        (other,) = yield [other]

        def piece(step):
            owner = self.owner(step)
            own = lax.dynamic_slice(split, (owner, self.core, 0, 0), (1, 1, half, width))
            pair = lax.dynamic_slice(other, (owner, 0, 0), (1, half, width))
            return own[0, 0].astype(FULL) + pair[0].astype(FULL)

        ahead = piece(self.far).astype(LOW)
        back = piece(-self.near).astype(LOW)
        for step in range(self.far - 1, -1, -1):
            moving = [self.hop(ahead, 1)]
            if step < self.near:
                moving.append(self.hop(back, -1))
            ahead, *rest = yield moving
            if step > 0:
                ahead = (ahead.astype(FULL) + piece(step)).astype(LOW)
            if rest:
                back = rest[0]
                if step > 0:
                    back = (back.astype(FULL) + piece(-step)).astype(LOW)
        total = (piece(0) + ahead.astype(FULL) + back.astype(FULL)).astype(LOW)
        return (yield from self.finish(total))


class Flow:
    def __init__(self):
        self.running = {}
        self.results = {}

    def start(self, name, steps):
        self._move(name, steps, None)

    def _move(self, name, steps, values):
        try:
            self.running[name] = (steps, steps.send(values))
        except StopIteration as end:
            self.running.pop(name, None)
            self.results[name] = end.value

    def advance(self, *values, near=None):
        running = [item for item in self.running.items() if near is None or item[0] in near]
        flat = list(values)
        for _, (_, flight) in running:
            flat += flight
        tied = tie(*flat) if flat else ()
        at = len(values)
        for name, (steps, flight) in running:
            self._move(name, steps, list(tied[at : at + len(flight)]))
            at += len(flight)
        return tied[0] if len(values) == 1 else tuple(tied[: len(values)])

    def take(self, name):
        while name in self.running:
            steps, flight = self.running[name]
            self._move(name, steps, flight)
        return self.results[name]


def shards(
    mesh,
    tokens,
    w_query,
    w_key,
    w_value,
    b_query,
    b_value,
    w_out,
    b_out,
    gain_one,
    shift_one,
    w_inner,
    b_inner,
    w_outer,
    b_outer,
    gain_two,
    shift_two,
    cotangent,
):
    links = Links(mesh)
    size = links.size
    width = D // size
    hidden = b_inner.shape[0]

    own_groups = [
        jnp.concatenate([w[:, g * WIDE : (g + 1) * WIDE] for w in (w_query, w_key, w_value)], axis=1)
        for g in range(GROUPS)
    ]
    vectors = (b_query, b_value, b_out, gain_one, shift_one, b_outer, gain_two, shift_two)
    used = len(vectors) * width + hidden
    ride = not links.direct and used <= 3 * WIDE and width == LANES and used <= width // links.reps * LANES
    flow = Flow()
    lines = [v.reshape(1, -1) for v in vectors + (b_inner,)]
    if ride:
        first_own = [links.quarter_of(w[:, :WIDE]) for w in (w_query, w_key, w_value)]
        first_own = jnp.concatenate(first_own + [lay(lines, width // links.reps)], axis=1)
        first_whole = links.gather_quarters(first_own)
    else:
        first_whole = lax.all_gather(own_groups[0], "shard", axis=0, tiled=True)
    whole_inner = links.gather_quarters(links.quarter_of(w_inner))
    flow.start("group1", links.gather(own_groups[1]))
    flow.advance()
    w_out = flow.advance(w_out)
    flow.start("out", links.gather(w_out))
    flow.advance()
    w_outer, tokens_turned = flow.advance(w_outer, turn(tokens))
    flow.start("outer", links.gather(w_outer))
    first_group = first_whole[:, : 3 * WIDE]
    if ride:
        vec, bias_inner, bias_groups = unpack(first_whole[:, 3 * WIDE :], size, size * hidden)
    else:
        vec, bias_inner, bias_groups = links.vectors(jnp.concatenate(lines, axis=1)[0], size * hidden)
    whole_groups = [first_group]

    projected = []
    attended, lse = None, []
    for g in range(GROUPS):
        bias = bias_groups[:, g * 3 * WIDE : (g + 1) * 3 * WIDE]
        projected.append((project(tokens, whole_groups[g]) + bias).astype(LOW))
        if g == 0:
            projected[g] = flow.advance(projected[g])
            attended, logs = attend(projected[g], g, attended)
            attended = flow.advance(attended)
            whole_groups.append(flow.take("group1"))
        else:
            projected[g] = flow.advance(projected[g])
            attended, logs = attend(projected[g], g, attended)
            attended = flow.advance(attended)
        lse.append(logs)
    whole_out = flow.take("out")
    unit_one, inverse_one, first_low = out_norm(attended, whole_out, tokens, vec)
    first_low = flow.advance(first_low)
    active, slope = inner_gelu(first_low, whole_inner, bias_inner)
    whole_outer = flow.take("outer")
    output, d_second, d_mid, sums_two = outer_norms(active, whole_outer, unit_one, vec, cotangent)

    grad_outer, d_mid = tie(gram(active, d_mid).astype(LOW), d_mid)
    flow.start("outer_back", links.reduce(grad_outer))
    d_pre, sum_inner = outer_back(d_mid, whole_outer, slope)
    d_pre = flow.advance(d_pre)
    grad_inner, d_pre = flow.advance(gram(first_low, d_pre).astype(LOW), d_pre)
    flow.start("inner_back", links.reduce(grad_inner))
    d_inner, d_branch, d_attended, sums_one = inner_back(
        d_pre, whole_inner, d_second, unit_one, inverse_one, vec, whole_out
    )
    d_branch, d_attended = flow.advance(d_branch, d_attended)
    grad_out, d_attended = tie(gram(attended, d_branch).astype(LOW), d_attended)

    d_groups, sums_group = [], []
    for g in range(GROUPS):
        d_group, sums = attend_back(projected[g], d_attended, lse[g], g)
        d_group, sums, d_attended = flow.advance(d_group, sums, d_attended)
        sums_group.append(sums)
        small = None
        if g == GROUPS - 1:
            arrays = [sums_one, sums_two, sum_inner] + sums_group
            spans = [[(3 + h, 0, place * WIDE, WIDE) for h in range(GROUPS)] for place in (0, 2)]
            spans += [[(i, row, 0, D)] for i, row in ((0, 2), (0, 0), (0, 1), (1, 2), (1, 0), (1, 1))]
            spans += [[(2, 0, 0, size * hidden)]]
            small = pack(arrays, spans, size)
        if ride and g == GROUPS - 1:
            small = jnp.pad(small, ((0, 0), (0, 3 * WIDE - used)))
            grad_group = product(tokens_turned, d_group, small, size)
        else:
            grad_group = product(tokens_turned, d_group)
        if g == 0:
            grad_group = jnp.concatenate([grad_group, grad_out], axis=1)
            grad_group, d_attended = tie(grad_group, d_attended)
        else:
            grad_group, d_group = flow.advance(grad_group, d_group)
        flow.start(f"back{g}", links.reduce(grad_group))
        d_groups.append(d_group)
    d_tokens = flow.advance(tokens_back(d_inner, d_groups[0], whole_groups[0], FULL))
    d_tokens = flow.advance(tokens_back(d_tokens, d_groups[1], whole_groups[1], LOW))
    own_outer = flow.take("outer_back")
    own_inner = flow.take("inner_back")
    own_groups = [flow.take(f"back{g}") for g in range(GROUPS)]
    own_out = own_groups[0][:, 3 * WIDE :]
    if ride:
        body = width // 2
        last = own_groups[1]
        own_small = last[body]
        own_groups[1] = jnp.concatenate([last[:body], last[body + EXTRA : 2 * body + EXTRA]], axis=0)
    else:
        own_small = lax.psum_scatter(small, "shard", scatter_dimension=0)
        own_small = lax.psum(own_small, ("cross", "core"))

    def joined(parts, place):
        columns = slice(place * WIDE, (place + 1) * WIDE)
        return jnp.concatenate([part[..., columns] for part in parts], axis=-1)

    (
        own_bias_query,
        own_bias_value,
        own_bias_out,
        own_gain_one,
        own_shift_one,
        own_bias_outer,
        own_gain_two,
        own_shift_two,
    ) = (own_small[i * width : (i + 1) * width] for i in range(len(vectors)))
    own_bias_inner = own_small[used - hidden : used]
    return (
        output,
        d_tokens,
        joined(own_groups, 0),
        joined(own_groups, 1),
        joined(own_groups, 2),
        own_bias_query,
        own_bias_value,
        own_out,
        own_bias_out,
        own_gain_one,
        own_shift_one,
        own_inner,
        own_bias_inner,
        own_outer,
        own_bias_outer,
        own_gain_two,
        own_shift_two,
    )


def solution(mesh):
    reps, size = mesh.shape["rep"], mesh.shape["shard"]
    mesh = jax.sharding.Mesh(mesh.devices.reshape(reps // 2, 2, size), AXES)
    rows = P(AXES, None)
    matrix = P("shard", None)
    vector = P("shard")
    return jax.shard_map(
        functools.partial(shards, mesh),
        mesh=mesh,
        in_specs=(
            rows,
            matrix,
            matrix,
            matrix,
            vector,
            vector,
            matrix,
            vector,
            vector,
            vector,
            matrix,
            vector,
            matrix,
            vector,
            vector,
            vector,
            rows,
        ),
        out_specs=(
            rows,
            rows,
            matrix,
            matrix,
            matrix,
            vector,
            vector,
            matrix,
            vector,
            vector,
            vector,
            matrix,
            vector,
            matrix,
            vector,
            vector,
            vector,
        ),
        check_vma=False,
    )
```

```python
import functools

import jax
import jax.numpy as jnp
from jax import lax
from jax.experimental import pallas as pl
from jax.experimental.pallas import tpu as pltpu
from jax.sharding import PartitionSpec as P

D = 1024
H = 16
DH = 64
SEQ = 512
LANES = 128
GROUPS = 2
PAIRS = D // LANES // GROUPS
WIDE = D // GROUPS
AXES = ("cross", "core", "shard")
RING_MOST = 16
LOW = jnp.bfloat16
FULL = jnp.float32


def project(left, right):
    return jnp.dot(left, right, preferred_element_type=FULL)


def gram(left, right):
    return lax.dot_general(left, right, (((0,), (0,)), ((), ())), preferred_element_type=FULL)


def against(left, right):
    return lax.dot_general(left, right, (((1,), (1,)), ((), ())), preferred_element_type=FULL)


def normal(values):
    centre = values - jnp.mean(values, axis=-1, keepdims=True)
    spread = jnp.mean(centre * centre, axis=-1, keepdims=True)
    inverse = lax.rsqrt(spread + 1e-12)
    return centre * inverse, inverse


def normal_back(scaled, unit, inverse):
    mean = jnp.mean(scaled, axis=-1, keepdims=True)
    along = jnp.mean(scaled * unit, axis=-1, keepdims=True)
    return (scaled - mean - unit * along) * inverse


def head_mask(head):
    lane = lax.broadcasted_iota(jnp.int32, (SEQ, LANES), 1)
    return (lane // DH) == head


def attend_kernel(query_ref, key_ref, value_ref, *rest):
    out_ref, lse_ref = rest[-2:]
    query = query_ref[...] * LOW(0.125)
    key = key_ref[...]
    value_t = value_ref[...].T
    parts = []
    for head in range(LANES // DH):
        own = jnp.where(head_mask(head), query, jnp.zeros_like(query))
        scores = against(key, own)
        top = jnp.max(scores, axis=0, keepdims=True)
        expo = jnp.exp(scores - top)
        total = jnp.sum(expo, axis=0, keepdims=True)
        mixed = project(value_t[head * DH : (head + 1) * DH], expo.astype(LOW))
        parts.append(mixed * (1.0 / total))
        lse_ref[0, head : head + 1, :] = top + jnp.log(total)
    out_ref[...] = jnp.concatenate(parts, axis=0).T.astype(LOW)


def attend_back_kernel(query_ref, key_ref, value_ref, d_ref, lse_ref, out_ref, sum_ref):
    seq, pair = pl.program_id(0), pl.program_id(1)
    query = query_ref[...] * LOW(0.125)
    key = key_ref[...]
    value = value_ref[...]
    d_out = d_ref[...]
    key_t = key.T
    d_key = None
    d_value = None
    d_query = []
    for head in range(LANES // DH):
        mask = head_mask(head)
        own = jnp.where(mask, query, jnp.zeros_like(query))
        d_own = jnp.where(mask, d_out, jnp.zeros_like(d_out))
        probs = jnp.exp(against(key, own) - lse_ref[0, head : head + 1, :])
        d_probs = against(value, d_own)
        inner = jnp.sum(probs * d_probs, axis=0, keepdims=True)
        d_scores = (probs * (d_probs - inner)).astype(LOW)
        part_value = project(probs.astype(LOW), d_own)
        part_key = project(d_scores, own)
        d_value = part_value if d_value is None else d_value + part_value
        d_key = part_key if d_key is None else d_key + part_key
        d_query.append(project(key_t[head * DH : (head + 1) * DH], d_scores))
    d_query = jnp.concatenate(d_query, axis=0).T * 0.125
    for place, grad in enumerate((d_query, d_key, d_value)):
        start = pl.multiple_of(place * WIDE + pair * LANES, LANES)
        out_ref[:, pl.ds(start, LANES)] = grad.astype(LOW)
        total = jnp.sum(grad, axis=0, keepdims=True)
        before = sum_ref[0:1, pl.ds(start, LANES)]
        sum_ref[0:1, pl.ds(start, LANES)] = jnp.where(seq == 0, total, before + total)


def column_block(first):
    return pl.BlockSpec((SEQ, LANES), lambda seq, pair: (seq, first + pair))


LSE_BLOCK = pl.BlockSpec((1, LANES // DH, SEQ), lambda seq, pair: (seq * PAIRS + pair, 0, 0))


def triple():
    return [column_block(place * PAIRS) for place in range(3)]


def attend(qkv, group, before):
    count = qkv.shape[0]
    seqs = count // SEQ
    kept = [] if before is None else [before]
    return pl.pallas_call(
        attend_kernel,
        grid=(seqs, PAIRS),
        in_specs=triple() + [pl.BlockSpec(memory_space=pl.ANY)] * len(kept),
        out_specs=[column_block(group * PAIRS), LSE_BLOCK],
        out_shape=[
            jax.ShapeDtypeStruct((count, D), LOW),
            jax.ShapeDtypeStruct((seqs * PAIRS, LANES // DH, SEQ), FULL),
        ],
        input_output_aliases={3: 0} if kept else {},
        compiler_params=pltpu.CompilerParams(vmem_limit_bytes=32 * 2**20),
        name="attend",
    )(qkv, qkv, qkv, *kept)


def attend_back(qkv, d_attended, lse, group):
    count = qkv.shape[0]
    return pl.pallas_call(
        attend_back_kernel,
        grid=(count // SEQ, PAIRS),
        in_specs=triple() + [column_block(group * PAIRS), LSE_BLOCK],
        out_specs=[
            pl.BlockSpec((SEQ, 3 * WIDE), lambda seq, pair: (seq, 0)),
            pl.BlockSpec((8, 3 * WIDE), lambda seq, pair: (0, 0)),
        ],
        out_shape=[
            jax.ShapeDtypeStruct((count, 3 * WIDE), LOW),
            jax.ShapeDtypeStruct((8, 3 * WIDE), FULL),
        ],
        compiler_params=pltpu.CompilerParams(vmem_limit_bytes=40 * 2**20),
        name="attend_back",
    )(qkv, qkv, qkv, d_attended, lse)


ROWS = 512
COLUMNS = 512
EXTRA = 16
PARTS = 2
(QUERY, VALUE, OUT, GAIN_ONE, SHIFT_ONE, OUTER, GAIN_TWO, SHIFT_TWO) = range(8)


def line(ref, row):
    return ref[row : row + 1, :]


def kept(shape):
    return pl.BlockSpec(shape, lambda i: (0,) * len(shape), pipeline_mode=pl.Buffered(1))


def rows_of(width):
    return pl.BlockSpec((ROWS, width), lambda i: (i, 0))


def columns_of(height):
    return pl.BlockSpec((height, COLUMNS), lambda i: (0, i))


def add_line(ref, row, values):
    ref[row : row + 1, :] += jnp.sum(values, axis=0, keepdims=True)


def clear(ref):
    @pl.when(pl.program_id(0) == 0)
    def _():
        ref[...] = jnp.zeros_like(ref)


def pieces(rows, count=PARTS):
    step = rows // count
    return [slice(i * step, (i + 1) * step) for i in range(count)]


LIMIT = pltpu.CompilerParams(vmem_limit_bytes=48 * 2**20)


def out_kernel(attended_ref, w_ref, tokens_ref, vec_ref, unit_ref, inverse_ref, low_ref):
    for rows in pieces(ROWS):
        branch = project(attended_ref[rows, :], w_ref[...]) + line(vec_ref, OUT)
        unit, inverse = normal(tokens_ref[rows, :].astype(FULL) + branch)
        unit_ref[rows, :] = unit
        inverse_ref[rows, :] = jnp.broadcast_to(inverse, (inverse.shape[0], LANES))
        low_ref[rows, :] = (unit * line(vec_ref, GAIN_ONE) + line(vec_ref, SHIFT_ONE)).astype(LOW)


def out_norm(attended, w_out, tokens, vec):
    count = tokens.shape[0]
    return pl.pallas_call(
        out_kernel,
        grid=(count // ROWS,),
        in_specs=[rows_of(D), kept((D, D)), rows_of(D), kept((8, D))],
        out_specs=[rows_of(D), rows_of(LANES), rows_of(D)],
        out_shape=[
            jax.ShapeDtypeStruct((count, D), FULL),
            jax.ShapeDtypeStruct((count, LANES), FULL),
            jax.ShapeDtypeStruct((count, D), LOW),
        ],
        compiler_params=LIMIT,
        name="out_norm",
    )(attended, w_out, tokens, vec)


def inner_kernel(low_ref, w_ref, bias_ref, active_ref, slope_ref):
    for rows in pieces(low_ref.shape[0], 4):
        pre = project(low_ref[rows, :], w_ref[...]) + bias_ref[...]
        below = 0.5 * (1.0 + lax.erf(pre * (0.5**0.5)))
        active_ref[rows, :] = (pre * below).astype(LOW)
        slope_ref[rows, :] = (below + pre * jnp.exp(-0.5 * pre * pre) * 0.3989422804014327).astype(LOW)


def inner_gelu(low, w_inner, bias):
    count, hidden = low.shape[0], w_inner.shape[1]
    return pl.pallas_call(
        inner_kernel,
        grid=(hidden // COLUMNS,),
        in_specs=[kept((count, D)), columns_of(D), columns_of(1)],
        out_specs=[columns_of(count), columns_of(count)],
        out_shape=[jax.ShapeDtypeStruct((count, hidden), LOW)] * 2,
        compiler_params=LIMIT,
        name="inner_gelu",
    )(low, w_inner, bias)


def outer_kernel(active_ref, w_ref, unit_ref, vec_ref, cot_ref, out_ref, d_ref, d_low_ref, sum_ref):
    clear(sum_ref)
    for rows in pieces(ROWS):
        first = unit_ref[rows, :] * line(vec_ref, GAIN_ONE) + line(vec_ref, SHIFT_ONE)
        second = first + project(active_ref[rows, :], w_ref[...]) + line(vec_ref, OUTER)
        unit, inverse = normal(second)
        out_ref[rows, :] = (unit * line(vec_ref, GAIN_TWO) + line(vec_ref, SHIFT_TWO)).astype(LOW)
        cot = cot_ref[rows, :].astype(FULL)
        d_second = normal_back(cot * line(vec_ref, GAIN_TWO), unit, inverse)
        d_ref[rows, :] = d_second
        d_low_ref[rows, :] = d_second.astype(LOW)
        add_line(sum_ref, 0, cot * unit)
        add_line(sum_ref, 1, cot)
        add_line(sum_ref, 2, d_second)


def outer_norms(active, w_outer, unit, vec, cotangent):
    count, hidden = active.shape
    return pl.pallas_call(
        outer_kernel,
        grid=(count // ROWS,),
        in_specs=[rows_of(hidden), kept((hidden, D)), rows_of(D), kept((8, D)), rows_of(D)],
        out_specs=[rows_of(D), rows_of(D), rows_of(D), kept((8, D))],
        out_shape=[
            jax.ShapeDtypeStruct((count, D), LOW),
            jax.ShapeDtypeStruct((count, D), FULL),
            jax.ShapeDtypeStruct((count, D), LOW),
            jax.ShapeDtypeStruct((8, D), FULL),
        ],
        compiler_params=LIMIT,
        name="outer_norms",
    )(active, w_outer, unit, vec, cotangent)


def outer_back_kernel(d_ref, w_ref, slope_ref, out_ref, sum_ref):
    sum_ref[...] = jnp.zeros_like(sum_ref)
    for rows in pieces(d_ref.shape[0]):
        d_pre = against(d_ref[rows, :], w_ref[...]) * slope_ref[rows, :].astype(FULL)
        out_ref[rows, :] = d_pre.astype(LOW)
        add_line(sum_ref, 0, d_pre)


def outer_back(d_mid, w_outer, slope):
    count, hidden = slope.shape
    return pl.pallas_call(
        outer_back_kernel,
        grid=(hidden // COLUMNS,),
        in_specs=[kept((count, D)), pl.BlockSpec((COLUMNS, D), lambda i: (i, 0)), columns_of(count)],
        out_specs=[columns_of(count), columns_of(1)],
        out_shape=[
            jax.ShapeDtypeStruct((count, hidden), LOW),
            jax.ShapeDtypeStruct((1, hidden), FULL),
        ],
        compiler_params=LIMIT,
        name="outer_back",
    )(d_mid, w_outer, slope)


def inner_back_kernel(
    d_pre_ref, w_ref, d_ref, unit_ref, inverse_ref, vec_ref, w_out_ref, out_ref, low_ref, attended_ref, sum_ref, total_ref
):
    step = pl.program_id(0)
    part = against(d_pre_ref[...], w_ref[...])

    @pl.when(step == 0)
    def _():
        total_ref[...] = d_ref[...] + part

    @pl.when(step > 0)
    def _():
        total_ref[...] += part

    @pl.when(step == pl.num_programs(0) - 1)
    def _():
        sum_ref[...] = jnp.zeros_like(sum_ref)
        for rows in pieces(total_ref.shape[0], 4):
            d_first = total_ref[rows, :]
            unit = unit_ref[rows, :]
            d_inner = normal_back(d_first * line(vec_ref, GAIN_ONE), unit, inverse_ref[rows, 0:1])
            low = d_inner.astype(LOW)
            out_ref[rows, :] = d_inner
            low_ref[rows, :] = low
            attended_ref[rows, :] = against(low, w_out_ref[...]).astype(LOW)
            add_line(sum_ref, 0, d_first * unit)
            add_line(sum_ref, 1, d_first)
            add_line(sum_ref, 2, d_inner)


def inner_back(d_pre, w_inner, d_second, unit, inverse, vec, w_out):
    count, hidden = d_pre.shape
    return pl.pallas_call(
        inner_back_kernel,
        grid=(hidden // D,),
        in_specs=[
            pl.BlockSpec((count, D), lambda i: (0, i)),
            pl.BlockSpec((D, D), lambda i: (0, i)),
            kept((count, D)),
            kept((count, D)),
            kept((count, LANES)),
            kept((8, D)),
            kept((D, D)),
        ],
        out_specs=[kept((count, D)), kept((count, D)), kept((count, D)), kept((8, D))],
        out_shape=[
            jax.ShapeDtypeStruct((count, D), FULL),
            jax.ShapeDtypeStruct((count, D), LOW),
            jax.ShapeDtypeStruct((count, D), LOW),
            jax.ShapeDtypeStruct((8, D), FULL),
        ],
        scratch_shapes=[pltpu.VMEM((count, D), FULL)],
        compiler_params=LIMIT,
        name="inner_back",
    )(d_pre, w_inner, d_second, unit, inverse, vec, w_out)


def tokens_kernel(base_ref, d_ref, w_ref, out_ref):
    out_ref[...] = (base_ref[...] + against(d_ref[...], w_ref[...])).astype(out_ref.dtype)


def tokens_back(base, d_group, w_group, kind):
    count, wide = d_group.shape
    rows = count // 2
    return pl.pallas_call(
        tokens_kernel,
        grid=(2,),
        in_specs=[
            pl.BlockSpec((rows, D), lambda i: (i, 0)),
            pl.BlockSpec((rows, wide), lambda i: (i, 0)),
            kept((D, wide)),
        ],
        out_specs=pl.BlockSpec((rows, D), lambda i: (i, 0)),
        out_shape=jax.ShapeDtypeStruct((count, D), kind),
        compiler_params=LIMIT,
        name="tokens_back",
    )(base, d_group, w_group)


def turn_kernel(ref, out_ref):
    out_ref[...] = ref[...].T


def turn(values):
    count, width = values.shape
    return pl.pallas_call(
        turn_kernel,
        grid=(count // ROWS,),
        in_specs=[rows_of(width)],
        out_specs=pl.BlockSpec((width, ROWS), lambda i: (0, i)),
        out_shape=jax.ShapeDtypeStruct((width, count), values.dtype),
        name="turn",
    )(values)


def product_kernel(left_ref, right_ref, out_ref):
    out_ref[...] = project(left_ref[...], right_ref[...]).astype(LOW)


def product_extra_kernel(size, left_ref, right_ref, small_ref, out_ref):
    found = project(left_ref[...], right_ref[...]).astype(LOW)
    body = found.shape[0] // size // 2
    for shard in range(size):
        extra = jnp.broadcast_to(small_ref[shard : shard + 1, :], (EXTRA, found.shape[1])).astype(LOW)
        for core in range(2):
            half = 2 * shard + core
            at = half * (body + EXTRA)
            out_ref[at : at + body, :] = found[half * body : (half + 1) * body]
            out_ref[at + body : at + body + EXTRA, :] = extra


def product(left, right, small=None, size=1):
    height, depth = left.shape
    rows = height if small is None else height + 2 * EXTRA * size
    return pl.pallas_call(
        product_kernel if small is None else functools.partial(product_extra_kernel, size),
        grid=(right.shape[1] // COLUMNS,),
        in_specs=[kept((height, depth)), columns_of(depth)] + ([] if small is None else [columns_of(size)]),
        out_specs=columns_of(rows),
        out_shape=jax.ShapeDtypeStruct((rows, right.shape[1]), LOW),
        compiler_params=LIMIT,
        name="product",
    )(left, right, *([] if small is None else [small]))


def assemble_kernel(moves, align, place_ref, *refs):
    out_ref, sems = refs[-2], refs[-1]
    copies = []
    for i, (which, start, rows) in enumerate(moves):
        place = pl.multiple_of(place_ref[i], align)
        source = refs[which].at[pl.ds(start, rows)]
        copies.append(pltpu.make_async_copy(source, out_ref.at[pl.ds(place, rows)], sems.at[i]))
    for copy in copies:
        copy.start()
    for copy in copies:
        copy.wait()


def assemble(arrays, moves, places, rows):
    align = min(move[2] for move in moves)
    return pl.pallas_call(
        functools.partial(assemble_kernel, moves, align),
        in_specs=[pl.BlockSpec(memory_space=pltpu.SMEM)] + [pl.BlockSpec(memory_space=pl.ANY)] * len(arrays),
        out_specs=pl.BlockSpec(memory_space=pltpu.VMEM),
        out_shape=jax.ShapeDtypeStruct((rows,) + arrays[0].shape[1:], arrays[0].dtype),
        scratch_shapes=[pltpu.SemaphoreType.DMA((len(moves),))],
        compiler_params=pltpu.CompilerParams(vmem_limit_bytes=24 * 2**20),
        name="assemble",
    )(jnp.stack(places).astype(jnp.int32), *arrays)


def pack_kernel(size, vectors, *refs):
    out_ref = refs[-1]
    for shard in range(size):
        at = 0
        for spans in vectors:
            lines = []
            for which, row, first, length in spans:
                lines += [(which, row, first + i) for i in range(0, length, LANES)]
            share = len(lines) // size
            for which, row, first in lines[shard * share : (shard + 1) * share]:
                out_ref[shard : shard + 1, at : at + LANES] = refs[which][row : row + 1, first : first + LANES]
                at += LANES


def pack(arrays, vectors, size):
    lengths = [sum(span[3] for span in spans) for spans in vectors]
    if any(length % (size * LANES) for length in lengths):
        whole = [
            jnp.concatenate([arrays[which][row, first : first + length] for which, row, first, length in spans])
            for spans in vectors
        ]
        return jnp.concatenate([vector.reshape(size, -1) for vector in whole], axis=1)
    return pl.pallas_call(
        functools.partial(pack_kernel, size, vectors),
        out_shape=jax.ShapeDtypeStruct((size, sum(lengths) // size), FULL),
        name="pack",
    )(*arrays)


def lay_kernel(*refs):
    row = jnp.concatenate([ref[...].astype(FULL) for ref in refs[:-1]], axis=1)
    refs[-1][...] = jnp.broadcast_to(row, refs[-1].shape).astype(LOW)


def lay(vectors):
    total = sum(vector.shape[1] for vector in vectors)
    return pl.pallas_call(
        lay_kernel,
        out_shape=jax.ShapeDtypeStruct((EXTRA, total), LOW),
        name="lay",
    )(*vectors)


def unpack_kernel(count, body, place_ref, *refs):
    vec_ref, bias_ref, group_ref = refs[count:]
    group_ref[...] = jnp.zeros_like(group_ref)
    hidden = bias_ref.shape[1] // count
    for i in range(count):
        packed = refs[i][body : body + EXTRA, :].astype(FULL)[0:1, :]
        owner = place_ref[i]
        start = pl.multiple_of(owner * LANES, LANES)
        for row in range(8):
            vec_ref[row : row + 1, pl.ds(start, LANES)] = packed[:, row * LANES : (row + 1) * LANES]
        first = pl.multiple_of(owner * hidden, LANES)
        bias_ref[:, pl.ds(first, hidden)] = packed[:, 8 * LANES : 8 * LANES + hidden]
        group = owner * LANES // WIDE
        for place, row in ((0, QUERY), (2, VALUE)):
            first = pl.multiple_of(group * 2 * WIDE + place * WIDE + start, LANES)
            group_ref[:, pl.ds(first, LANES)] = packed[:, row * LANES : (row + 1) * LANES]


def unpack(chunks, owners, body, hidden):
    count = len(chunks)
    return pl.pallas_call(
        functools.partial(unpack_kernel, count, body),
        in_specs=[pl.BlockSpec(memory_space=pltpu.SMEM)] + [pl.BlockSpec(memory_space=pltpu.VMEM)] * count,
        out_shape=[
            jax.ShapeDtypeStruct((8, D), FULL),
            jax.ShapeDtypeStruct((1, hidden), FULL),
            jax.ShapeDtypeStruct((1, 3 * D), FULL),
        ],
        compiler_params=LIMIT,
        name="unpack",
    )(jnp.stack(owners).astype(jnp.int32), *chunks)


def tie(*values):
    return lax.optimization_barrier(values)


class Links:
    def __init__(self, mesh):
        self.reps, self.size = mesh.shape["cross"] * mesh.shape["core"], mesh.shape["shard"]
        size = self.size
        self.direct = size > RING_MOST or size % 2 == 1
        self.order = list(range(0, size, 2)) + list(range(size - 1, 0, -2))
        self.far = size // 2
        self.near = size - 1 - self.far
        shard = lax.axis_index("shard")
        self.core = lax.axis_index("core")
        self.sign = 1 - 2 * self.core
        self.place = jnp.where(shard % 2 == 0, shard // 2, size - 1 - shard // 2)

    def owner(self, step):
        place = (self.place + self.sign * step + 2 * self.size) % self.size
        return jnp.where(place < self.size // 2, 2 * place, 2 * (self.size - place) - 1)

    def hop(self, values, sign):
        pairs = []
        for rep in range(self.reps):
            turn = sign if rep % 2 == 0 else -sign
            for i, shard in enumerate(self.order):
                target = self.order[(i + turn) % self.size]
                pairs.append((rep * self.size + shard, rep * self.size + target))
        return lax.ppermute(values, AXES, pairs)

    def swap(self, values, bit):
        pairs = []
        for rep in range(self.reps):
            for shard in range(self.size):
                pairs.append((rep * self.size + shard, (rep ^ bit) * self.size + shard))
        return lax.ppermute(values, AXES, pairs)

    def half_of(self, values):
        half = values.shape[0] // 2
        return lax.dynamic_slice_in_dim(values, self.core * half, half, axis=0)


    def vectors(self, packed, hidden):
        small = lax.all_gather(packed, "shard", axis=0).astype(FULL)
        width, share = D // self.size, hidden // self.size
        vec = small[:, : 8 * width].reshape(self.size, 8, width).swapaxes(0, 1).reshape(8, D)
        bias = small[:, 8 * width : 8 * width + share].reshape(1, hidden)
        none = jnp.zeros((WIDE,), FULL)
        spans = [slice(g * WIDE, (g + 1) * WIDE) for g in range(GROUPS)]
        parts = [part for span in spans for part in (vec[QUERY, span], none, vec[VALUE, span])]
        return vec, bias, jnp.concatenate(parts).reshape(1, 3 * D)

    def half_of(self, values):
        half = values.shape[0] // 2
        return lax.dynamic_slice_in_dim(values, self.core * half, half, axis=0)

    def gather(self, values, sent=None):
        if self.direct:
            return lax.all_gather(values, "shard", axis=0, tiled=True)
        rows = values.shape[0]
        body = rows // 2
        arrays = [values]
        moves = [(0, 0, rows)]
        places = [self.owner(0) * rows]
        chunks, owners = [sent], [self.owner(0)]

        def keep(chunk, mine, step):
            moves.append((len(arrays), 0, body))
            arrays.append(chunk)
            core = self.core if mine else 1 - self.core
            places.append(self.owner(step) * rows + core * body)
            if mine:
                chunks.append(chunk)
                owners.append(self.owner(step))

        ahead = back = self.half_of(values) if sent is None else sent
        for step in range(1, self.far + 2):
            flight = []
            if step > 1:
                keep(ahead, True, 1 - step)
                flight.append((self.swap(ahead, 1), step - 1))
                if step - 1 <= self.near:
                    keep(back, True, step - 1)
                    flight.append((self.swap(back, 1), 1 - step))
            if step <= self.far:
                ahead = self.hop(ahead, 1)
            if step <= self.near:
                back = self.hop(back, -1)
            ahead, back, *swapped = yield [ahead, back] + [chunk for chunk, _ in flight]
            for chunk, (_, place) in zip(swapped, flight):
                keep(chunk, False, place)
        whole = assemble(arrays, moves, places, self.size * rows)
        return whole if sent is None else (whole, chunks, owners)

    def gather_quarters(self, values):
        rows = values.shape[0] // self.reps
        index = lax.axis_index("cross") * 2 + self.core
        mine = lax.dynamic_slice_in_dim(values, index * rows, rows, axis=0)
        return lax.all_gather(mine, ("shard", "cross", "core"), axis=0, tiled=True)

    def finish(self, total):
        (cross,) = yield [self.swap(total, 2)]
        total = (total.astype(FULL) + cross.astype(FULL)).astype(LOW)
        (pair,) = yield [self.swap(total, 1)]
        low = jnp.where(self.core == 0, total, pair)
        high = jnp.where(self.core == 0, pair, total)
        return jnp.concatenate([low, high], axis=0).astype(FULL)

    def reduce(self, values):
        if self.direct:
            own = lax.psum_scatter(values, "shard", scatter_dimension=0, tiled=True)
            return lax.psum(own, ("cross", "core")).astype(FULL)
        width = values.shape[1]
        half = values.shape[0] // self.size // 2
        split = values.reshape(self.size, 2, half, width)
        other = self.swap(lax.dynamic_index_in_dim(split, 1 - self.core, axis=1, keepdims=False), 1)
        (other,) = yield [other]

        def piece(step):
            owner = self.owner(step)
            own = lax.dynamic_slice(split, (owner, self.core, 0, 0), (1, 1, half, width))
            pair = lax.dynamic_slice(other, (owner, 0, 0), (1, half, width))
            return own[0, 0].astype(FULL) + pair[0].astype(FULL)

        ahead = piece(self.far).astype(LOW)
        back = piece(-self.near).astype(LOW)
        for step in range(self.far - 1, -1, -1):
            moving = [self.hop(ahead, 1)]
            if step < self.near:
                moving.append(self.hop(back, -1))
            ahead, *rest = yield moving
            if step > 0:
                ahead = (ahead.astype(FULL) + piece(step)).astype(LOW)
            if rest:
                back = rest[0]
                if step > 0:
                    back = (back.astype(FULL) + piece(-step)).astype(LOW)
        total = (piece(0) + ahead.astype(FULL) + back.astype(FULL)).astype(LOW)
        return (yield from self.finish(total))


class Flow:
    def __init__(self):
        self.running = {}
        self.results = {}

    def start(self, name, steps):
        self._move(name, steps, None)

    def _move(self, name, steps, values):
        try:
            self.running[name] = (steps, steps.send(values))
        except StopIteration as end:
            self.running.pop(name, None)
            self.results[name] = end.value

    def advance(self, *values, near=None):
        running = [item for item in self.running.items() if near is None or item[0] in near]
        flat = list(values)
        for _, (_, flight) in running:
            flat += flight
        tied = tie(*flat) if flat else ()
        at = len(values)
        for name, (steps, flight) in running:
            self._move(name, steps, list(tied[at : at + len(flight)]))
            at += len(flight)
        return tied[0] if len(values) == 1 else tuple(tied[: len(values)])

    def take(self, name):
        while name in self.running:
            steps, flight = self.running[name]
            self._move(name, steps, flight)
        return self.results[name]


def shards(
    mesh,
    tokens,
    w_query,
    w_key,
    w_value,
    b_query,
    b_value,
    w_out,
    b_out,
    gain_one,
    shift_one,
    w_inner,
    b_inner,
    w_outer,
    b_outer,
    gain_two,
    shift_two,
    cotangent,
):
    links = Links(mesh)
    size = links.size
    width = D // size
    hidden = b_inner.shape[0]

    own_groups = [
        jnp.concatenate([w[:, g * WIDE : (g + 1) * WIDE] for w in (w_query, w_key, w_value)], axis=1)
        for g in range(GROUPS)
    ]
    vectors = (b_query, b_value, b_out, gain_one, shift_one, b_outer, gain_two, shift_two)
    used = len(vectors) * width + hidden
    ride = not links.direct and used <= 3 * WIDE and width == LANES
    rows_in = [v.reshape(1, -1) for v in vectors + (b_inner,)]
    packed = jnp.concatenate(rows_in, axis=1)
    sent = None
    if ride:
        extra = jnp.pad(lay(rows_in), ((0, 0), (0, 3 * WIDE - used)))
        halves = [links.half_of(w[:, :WIDE]) for w in (w_query, w_key, w_value)]
        sent = jnp.concatenate([jnp.concatenate(halves, axis=1), extra], axis=0)
        sent, w_inner, w_outer = tie(sent, w_inner, w_outer)
    flow = Flow()
    flow.start("group0", links.gather(own_groups[0], sent))
    whole_inner = links.gather_quarters(w_inner)
    whole_outer = links.gather_quarters(w_outer)
    flow.advance()
    own_groups[1] = flow.advance(own_groups[1])
    flow.start("group1", links.gather(own_groups[1]))
    w_out = flow.advance(w_out)
    flow.start("out", links.gather(w_out))
    tokens_turned = flow.advance(turn(tokens))
    if ride:
        first_group, chunks, owners = flow.take("group0")
        vec, bias_inner, bias_groups = unpack(chunks, owners, width // 2, size * hidden)
    else:
        first_group = flow.take("group0")
        vec, bias_inner, bias_groups = links.vectors(packed[0], size * hidden)
    whole_groups = [first_group]

    projected = []
    attended, lse = None, []
    for g in range(GROUPS):
        bias = bias_groups[:, g * 3 * WIDE : (g + 1) * 3 * WIDE]
        projected.append((project(tokens, whole_groups[g]) + bias).astype(LOW))
        if g == 0:
            projected[g] = flow.advance(projected[g])
            attended, logs = attend(projected[g], g, attended)
            attended = flow.advance(attended)
            whole_groups.append(flow.take("group1"))
        else:
            projected[g] = flow.advance(projected[g])
            attended, logs = attend(projected[g], g, attended)
            attended = flow.advance(attended)
        lse.append(logs)
    whole_out = flow.take("out")
    unit_one, inverse_one, first_low = out_norm(attended, whole_out, tokens, vec)
    active, slope = inner_gelu(first_low, whole_inner, bias_inner)
    output, d_second, d_mid, sums_two = outer_norms(active, whole_outer, unit_one, vec, cotangent)

    grad_outer, d_mid = tie(gram(active, d_mid).astype(LOW), d_mid)
    flow.start("outer_back", links.reduce(grad_outer))
    d_pre, sum_inner = outer_back(d_mid, whole_outer, slope)
    d_pre = flow.advance(d_pre)
    grad_inner, d_pre = flow.advance(gram(first_low, d_pre).astype(LOW), d_pre)
    flow.start("inner_back", links.reduce(grad_inner))
    d_inner, d_branch, d_attended, sums_one = inner_back(
        d_pre, whole_inner, d_second, unit_one, inverse_one, vec, whole_out
    )
    d_branch, d_attended = flow.advance(d_branch, d_attended)
    grad_out, d_attended = tie(gram(attended, d_branch).astype(LOW), d_attended)

    d_groups, sums_group = [], []
    for g in range(GROUPS):
        d_group, sums = attend_back(projected[g], d_attended, lse[g], g)
        d_group, sums, d_attended = flow.advance(d_group, sums, d_attended)
        sums_group.append(sums)
        small = None
        if g == GROUPS - 1:
            arrays = [sums_one, sums_two, sum_inner] + sums_group
            spans = [[(3 + h, 0, place * WIDE, WIDE) for h in range(GROUPS)] for place in (0, 2)]
            spans += [[(i, row, 0, D)] for i, row in ((0, 2), (0, 0), (0, 1), (1, 2), (1, 0), (1, 1))]
            spans += [[(2, 0, 0, size * hidden)]]
            small = pack(arrays, spans, size)
        if ride and g == GROUPS - 1:
            small = jnp.pad(small, ((0, 0), (0, 3 * WIDE - used)))
            grad_group = product(tokens_turned, d_group, small, size)
        else:
            grad_group = product(tokens_turned, d_group)
        if g == 0:
            grad_group = jnp.concatenate([grad_group, grad_out], axis=1)
            grad_group, d_attended = tie(grad_group, d_attended)
        else:
            grad_group, d_group = flow.advance(grad_group, d_group)
        flow.start(f"back{g}", links.reduce(grad_group))
        d_groups.append(d_group)
    d_tokens = flow.advance(tokens_back(d_inner, d_groups[0], whole_groups[0], FULL))
    d_tokens = flow.advance(tokens_back(d_tokens, d_groups[1], whole_groups[1], LOW))
    own_outer = flow.take("outer_back")
    own_inner = flow.take("inner_back")
    own_groups = [flow.take(f"back{g}") for g in range(GROUPS)]
    own_out = own_groups[0][:, 3 * WIDE :]
    if ride:
        body = width // 2
        last = own_groups[1]
        own_small = last[body]
        own_groups[1] = jnp.concatenate([last[:body], last[body + EXTRA : 2 * body + EXTRA]], axis=0)
    else:
        own_small = lax.psum_scatter(small, "shard", scatter_dimension=0)
        own_small = lax.psum(own_small, ("cross", "core"))

    def joined(parts, place):
        columns = slice(place * WIDE, (place + 1) * WIDE)
        return jnp.concatenate([part[..., columns] for part in parts], axis=-1)

    (
        own_bias_query,
        own_bias_value,
        own_bias_out,
        own_gain_one,
        own_shift_one,
        own_bias_outer,
        own_gain_two,
        own_shift_two,
    ) = (own_small[i * width : (i + 1) * width] for i in range(len(vectors)))
    own_bias_inner = own_small[used - hidden : used]
    return (
        output,
        d_tokens,
        joined(own_groups, 0),
        joined(own_groups, 1),
        joined(own_groups, 2),
        own_bias_query,
        own_bias_value,
        own_out,
        own_bias_out,
        own_gain_one,
        own_shift_one,
        own_inner,
        own_bias_inner,
        own_outer,
        own_bias_outer,
        own_gain_two,
        own_shift_two,
    )


def solution(mesh):
    reps, size = mesh.shape["rep"], mesh.shape["shard"]
    mesh = jax.sharding.Mesh(mesh.devices.reshape(reps // 2, 2, size), AXES)
    rows = P(AXES, None)
    matrix = P("shard", None)
    vector = P("shard")
    return jax.shard_map(
        functools.partial(shards, mesh),
        mesh=mesh,
        in_specs=(
            rows,
            matrix,
            matrix,
            matrix,
            vector,
            vector,
            matrix,
            vector,
            vector,
            vector,
            matrix,
            vector,
            matrix,
            vector,
            vector,
            vector,
            rows,
        ),
        out_specs=(
            rows,
            rows,
            matrix,
            matrix,
            matrix,
            vector,
            vector,
            matrix,
            vector,
            vector,
            vector,
            matrix,
            vector,
            matrix,
            vector,
            vector,
            vector,
        ),
        check_vma=False,
    )
```

```python
import functools

import jax
import jax.numpy as jnp
from jax import lax
from jax.experimental import pallas as pl
from jax.experimental.pallas import tpu as pltpu
from jax.sharding import PartitionSpec as P

D = 1024
H = 16
DH = 64
SEQ = 512
LANES = 128
GROUPS = 2
PAIRS = D // LANES // GROUPS
WIDE = D // GROUPS
AXES = ("cross", "core", "shard")
RING_MOST = 16
LOW = jnp.bfloat16
FULL = jnp.float32


def project(left, right):
    return jnp.dot(left, right, preferred_element_type=FULL)


def gram(left, right):
    return lax.dot_general(left, right, (((0,), (0,)), ((), ())), preferred_element_type=FULL)


def against(left, right):
    return lax.dot_general(left, right, (((1,), (1,)), ((), ())), preferred_element_type=FULL)


def normal(values):
    centre = values - jnp.mean(values, axis=-1, keepdims=True)
    spread = jnp.mean(centre * centre, axis=-1, keepdims=True)
    inverse = lax.rsqrt(spread + 1e-12)
    return centre * inverse, inverse


def normal_back(scaled, unit, inverse):
    mean = jnp.mean(scaled, axis=-1, keepdims=True)
    along = jnp.mean(scaled * unit, axis=-1, keepdims=True)
    return (scaled - mean - unit * along) * inverse


def head_mask(head):
    lane = lax.broadcasted_iota(jnp.int32, (SEQ, LANES), 1)
    return (lane // DH) == head


def attend_kernel(query_ref, key_ref, value_ref, *rest):
    out_ref, lse_ref = rest[-2:]
    query = query_ref[...] * LOW(0.125)
    key = key_ref[...]
    value_t = value_ref[...].T
    parts = []
    for head in range(LANES // DH):
        own = jnp.where(head_mask(head), query, jnp.zeros_like(query))
        scores = against(key, own)
        top = jnp.max(scores, axis=0, keepdims=True)
        expo = jnp.exp(scores - top)
        total = jnp.sum(expo, axis=0, keepdims=True)
        mixed = project(value_t[head * DH : (head + 1) * DH], expo.astype(LOW))
        parts.append(mixed * (1.0 / total))
        lse_ref[0, head : head + 1, :] = top + jnp.log(total)
    out_ref[...] = jnp.concatenate(parts, axis=0).T.astype(LOW)


def attend_back_kernel(query_ref, key_ref, value_ref, d_ref, lse_ref, out_ref, sum_ref):
    seq, pair = pl.program_id(0), pl.program_id(1)
    query = query_ref[...] * LOW(0.125)
    key = key_ref[...]
    value = value_ref[...]
    d_out = d_ref[...]
    key_t = key.T
    d_key = None
    d_value = None
    d_query = []
    for head in range(LANES // DH):
        mask = head_mask(head)
        own = jnp.where(mask, query, jnp.zeros_like(query))
        d_own = jnp.where(mask, d_out, jnp.zeros_like(d_out))
        probs = jnp.exp(against(key, own) - lse_ref[0, head : head + 1, :])
        d_probs = against(value, d_own)
        inner = jnp.sum(probs * d_probs, axis=0, keepdims=True)
        d_scores = (probs * (d_probs - inner)).astype(LOW)
        part_value = project(probs.astype(LOW), d_own)
        part_key = project(d_scores, own)
        d_value = part_value if d_value is None else d_value + part_value
        d_key = part_key if d_key is None else d_key + part_key
        d_query.append(project(key_t[head * DH : (head + 1) * DH], d_scores))
    d_query = jnp.concatenate(d_query, axis=0).T * 0.125
    for place, grad in enumerate((d_query, d_key, d_value)):
        start = pl.multiple_of(place * WIDE + pair * LANES, LANES)
        out_ref[:, pl.ds(start, LANES)] = grad.astype(LOW)
        total = jnp.sum(grad, axis=0, keepdims=True)
        before = sum_ref[0:1, pl.ds(start, LANES)]
        sum_ref[0:1, pl.ds(start, LANES)] = jnp.where(seq == 0, total, before + total)


def column_block(first):
    return pl.BlockSpec((SEQ, LANES), lambda seq, pair: (seq, first + pair))


LSE_BLOCK = pl.BlockSpec((1, LANES // DH, SEQ), lambda seq, pair: (seq * PAIRS + pair, 0, 0))


def triple():
    return [column_block(place * PAIRS) for place in range(3)]


def attend(qkv, group, before):
    count = qkv.shape[0]
    seqs = count // SEQ
    kept = [] if before is None else [before]
    return pl.pallas_call(
        attend_kernel,
        grid=(seqs, PAIRS),
        in_specs=triple() + [pl.BlockSpec(memory_space=pl.ANY)] * len(kept),
        out_specs=[column_block(group * PAIRS), LSE_BLOCK],
        out_shape=[
            jax.ShapeDtypeStruct((count, D), LOW),
            jax.ShapeDtypeStruct((seqs * PAIRS, LANES // DH, SEQ), FULL),
        ],
        input_output_aliases={3: 0} if kept else {},
        compiler_params=pltpu.CompilerParams(vmem_limit_bytes=32 * 2**20),
        name="attend",
    )(qkv, qkv, qkv, *kept)


def attend_back(qkv, d_attended, lse, group):
    count = qkv.shape[0]
    return pl.pallas_call(
        attend_back_kernel,
        grid=(count // SEQ, PAIRS),
        in_specs=triple() + [column_block(group * PAIRS), LSE_BLOCK],
        out_specs=[
            pl.BlockSpec((SEQ, 3 * WIDE), lambda seq, pair: (seq, 0)),
            pl.BlockSpec((8, 3 * WIDE), lambda seq, pair: (0, 0)),
        ],
        out_shape=[
            jax.ShapeDtypeStruct((count, 3 * WIDE), LOW),
            jax.ShapeDtypeStruct((8, 3 * WIDE), FULL),
        ],
        compiler_params=pltpu.CompilerParams(vmem_limit_bytes=40 * 2**20),
        name="attend_back",
    )(qkv, qkv, qkv, d_attended, lse)


ROWS = 512
COLUMNS = 512
EXTRA = 16
PARTS = 2
(QUERY, VALUE, OUT, GAIN_ONE, SHIFT_ONE, OUTER, GAIN_TWO, SHIFT_TWO) = range(8)


def line(ref, row):
    return ref[row : row + 1, :]


def kept(shape):
    return pl.BlockSpec(shape, lambda i: (0,) * len(shape), pipeline_mode=pl.Buffered(1))


def rows_of(width):
    return pl.BlockSpec((ROWS, width), lambda i: (i, 0))


def columns_of(height):
    return pl.BlockSpec((height, COLUMNS), lambda i: (0, i))


def add_line(ref, row, values):
    ref[row : row + 1, :] += jnp.sum(values, axis=0, keepdims=True)


def clear(ref):
    @pl.when(pl.program_id(0) == 0)
    def _():
        ref[...] = jnp.zeros_like(ref)


def pieces(rows, count=PARTS):
    step = rows // count
    return [slice(i * step, (i + 1) * step) for i in range(count)]


LIMIT = pltpu.CompilerParams(vmem_limit_bytes=48 * 2**20)


def out_kernel(attended_ref, w_ref, tokens_ref, vec_ref, unit_ref, inverse_ref, low_ref):
    for rows in pieces(ROWS):
        branch = project(attended_ref[rows, :], w_ref[...]) + line(vec_ref, OUT)
        unit, inverse = normal(tokens_ref[rows, :].astype(FULL) + branch)
        unit_ref[rows, :] = unit
        inverse_ref[rows, :] = jnp.broadcast_to(inverse, (inverse.shape[0], LANES))
        low_ref[rows, :] = (unit * line(vec_ref, GAIN_ONE) + line(vec_ref, SHIFT_ONE)).astype(LOW)


def out_norm(attended, w_out, tokens, vec):
    count = tokens.shape[0]
    return pl.pallas_call(
        out_kernel,
        grid=(count // ROWS,),
        in_specs=[rows_of(D), kept((D, D)), rows_of(D), kept((8, D))],
        out_specs=[rows_of(D), rows_of(LANES), rows_of(D)],
        out_shape=[
            jax.ShapeDtypeStruct((count, D), FULL),
            jax.ShapeDtypeStruct((count, LANES), FULL),
            jax.ShapeDtypeStruct((count, D), LOW),
        ],
        compiler_params=LIMIT,
        name="out_norm",
    )(attended, w_out, tokens, vec)


def inner_kernel(low_ref, w_ref, bias_ref, active_ref, slope_ref):
    for rows in pieces(low_ref.shape[0], 4):
        pre = project(low_ref[rows, :], w_ref[...]) + bias_ref[...]
        below = 0.5 * (1.0 + lax.erf(pre * (0.5**0.5)))
        active_ref[rows, :] = (pre * below).astype(LOW)
        slope_ref[rows, :] = (below + pre * jnp.exp(-0.5 * pre * pre) * 0.3989422804014327).astype(LOW)


def inner_gelu(low, w_inner, bias):
    count, hidden = low.shape[0], w_inner.shape[1]
    return pl.pallas_call(
        inner_kernel,
        grid=(hidden // COLUMNS,),
        in_specs=[kept((count, D)), columns_of(D), columns_of(1)],
        out_specs=[columns_of(count), columns_of(count)],
        out_shape=[jax.ShapeDtypeStruct((count, hidden), LOW)] * 2,
        compiler_params=LIMIT,
        name="inner_gelu",
    )(low, w_inner, bias)


def outer_kernel(active_ref, w_ref, unit_ref, vec_ref, cot_ref, out_ref, d_ref, d_low_ref, sum_ref):
    clear(sum_ref)
    for rows in pieces(ROWS):
        first = unit_ref[rows, :] * line(vec_ref, GAIN_ONE) + line(vec_ref, SHIFT_ONE)
        second = first + project(active_ref[rows, :], w_ref[...]) + line(vec_ref, OUTER)
        unit, inverse = normal(second)
        out_ref[rows, :] = (unit * line(vec_ref, GAIN_TWO) + line(vec_ref, SHIFT_TWO)).astype(LOW)
        cot = cot_ref[rows, :].astype(FULL)
        d_second = normal_back(cot * line(vec_ref, GAIN_TWO), unit, inverse)
        d_ref[rows, :] = d_second
        d_low_ref[rows, :] = d_second.astype(LOW)
        add_line(sum_ref, 0, cot * unit)
        add_line(sum_ref, 1, cot)
        add_line(sum_ref, 2, d_second)


def outer_norms(active, w_outer, unit, vec, cotangent):
    count, hidden = active.shape
    return pl.pallas_call(
        outer_kernel,
        grid=(count // ROWS,),
        in_specs=[rows_of(hidden), kept((hidden, D)), rows_of(D), kept((8, D)), rows_of(D)],
        out_specs=[rows_of(D), rows_of(D), rows_of(D), kept((8, D))],
        out_shape=[
            jax.ShapeDtypeStruct((count, D), LOW),
            jax.ShapeDtypeStruct((count, D), FULL),
            jax.ShapeDtypeStruct((count, D), LOW),
            jax.ShapeDtypeStruct((8, D), FULL),
        ],
        compiler_params=LIMIT,
        name="outer_norms",
    )(active, w_outer, unit, vec, cotangent)


def outer_back_kernel(d_ref, w_ref, slope_ref, out_ref, sum_ref):
    sum_ref[...] = jnp.zeros_like(sum_ref)
    for rows in pieces(d_ref.shape[0]):
        d_pre = against(d_ref[rows, :], w_ref[...]) * slope_ref[rows, :].astype(FULL)
        out_ref[rows, :] = d_pre.astype(LOW)
        add_line(sum_ref, 0, d_pre)


def outer_back(d_mid, w_outer, slope):
    count, hidden = slope.shape
    return pl.pallas_call(
        outer_back_kernel,
        grid=(hidden // COLUMNS,),
        in_specs=[kept((count, D)), pl.BlockSpec((COLUMNS, D), lambda i: (i, 0)), columns_of(count)],
        out_specs=[columns_of(count), columns_of(1)],
        out_shape=[
            jax.ShapeDtypeStruct((count, hidden), LOW),
            jax.ShapeDtypeStruct((1, hidden), FULL),
        ],
        compiler_params=LIMIT,
        name="outer_back",
    )(d_mid, w_outer, slope)


def inner_back_kernel(
    d_pre_ref, w_ref, d_ref, unit_ref, inverse_ref, vec_ref, w_out_ref, out_ref, low_ref, attended_ref, sum_ref, total_ref
):
    step = pl.program_id(0)
    part = against(d_pre_ref[...], w_ref[...])

    @pl.when(step == 0)
    def _():
        total_ref[...] = d_ref[...] + part

    @pl.when(step > 0)
    def _():
        total_ref[...] += part

    @pl.when(step == pl.num_programs(0) - 1)
    def _():
        sum_ref[...] = jnp.zeros_like(sum_ref)
        for rows in pieces(total_ref.shape[0], 4):
            d_first = total_ref[rows, :]
            unit = unit_ref[rows, :]
            d_inner = normal_back(d_first * line(vec_ref, GAIN_ONE), unit, inverse_ref[rows, 0:1])
            low = d_inner.astype(LOW)
            out_ref[rows, :] = d_inner
            low_ref[rows, :] = low
            attended_ref[rows, :] = against(low, w_out_ref[...]).astype(LOW)
            add_line(sum_ref, 0, d_first * unit)
            add_line(sum_ref, 1, d_first)
            add_line(sum_ref, 2, d_inner)


def inner_back(d_pre, w_inner, d_second, unit, inverse, vec, w_out):
    count, hidden = d_pre.shape
    return pl.pallas_call(
        inner_back_kernel,
        grid=(hidden // D,),
        in_specs=[
            pl.BlockSpec((count, D), lambda i: (0, i)),
            pl.BlockSpec((D, D), lambda i: (0, i)),
            kept((count, D)),
            kept((count, D)),
            kept((count, LANES)),
            kept((8, D)),
            kept((D, D)),
        ],
        out_specs=[kept((count, D)), kept((count, D)), kept((count, D)), kept((8, D))],
        out_shape=[
            jax.ShapeDtypeStruct((count, D), FULL),
            jax.ShapeDtypeStruct((count, D), LOW),
            jax.ShapeDtypeStruct((count, D), LOW),
            jax.ShapeDtypeStruct((8, D), FULL),
        ],
        scratch_shapes=[pltpu.VMEM((count, D), FULL)],
        compiler_params=LIMIT,
        name="inner_back",
    )(d_pre, w_inner, d_second, unit, inverse, vec, w_out)


def tokens_kernel(base_ref, d_ref, w_ref, out_ref):
    out_ref[...] = (base_ref[...] + against(d_ref[...], w_ref[...])).astype(out_ref.dtype)


def tokens_back(base, d_group, w_group, kind):
    count, wide = d_group.shape
    rows = count // 2
    return pl.pallas_call(
        tokens_kernel,
        grid=(2,),
        in_specs=[
            pl.BlockSpec((rows, D), lambda i: (i, 0)),
            pl.BlockSpec((rows, wide), lambda i: (i, 0)),
            kept((D, wide)),
        ],
        out_specs=pl.BlockSpec((rows, D), lambda i: (i, 0)),
        out_shape=jax.ShapeDtypeStruct((count, D), kind),
        compiler_params=LIMIT,
        name="tokens_back",
    )(base, d_group, w_group)


def turn_kernel(ref, out_ref):
    out_ref[...] = ref[...].T


def turn(values):
    count, width = values.shape
    return pl.pallas_call(
        turn_kernel,
        grid=(count // ROWS,),
        in_specs=[rows_of(width)],
        out_specs=pl.BlockSpec((width, ROWS), lambda i: (0, i)),
        out_shape=jax.ShapeDtypeStruct((width, count), values.dtype),
        name="turn",
    )(values)


def product_kernel(left_ref, right_ref, out_ref):
    out_ref[...] = project(left_ref[...], right_ref[...]).astype(LOW)


def product(left, right):
    height, depth = left.shape
    return pl.pallas_call(
        product_kernel,
        grid=(right.shape[1] // COLUMNS,),
        in_specs=[kept((height, depth)), columns_of(depth)],
        out_specs=columns_of(height),
        out_shape=jax.ShapeDtypeStruct((height, right.shape[1]), LOW),
        compiler_params=LIMIT,
        name="product",
    )(left, right)


def split_kernel(size, steps, tailed, core_ref, left_ref, right_ref, more_ref, mine_ref, other_ref, found_ref):
    step = pl.program_id(0)
    body = found_ref.shape[0] // size // 2

    @pl.when(step < steps)
    def _():
        found_ref[...] = project(left_ref[...], right_ref[...]).astype(LOW)

    if tailed:

        @pl.when(step >= steps)
        def _():
            found_ref[...] = more_ref[...]

    extra = 0 if tailed else EXTRA
    for shard in range(size):
        at = shard * (body + extra)
        for out_ref, half in ((mine_ref, core_ref[0]), (other_ref, 1 - core_ref[0])):
            start = pl.multiple_of((2 * shard + half) * body, body)
            out_ref[at : at + body, :] = found_ref[pl.ds(start, body), :]
            if extra:
                row = jnp.broadcast_to(more_ref[shard : shard + 1, :], (EXTRA, more_ref.shape[1]))
                out_ref[at + body : at + body + EXTRA, :] = row.astype(LOW)


def split_product(core, left, right, size, tail=None, small=None):
    height, depth = left.shape
    steps = right.shape[1] // COLUMNS
    width = right.shape[1] + (0 if tail is None else tail.shape[1])
    rows = height // 2 + (EXTRA * size if tail is None else 0)
    last = lambda i: (0, jnp.minimum(i, steps - 1))
    if tail is None:
        more, more_spec = small, pl.BlockSpec((size, COLUMNS), last)
    else:
        more, more_spec = tail, pl.BlockSpec((height, COLUMNS), lambda i: (0, jnp.maximum(i - steps, 0)))
    return pl.pallas_call(
        functools.partial(split_kernel, size, steps, tail is not None),
        grid=(width // COLUMNS,),
        in_specs=[
            pl.BlockSpec(memory_space=pltpu.SMEM),
            kept((height, depth)),
            pl.BlockSpec((depth, COLUMNS), last),
            more_spec,
        ],
        out_specs=[columns_of(rows), columns_of(rows)],
        out_shape=[jax.ShapeDtypeStruct((rows, width), LOW)] * 2,
        scratch_shapes=[pltpu.VMEM((height, COLUMNS), LOW)],
        compiler_params=LIMIT,
        name="split_product",
    )(core.reshape(1).astype(jnp.int32), left, right, more)


def assemble_kernel(moves, align, place_ref, *refs):
    out_ref, sems = refs[-2], refs[-1]
    copies = []
    for i, (which, start, rows) in enumerate(moves):
        place = pl.multiple_of(place_ref[i], align)
        source = refs[which].at[pl.ds(start, rows)]
        copies.append(pltpu.make_async_copy(source, out_ref.at[pl.ds(place, rows)], sems.at[i]))
    for copy in copies:
        copy.start()
    for copy in copies:
        copy.wait()


def assemble(arrays, moves, places, rows):
    align = min(move[2] for move in moves)
    return pl.pallas_call(
        functools.partial(assemble_kernel, moves, align),
        in_specs=[pl.BlockSpec(memory_space=pltpu.SMEM)] + [pl.BlockSpec(memory_space=pl.ANY)] * len(arrays),
        out_specs=pl.BlockSpec(memory_space=pltpu.VMEM),
        out_shape=jax.ShapeDtypeStruct((rows,) + arrays[0].shape[1:], arrays[0].dtype),
        scratch_shapes=[pltpu.SemaphoreType.DMA((len(moves),))],
        compiler_params=pltpu.CompilerParams(vmem_limit_bytes=24 * 2**20),
        name="assemble",
    )(jnp.stack(places).astype(jnp.int32), *arrays)


def pack_kernel(size, vectors, *refs):
    out_ref = refs[-1]
    for shard in range(size):
        at = 0
        for spans in vectors:
            lines = []
            for which, row, first, length in spans:
                lines += [(which, row, first + i) for i in range(0, length, LANES)]
            share = len(lines) // size
            for which, row, first in lines[shard * share : (shard + 1) * share]:
                out_ref[shard : shard + 1, at : at + LANES] = refs[which][row : row + 1, first : first + LANES]
                at += LANES


def pack(arrays, vectors, size):
    lengths = [sum(span[3] for span in spans) for spans in vectors]
    if any(length % (size * LANES) for length in lengths):
        whole = [
            jnp.concatenate([arrays[which][row, first : first + length] for which, row, first, length in spans])
            for spans in vectors
        ]
        return jnp.concatenate([vector.reshape(size, -1) for vector in whole], axis=1)
    return pl.pallas_call(
        functools.partial(pack_kernel, size, vectors),
        out_shape=jax.ShapeDtypeStruct((size, sum(lengths) // size), FULL),
        name="pack",
    )(*arrays)


def lay_kernel(*refs):
    row = jnp.concatenate([ref[...].astype(FULL) for ref in refs[:-1]], axis=1)
    refs[-1][...] = jnp.broadcast_to(row, refs[-1].shape).astype(LOW)


def lay(vectors):
    total = sum(vector.shape[1] for vector in vectors)
    return pl.pallas_call(
        lay_kernel,
        out_shape=jax.ShapeDtypeStruct((EXTRA, total), LOW),
        name="lay",
    )(*vectors)


def unpack_kernel(count, body, place_ref, *refs):
    vec_ref, bias_ref, group_ref = refs[count:]
    group_ref[...] = jnp.zeros_like(group_ref)
    hidden = bias_ref.shape[1] // count
    for i in range(count):
        packed = refs[i][body : body + EXTRA, :].astype(FULL)[0:1, :]
        owner = place_ref[i]
        start = pl.multiple_of(owner * LANES, LANES)
        for row in range(8):
            vec_ref[row : row + 1, pl.ds(start, LANES)] = packed[:, row * LANES : (row + 1) * LANES]
        first = pl.multiple_of(owner * hidden, LANES)
        bias_ref[:, pl.ds(first, hidden)] = packed[:, 8 * LANES : 8 * LANES + hidden]
        group = owner * LANES // WIDE
        for place, row in ((0, QUERY), (2, VALUE)):
            first = pl.multiple_of(group * 2 * WIDE + place * WIDE + start, LANES)
            group_ref[:, pl.ds(first, LANES)] = packed[:, row * LANES : (row + 1) * LANES]


def unpack(chunks, owners, body, hidden):
    count = len(chunks)
    return pl.pallas_call(
        functools.partial(unpack_kernel, count, body),
        in_specs=[pl.BlockSpec(memory_space=pltpu.SMEM)] + [pl.BlockSpec(memory_space=pltpu.VMEM)] * count,
        out_shape=[
            jax.ShapeDtypeStruct((8, D), FULL),
            jax.ShapeDtypeStruct((1, hidden), FULL),
            jax.ShapeDtypeStruct((1, 3 * D), FULL),
        ],
        compiler_params=LIMIT,
        name="unpack",
    )(jnp.stack(owners).astype(jnp.int32), *chunks)


def tie(*values):
    return lax.optimization_barrier(values)


class Links:
    def __init__(self, mesh):
        self.reps, self.size = mesh.shape["cross"] * mesh.shape["core"], mesh.shape["shard"]
        size = self.size
        self.direct = size > RING_MOST or size % 2 == 1
        self.order = list(range(0, size, 2)) + list(range(size - 1, 0, -2))
        self.far = size // 2
        self.near = size - 1 - self.far
        shard = lax.axis_index("shard")
        self.core = lax.axis_index("core")
        self.sign = 1 - 2 * self.core
        self.place = jnp.where(shard % 2 == 0, shard // 2, size - 1 - shard // 2)

    def owner(self, step):
        place = (self.place + self.sign * step + 2 * self.size) % self.size
        return jnp.where(place < self.size // 2, 2 * place, 2 * (self.size - place) - 1)

    def hop(self, values, sign):
        pairs = []
        for rep in range(self.reps):
            turn = sign if rep % 2 == 0 else -sign
            for i, shard in enumerate(self.order):
                target = self.order[(i + turn) % self.size]
                pairs.append((rep * self.size + shard, rep * self.size + target))
        return lax.ppermute(values, AXES, pairs)

    def swap(self, values, bit):
        pairs = []
        for rep in range(self.reps):
            for shard in range(self.size):
                pairs.append((rep * self.size + shard, (rep ^ bit) * self.size + shard))
        return lax.ppermute(values, AXES, pairs)

    def half_of(self, values):
        half = values.shape[0] // 2
        return lax.dynamic_slice_in_dim(values, self.core * half, half, axis=0)


    def vectors(self, packed, hidden):
        small = lax.all_gather(packed, "shard", axis=0).astype(FULL)
        width, share = D // self.size, hidden // self.size
        vec = small[:, : 8 * width].reshape(self.size, 8, width).swapaxes(0, 1).reshape(8, D)
        bias = small[:, 8 * width : 8 * width + share].reshape(1, hidden)
        none = jnp.zeros((WIDE,), FULL)
        spans = [slice(g * WIDE, (g + 1) * WIDE) for g in range(GROUPS)]
        parts = [part for span in spans for part in (vec[QUERY, span], none, vec[VALUE, span])]
        return vec, bias, jnp.concatenate(parts).reshape(1, 3 * D)

    def half_of(self, values):
        half = values.shape[0] // 2
        return lax.dynamic_slice_in_dim(values, self.core * half, half, axis=0)

    def gather(self, values, sent=None):
        if self.direct:
            return lax.all_gather(values, "shard", axis=0, tiled=True)
        rows = values.shape[0]
        body = rows // 2
        arrays = [values]
        moves = [(0, 0, rows)]
        places = [self.owner(0) * rows]
        chunks, owners = [sent], [self.owner(0)]

        def keep(chunk, mine, step):
            moves.append((len(arrays), 0, body))
            arrays.append(chunk)
            core = self.core if mine else 1 - self.core
            places.append(self.owner(step) * rows + core * body)
            if mine:
                chunks.append(chunk)
                owners.append(self.owner(step))

        ahead = back = self.half_of(values) if sent is None else sent
        for step in range(1, self.far + 2):
            flight = []
            if step > 1:
                keep(ahead, True, 1 - step)
                flight.append((self.swap(ahead, 1), step - 1))
                if step - 1 <= self.near:
                    keep(back, True, step - 1)
                    flight.append((self.swap(back, 1), 1 - step))
            if step <= self.far:
                ahead = self.hop(ahead, 1)
            if step <= self.near:
                back = self.hop(back, -1)
            ahead, back, *swapped = yield [ahead, back] + [chunk for chunk, _ in flight]
            for chunk, (_, place) in zip(swapped, flight):
                keep(chunk, False, place)
        whole = assemble(arrays, moves, places, self.size * rows)
        return whole if sent is None else (whole, chunks, owners)

    def gather_quarters(self, values):
        rows = values.shape[0] // self.reps
        index = lax.axis_index("cross") * 2 + self.core
        mine = lax.dynamic_slice_in_dim(values, index * rows, rows, axis=0)
        return lax.all_gather(mine, ("shard", "cross", "core"), axis=0, tiled=True)

    def finish(self, total):
        (cross,) = yield [self.swap(total, 2)]
        total = (total.astype(FULL) + cross.astype(FULL)).astype(LOW)
        (pair,) = yield [self.swap(total, 1)]
        low = jnp.where(self.core == 0, total, pair)
        high = jnp.where(self.core == 0, pair, total)
        return jnp.concatenate([low, high], axis=0).astype(FULL)

    def reduce(self, values):
        if self.direct:
            own = lax.psum_scatter(values, "shard", scatter_dimension=0, tiled=True)
            return lax.psum(own, ("cross", "core")).astype(FULL)
        if isinstance(values, tuple):
            kept_rows, other = (part.reshape(self.size, -1, part.shape[1]) for part in values)
            _, half, width = other.shape
        else:
            width = values.shape[1]
            half = values.shape[0] // self.size // 2
            split = values.reshape(self.size, 2, half, width)
            other = lax.dynamic_index_in_dim(split, 1 - self.core, axis=1, keepdims=False)
        (other,) = yield [self.swap(other, 1)]

        def piece(step):
            owner = self.owner(step)
            if isinstance(values, tuple):
                own = lax.dynamic_slice(kept_rows, (owner, 0, 0), (1, half, width))[0]
            else:
                own = lax.dynamic_slice(split, (owner, self.core, 0, 0), (1, 1, half, width))[0, 0]
            pair = lax.dynamic_slice(other, (owner, 0, 0), (1, half, width))
            return own.astype(FULL) + pair[0].astype(FULL)

        ahead = piece(self.far).astype(LOW)
        back = piece(-self.near).astype(LOW)
        for step in range(self.far - 1, -1, -1):
            moving = [self.hop(ahead, 1)]
            if step < self.near:
                moving.append(self.hop(back, -1))
            ahead, *rest = yield moving
            if step > 0:
                ahead = (ahead.astype(FULL) + piece(step)).astype(LOW)
            if rest:
                back = rest[0]
                if step > 0:
                    back = (back.astype(FULL) + piece(-step)).astype(LOW)
        total = (piece(0) + ahead.astype(FULL) + back.astype(FULL)).astype(LOW)
        return (yield from self.finish(total))


class Flow:
    def __init__(self):
        self.running = {}
        self.results = {}

    def start(self, name, steps):
        self._move(name, steps, None)

    def _move(self, name, steps, values):
        try:
            self.running[name] = (steps, steps.send(values))
        except StopIteration as end:
            self.running.pop(name, None)
            self.results[name] = end.value

    def advance(self, *values, near=None):
        running = [item for item in self.running.items() if near is None or item[0] in near]
        flat = list(values)
        for _, (_, flight) in running:
            flat += flight
        tied = tie(*flat) if flat else ()
        at = len(values)
        for name, (steps, flight) in running:
            self._move(name, steps, list(tied[at : at + len(flight)]))
            at += len(flight)
        return tied[0] if len(values) == 1 else tuple(tied[: len(values)])

    def take(self, name):
        while name in self.running:
            steps, flight = self.running[name]
            self._move(name, steps, flight)
        return self.results[name]


def shards(
    mesh,
    tokens,
    w_query,
    w_key,
    w_value,
    b_query,
    b_value,
    w_out,
    b_out,
    gain_one,
    shift_one,
    w_inner,
    b_inner,
    w_outer,
    b_outer,
    gain_two,
    shift_two,
    cotangent,
):
    links = Links(mesh)
    size = links.size
    width = D // size
    hidden = b_inner.shape[0]

    own_groups = [
        jnp.concatenate([w[:, g * WIDE : (g + 1) * WIDE] for w in (w_query, w_key, w_value)], axis=1)
        for g in range(GROUPS)
    ]
    vectors = (b_query, b_value, b_out, gain_one, shift_one, b_outer, gain_two, shift_two)
    used = len(vectors) * width + hidden
    ride = not links.direct and used <= 3 * WIDE and width == LANES
    rows_in = [v.reshape(1, -1) for v in vectors + (b_inner,)]
    packed = jnp.concatenate(rows_in, axis=1)
    sent = None
    if ride:
        extra = jnp.pad(lay(rows_in), ((0, 0), (0, 3 * WIDE - used)))
        halves = [links.half_of(w[:, :WIDE]) for w in (w_query, w_key, w_value)]
        sent = jnp.concatenate([jnp.concatenate(halves, axis=1), extra], axis=0)
        sent, w_inner, w_outer = tie(sent, w_inner, w_outer)
    flow = Flow()
    flow.start("group0", links.gather(own_groups[0], sent))
    whole_inner = links.gather_quarters(w_inner)
    whole_outer = links.gather_quarters(w_outer)
    flow.advance()
    own_groups[1] = flow.advance(own_groups[1])
    flow.start("group1", links.gather(own_groups[1]))
    w_out = flow.advance(w_out)
    flow.start("out", links.gather(w_out))
    tokens_turned = flow.advance(turn(tokens))
    if ride:
        first_group, chunks, owners = flow.take("group0")
        vec, bias_inner, bias_groups = unpack(chunks, owners, width // 2, size * hidden)
    else:
        first_group = flow.take("group0")
        vec, bias_inner, bias_groups = links.vectors(packed[0], size * hidden)
    whole_groups = [first_group]

    projected = []
    attended, lse = None, []
    for g in range(GROUPS):
        bias = bias_groups[:, g * 3 * WIDE : (g + 1) * 3 * WIDE]
        projected.append((project(tokens, whole_groups[g]) + bias).astype(LOW))
        if g == 0:
            projected[g] = flow.advance(projected[g])
            attended, logs = attend(projected[g], g, attended)
            attended = flow.advance(attended)
            whole_groups.append(flow.take("group1"))
        else:
            projected[g] = flow.advance(projected[g])
            attended, logs = attend(projected[g], g, attended)
            attended = flow.advance(attended)
        lse.append(logs)
    whole_out = flow.take("out")
    unit_one, inverse_one, first_low = out_norm(attended, whole_out, tokens, vec)
    active, slope = inner_gelu(first_low, whole_inner, bias_inner)
    output, d_second, d_mid, sums_two = outer_norms(active, whole_outer, unit_one, vec, cotangent)

    grad_outer, d_mid = tie(gram(active, d_mid).astype(LOW), d_mid)
    flow.start("outer_back", links.reduce(grad_outer))
    d_pre, sum_inner = outer_back(d_mid, whole_outer, slope)
    d_pre = flow.advance(d_pre)
    grad_inner, d_pre = flow.advance(gram(first_low, d_pre).astype(LOW), d_pre)
    flow.start("inner_back", links.reduce(grad_inner))
    d_inner, d_branch, d_attended, sums_one = inner_back(
        d_pre, whole_inner, d_second, unit_one, inverse_one, vec, whole_out
    )
    d_branch, d_attended = flow.advance(d_branch, d_attended)
    grad_out, d_attended = tie(gram(attended, d_branch).astype(LOW), d_attended)

    d_groups, sums_group = [], []
    for g in range(GROUPS):
        d_group, sums = attend_back(projected[g], d_attended, lse[g], g)
        d_group, sums, d_attended = flow.advance(d_group, sums, d_attended)
        sums_group.append(sums)
        small = None
        if g == GROUPS - 1:
            arrays = [sums_one, sums_two, sum_inner] + sums_group
            spans = [[(3 + h, 0, place * WIDE, WIDE) for h in range(GROUPS)] for place in (0, 2)]
            spans += [[(i, row, 0, D)] for i, row in ((0, 2), (0, 0), (0, 1), (1, 2), (1, 0), (1, 1))]
            spans += [[(2, 0, 0, size * hidden)]]
            small = pack(arrays, spans, size)
        if ride and g == 0:
            halves = split_product(links.core, tokens_turned, d_group, size, tail=grad_out)
            *halves, d_attended = tie(*halves, d_attended)
            grad_group = tuple(halves)
        elif ride:
            small = jnp.pad(small, ((0, 0), (0, 3 * WIDE - used)))
            halves = split_product(links.core, tokens_turned, d_group, size, small=small)
            *halves, d_group = flow.advance(*halves, d_group)
            grad_group = tuple(halves)
        else:
            grad_group = product(tokens_turned, d_group)
            if g == 0:
                grad_group = jnp.concatenate([grad_group, grad_out], axis=1)
        flow.start(f"back{g}", links.reduce(grad_group))
        d_groups.append(d_group)
    d_tokens = flow.advance(tokens_back(d_inner, d_groups[0], whole_groups[0], FULL))
    d_tokens = flow.advance(tokens_back(d_tokens, d_groups[1], whole_groups[1], LOW))
    own_outer = flow.take("outer_back")
    own_inner = flow.take("inner_back")
    own_groups = [flow.take(f"back{g}") for g in range(GROUPS)]
    own_out = own_groups[0][:, 3 * WIDE :]
    if ride:
        body = width // 2
        last = own_groups[1]
        own_small = last[body]
        own_groups[1] = jnp.concatenate([last[:body], last[body + EXTRA : 2 * body + EXTRA]], axis=0)
    else:
        own_small = lax.psum_scatter(small, "shard", scatter_dimension=0)
        own_small = lax.psum(own_small, ("cross", "core"))

    def joined(parts, place):
        columns = slice(place * WIDE, (place + 1) * WIDE)
        return jnp.concatenate([part[..., columns] for part in parts], axis=-1)

    (
        own_bias_query,
        own_bias_value,
        own_bias_out,
        own_gain_one,
        own_shift_one,
        own_bias_outer,
        own_gain_two,
        own_shift_two,
    ) = (own_small[i * width : (i + 1) * width] for i in range(len(vectors)))
    own_bias_inner = own_small[used - hidden : used]
    return (
        output,
        d_tokens,
        joined(own_groups, 0),
        joined(own_groups, 1),
        joined(own_groups, 2),
        own_bias_query,
        own_bias_value,
        own_out,
        own_bias_out,
        own_gain_one,
        own_shift_one,
        own_inner,
        own_bias_inner,
        own_outer,
        own_bias_outer,
        own_gain_two,
        own_shift_two,
    )


def solution(mesh):
    reps, size = mesh.shape["rep"], mesh.shape["shard"]
    mesh = jax.sharding.Mesh(mesh.devices.reshape(reps // 2, 2, size), AXES)
    rows = P(AXES, None)
    matrix = P("shard", None)
    vector = P("shard")
    return jax.shard_map(
        functools.partial(shards, mesh),
        mesh=mesh,
        in_specs=(
            rows,
            matrix,
            matrix,
            matrix,
            vector,
            vector,
            matrix,
            vector,
            vector,
            vector,
            matrix,
            vector,
            matrix,
            vector,
            vector,
            vector,
            rows,
        ),
        out_specs=(
            rows,
            rows,
            matrix,
            matrix,
            matrix,
            vector,
            vector,
            matrix,
            vector,
            vector,
            vector,
            matrix,
            vector,
            matrix,
            vector,
            vector,
            vector,
        ),
        check_vma=False,
    )
```
